128 devices in a mesh: row: 8 (over y_lo, x), col: 16 (over y_hi, z, core).
Axes of the slice: x: 4, y: 4 (y_hi: 2, y_lo: 2; y = y_hi * 2 + y_lo), z: 4, core: 2. Of those that a mesh axis runs over, the one named last changes fastest.
Arguments:
- known_inverse: float32 [7168, 7168], P('col', 'row'), may hold values from -6 to 6
- factor_panel: float32 [7168, 4096], P('col', 'row'), may hold values from -0.0625 to 0.0625
- diag_base: float32 [4096, 4096], P('row', 'col'), may hold values from -6 to 6
- ancestor_map: int32 [28], replicated, may hold values from 0 to 27, each once
Outputs:
- new_column: float32 [7168, 4096], P('col', 'row')
- diagonal_block: float32 [4096, 4096], P('row', 'col')
The draws below stay inside these ranges and needn't reach their ends.
Inputs may be any that keep to these rules, and one draw needn't show every extreme that they name: `ancestor_map`: a permutation of the 28 ancestor blocks.
All inputs are finite; a program needn't handle non-finite values.
Results may differ from the reference program's by a relative error of at most 0.000071.
Values sent between devices are 32-bit elements; how exact they have to be, the bound alone decides.
A program may use at most 128 MiB of HBM per device.

```python
import jax
import jax.numpy as jnp
from jax import lax

S = 4096
R = 7168
BLK = 256
NBLK = 28


def draw_known_inverse(key, part):
    key = jax.random.fold_in(key, 11)
    first = jax.random.fold_in(key, 0)
    values = jnp.clip(jax.random.normal(first, (R, R), jnp.float32), -6.0, 6.0)
    return 0.5 * (values + values.T)


def draw_diag_base(key, part):
    key = jax.random.fold_in(key, 23)
    first = jax.random.fold_in(key, 0)
    values = jnp.clip(jax.random.normal(first, (S, S), jnp.float32), -6.0, 6.0)
    return 0.5 * (values + values.T)


def levels(stream_key, dims, cuts, low, largest):
    def one(dim, blocks):
        draws = jax.random.uniform(jax.random.fold_in(jax.random.fold_in(stream_key, 6), dim), (blocks,), jnp.float32, low / len(cuts), largest / len(cuts))
        return jnp.repeat(jnp.exp(draws), dims[dim] // blocks).reshape((-1,) + (1,) * (len(dims) - dim - 1))

    factor_of = one(*cuts[0])
    for cut in cuts[1:]:
        factor_of = factor_of * one(*cut)
    return factor_of


def centred(own_key, dims, deviation, limit, pieces=(), kind=jnp.bfloat16):
    gain = levels(own_key, dims, pieces, -0.22, 0.18) if pieces else 1.0
    drawn = jax.random.normal(own_key, dims, jnp.float32) * deviation * gain
    return jnp.minimum(jnp.maximum(drawn, -limit), limit).astype(kind)


def setup_inputs(seed: int = 0) -> dict:
    key_list = jax.random.split(jax.random.key(seed), 5)
    return {
        "known_inverse": draw_known_inverse(jax.random.fold_in(key_list[4], 71), 0),
        "factor_panel": centred(key_list[1], (R, S), R ** -0.5, 0.0625, ((0, 16), (1, 8)), jnp.float32),
        "diag_base": draw_diag_base(jax.random.fold_in(key_list[4], 71), 0),
        "ancestor_map": jax.random.permutation(key_list[3], NBLK).astype(jnp.int32),
    }


def reference(known_inverse, factor_panel, diag_base, ancestor_map):
    inverse = jnp.zeros((NBLK,), jnp.int32).at[ancestor_map].set(jnp.arange(NBLK, dtype=jnp.int32))
    placed = jnp.take(factor_panel.reshape(NBLK, BLK, S), inverse, axis=0).reshape(R, S)
    new_column = -jnp.dot(known_inverse, placed, precision=lax.Precision.HIGHEST, preferred_element_type=jnp.float32)
    product = jnp.dot(placed.T, new_column, precision=lax.Precision.HIGHEST, preferred_element_type=jnp.float32)
    diagonal_block = diag_base - product
    return new_column, diagonal_block
```

```python
import functools

import jax
import jax.numpy as jnp
from jax import lax
from jax.experimental import pallas as pl
from jax.experimental.pallas import tpu as pltpu
from jax.sharding import PartitionSpec as P

MESH = pl.DeviceIdType.MESH
BF = jnp.bfloat16
F32 = jnp.float32

OWN_Y, OWN_UP, OWN_DOWN, FAR_UP, FAR_DOWN, OWN_HALF_UP, OWN_HALF_DOWN, FAR_HALF_UP, FAR_HALF_DOWN, CORE = range(10)


def split(value):
    high = value.astype(BF)
    return high, (value - high.astype(F32)).astype(BF)


def three(a_high, a_low, b_high, b_low):
    def dot(a, b):
        return jnp.dot(a, b, preferred_element_type=F32)

    return dot(a_high, b_high) + (dot(a_high, b_low) + dot(a_low, b_high))


def kernel(
    inv_ref, k_ref, f_ref, n_ref, d_ref,
    k_other, k_high, k_low, sent, picked, panel, p_high, p_low,
    n_part, n_got, n_rows, t_high, t_low, d_part, d_got,
    k_sem, one_send, one_recv, two_send, two_recv, gather_send, gather_recv,
    n_send, n_recv, turn_send, turn_recv, side_send, side_recv, d_send, d_recv, local_sem,
):
    row, col = lax.axis_index("row"), lax.axis_index("col")
    x, y_lo = row % 4, row // 4
    core, z, y_hi = col % 2, (col // 2) % 4, col // 8
    own = y_hi * 4 + z
    up, down = (z + 1) % 4, (z + 3) % 4

    def at(y_hi_, z_, core_, y_lo_, x_):
        return (y_lo_ * 4 + x_, y_hi_ * 8 + z_ * 2 + core_)

    def remote(src, dst, send, recv, device):
        return pltpu.make_async_remote_copy(
            src_ref=src, dst_ref=dst, send_sem=send, recv_sem=recv, device_id=device, device_id_type=MESH
        )

    stays = jnp.logical_and(y_hi == y_lo, z == x)
    row_partner = (1 - y_lo) * 4 + x

    barrier = pltpu.get_barrier_semaphore()

    def greet(device):
        pl.semaphore_signal(barrier, inc=1, device_id=device, device_id_type=MESH)

    @pl.loop(1, 16)
    def _(k):
        greet((row, (col + k) % 16))

    @pl.loop(1, 4)
    def _(k):
        greet((y_lo * 4 + (x + k) % 4, col))

    greet((row_partner, col))
    for g in range(2):
        away = jnp.logical_not(jnp.logical_and(stays, core == g))

        @pl.when(away)
        def _():
            greet(at(y_lo, x, g, y_hi, z))

    pl.semaphore_wait(barrier, 21 - stays.astype(jnp.int32))

    k_copy = remote(k_ref, k_other, k_sem.at[0], k_sem.at[1], (row_partner, col))

    def first(k):
        to = (col + k) % 16
        src = f_ref.at[:, to // 2, :, pl.ds(pl.multiple_of((to % 2) * 256, 256), 256)]
        return remote(src, sent.at[pl.ds(col * 7, 7)], one_send.at[k], one_recv.at[k], (row, to))

    @pl.loop(1, 16)
    def _(k):
        first(k).start()

    k_copy.start()
    mine = pltpu.make_async_copy(
        f_ref.at[:, own, :, pl.ds(pl.multiple_of(core * 256, 256), 256)], sent.at[pl.ds(col * 7, 7)], local_sem.at[0]
    )
    mine.start()

    @pl.when(y_lo == 0)
    def _():
        k_high[:, 0:896], k_low[:, 0:896] = split(k_ref[...])

    @pl.when(y_lo == 1)
    def _():
        k_high[:, 896:1792], k_low[:, 896:1792] = split(k_ref[...])

    mine.wait()

    @pl.loop(1, 16)
    def _(k):
        first(k).wait_recv()

    for k in range(56):
        start = inv_ref[k // 2] * 4 + (k % 2) * 2
        to, pos = (k % 28) // 7, (k // 28) * 14 + (k % 7) * 2
        picked[to, pos : pos + 2] = sent[pl.ds(start, 2)]

    def piece(block, member, chunk=0, chunks=28):
        return panel.at[block, core, pl.ds(chunk, chunks), pl.ds(pl.multiple_of(member * 8, 8), 8), :]

    def second(k):
        to = (x + 4 - k) % 4
        return remote(picked.at[to], piece(x, own), two_send.at[k], two_recv.at[k], (y_lo * 4 + to, col))

    @pl.loop(1, 4)
    def _(k):
        second(k).start()

    keep = pltpu.make_async_copy(picked.at[x], piece(x, own), local_sem.at[1])
    keep.start()

    far = (1 - y_hi) * 4

    def gather(kind, i):
        block = (x + i + 1) % 4
        near = y_hi * 4
        high_z = at(y_hi, up, core, y_lo, x)
        low_z = at(y_hi, down, core, y_lo, x)
        if kind == CORE:
            ref, to = panel.at[block, core], (row, y_hi * 8 + z * 2 + 1 - core)
        else:
            ref, to = {
                OWN_Y: (piece(block, own), at(1 - y_hi, z, core, y_lo, x)),
                OWN_UP: (piece(block, own), high_z),
                OWN_DOWN: (piece(block, own), low_z),
                FAR_UP: (piece(block, far + z), high_z),
                FAR_DOWN: (piece(block, far + z), low_z),
                OWN_HALF_UP: (piece(block, near + down, 0, 14), high_z),
                OWN_HALF_DOWN: (piece(block, near + up, 14, 14), low_z),
                FAR_HALF_UP: (piece(block, far + down, 0, 14), high_z),
                FAR_HALF_DOWN: (piece(block, far + up, 14, 14), low_z),
            }[kind]
        return remote(ref, ref, gather_send.at[kind, i], gather_recv.at[kind, i], to)

    def own_sends(i):
        for kind in (OWN_Y, OWN_UP, OWN_DOWN):
            gather(kind, i).start()

    @pl.loop(0, 3)
    def _(i):
        second(i + 1).wait_recv()
        own_sends(i)

    keep.wait()
    own_sends(3)

    k_copy.wait_recv()

    @pl.when(y_lo == 0)
    def _():
        k_high[:, 896:1792], k_low[:, 896:1792] = split(k_other[...])

    @pl.when(y_lo == 1)
    def _():
        k_high[:, 0:896], k_low[:, 0:896] = split(k_other[...])

    def n_copy(i, turn):
        to = (x + i + 1) % 4
        return remote(
            n_part.at[i, turn], n_got.at[i, turn], n_send.at[i, turn], n_recv.at[i, turn], (y_lo * 4 + to, col)
        )

    def n_unit(i, turn):
        block = (x + i + 1) % 4
        half = (core + turn) % 2

        @pl.loop(0, 7)
        def _(k):
            value = panel[block, half, pl.ds(k * 4, 4)].reshape(256, 256)
            rows = pl.ds(pl.multiple_of(k * 256, 256), 256)
            p_high[block, half, rows], p_low[block, half, rows] = split(value)

        n_part[i, turn] = three(k_high[...], k_low[...], p_high[block, half], p_low[block, half])

        @pl.when(i < 3)
        def _():
            n_copy(i, turn).start()

    @pl.loop(0, 6)
    def _(t):
        @pl.when(t < 4)
        def _():
            gather(OWN_Y, t).wait_recv()
            gather(FAR_UP, t).start()
            gather(FAR_DOWN, t).start()

        @pl.when(jnp.logical_and(t >= 1, t < 5))
        def _():
            for arrived, passed in (
                (OWN_UP, OWN_HALF_UP), (OWN_DOWN, OWN_HALF_DOWN),
                (FAR_UP, FAR_HALF_UP), (FAR_DOWN, FAR_HALF_DOWN),
            ):
                gather(arrived, t - 1).wait_recv()
                gather(passed, t - 1).start()

        @pl.when(t >= 2)
        def _():
            i = t - 2
            for kind in (OWN_HALF_UP, OWN_HALF_DOWN, FAR_HALF_UP, FAR_HALF_DOWN):
                gather(kind, i).wait_recv()
            gather(CORE, i).start()
            n_unit(i, 0)
            gather(CORE, i).wait_recv()
            n_unit(i, 1)

    def turned(g):
        slot = pl.ds(pl.multiple_of((y_hi * 2 + core) * 448, 64), 448)
        return n_ref.at[:, pl.ds(g * 256, 256)], n_rows.at[slot]

    def turn(g):
        src, dst = turned(g)
        return remote(src, dst, turn_send.at[g], turn_recv.at[core], at(y_lo, x, g, y_hi, z))

    def turn_here(g):
        src, dst = turned(g)
        return pltpu.make_async_copy(src, dst, turn_recv.at[core])

    for turn_index in range(2):
        for i in range(3):
            n_copy(i, turn_index).wait_recv()
        total = n_part[3, turn_index] + n_got[0, turn_index] + n_got[1, turn_index] + n_got[2, turn_index]
        for g in range(2):

            @pl.when((core + turn_index) % 2 == g)
            def _():
                n_ref[:, g * 256 : (g + 1) * 256] = total

                @pl.when(jnp.logical_and(stays, core == g))
                def _():
                    turn_here(g).start()

                @pl.when(jnp.logical_not(jnp.logical_and(stays, core == g)))
                def _():
                    turn(g).start()

    def side(g):
        rows = n_rows.at[pl.ds(pl.multiple_of((y_lo * 2 + g) * 448, 64), 448)]
        return remote(rows, rows, side_send.at[g], side_recv.at[g], (row_partner, col))

    for g in range(2):
        rows = n_rows.at[pl.ds(pl.multiple_of((y_lo * 2 + g) * 448, 64), 448)]
        pltpu.make_async_copy(rows, rows, turn_recv.at[g]).wait()
        side(g).start()
    for g in range(2):
        side(g).wait_recv()

    for k in range(7):
        rows = slice(k * 256, (k + 1) * 256)
        t_high[:, rows], t_low[:, rows] = split(n_rows[rows, :].T)

    def d_copy(i):
        to = (x + i + 1) % 4
        return remote(d_part.at[i], d_got.at[i], d_send.at[i], d_recv.at[i], (y_lo * 4 + to, col))

    @pl.loop(0, 4)
    def _(i):
        block = (x + i + 1) % 4
        for half in range(2):
            d_part[i, :, half * 256 : (half + 1) * 256] = three(
                t_high[...], t_low[...], p_high[block, half], p_low[block, half]
            )

        @pl.when(i < 3)
        def _():
            d_copy(i).start()

    for i in range(3):
        d_copy(i).wait_recv()
    d_ref[...] = d_part[3] + d_got[0] + d_got[1] + d_got[2]

    @pl.loop(1, 16)
    def _(k):
        first(k).wait_send()

    @pl.loop(1, 4)
    def _(k):
        second(k).wait_send()

    k_copy.wait_send()

    @pl.loop(0, 4)
    def _(i):
        for kind in range(10):
            gather(kind, i).wait_send()

    @pl.loop(0, 3)
    def _(i):
        for turn_index in range(2):
            n_copy(i, turn_index).wait_send()
        d_copy(i).wait_send()

    for g in range(2):
        side(g).wait_send()

        @pl.when(jnp.logical_not(jnp.logical_and(stays, core == g)))
        def _():
            turn(g).wait_send()


def on_device(known_inverse, factor_panel, diag_base, ancestor_map):
    blocks = jnp.arange(28, dtype=jnp.int32)
    inverse = jnp.sum(jnp.where(ancestor_map[None, :] == blocks[:, None], blocks[None, :], 0), axis=1)
    vmem = pl.BlockSpec(memory_space=pltpu.VMEM)
    dma = pltpu.SemaphoreType.DMA
    product, reduced = pl.pallas_call(
        kernel,
        out_shape=(jax.ShapeDtypeStruct((448, 512), F32), jax.ShapeDtypeStruct((256, 512), F32)),
        in_specs=[pl.BlockSpec(memory_space=pltpu.SMEM), vmem, vmem],
        out_specs=(vmem, vmem),
        scratch_shapes=[
            pltpu.VMEM((448, 896), F32),
            pltpu.VMEM((448, 1792), BF),
            pltpu.VMEM((448, 1792), BF),
            pltpu.VMEM((112, 8, 256), F32),
            pltpu.VMEM((4, 28, 8, 256), F32),
            pltpu.VMEM((4, 2, 28, 64, 256), F32),
            pltpu.VMEM((4, 2, 1792, 256), BF),
            pltpu.VMEM((4, 2, 1792, 256), BF),
            pltpu.VMEM((4, 2, 448, 256), F32),
            pltpu.VMEM((3, 2, 448, 256), F32),
            pltpu.VMEM((1792, 256), F32),
            pltpu.VMEM((256, 1792), BF),
            pltpu.VMEM((256, 1792), BF),
            pltpu.VMEM((4, 256, 512), F32),
            pltpu.VMEM((3, 256, 512), F32),
            dma((2,)), dma((16,)), dma((16,)), dma((4,)), dma((4,)), dma((10, 4)), dma((10, 4)),
            dma((3, 2)), dma((3, 2)), dma((2,)), dma((2,)), dma((2,)), dma((2,)), dma((3,)), dma((3,)), dma((2,)),
        ],
        compiler_params=pltpu.CompilerParams(collective_id=0, has_side_effects=True, vmem_limit_bytes=60 << 20),
        cost_estimate=pl.CostEstimate(flops=3 * 2 * (448 * 1792 * 2048 + 256 * 1792 * 2048), bytes_accessed=4 << 20, transcendentals=0),
        name="selected_inverse",
    )(inverse, known_inverse, factor_panel.reshape(7, 8, 8, 512))
    return (-product, diag_base + reduced.T)


def solution(mesh):
    placed = (P("col", "row"), P("col", "row"), P("row", "col"), P())
    return jax.shard_map(
        on_device,
        mesh=mesh,
        in_specs=placed,
        out_specs=(P("col", "row"), P("row", "col")),
        check_vma=False,
    )
```

```python
import jax
import jax.numpy as jnp
from jax import lax
from jax.experimental import pallas as pl
from jax.experimental.pallas import tpu as pltpu
from jax.sharding import PartitionSpec as P

MESH = pl.DeviceIdType.MESH
BF = jnp.bfloat16
F32 = jnp.float32

UP, DOWN, HALF_UP, HALF_DOWN, CORE = range(5)


def split(value):
    high = value.astype(BF)
    return high, (value - high.astype(F32)).astype(BF)


def three(a_high, a_low, b_high, b_low):
    def dot(a, b):
        return jnp.dot(a, b, preferred_element_type=F32)

    return dot(a_high, b_high) + (dot(a_high, b_low) + dot(a_low, b_high))


def kernel(
    inv_ref, k_ref, f_ref, n_ref, d_ref,
    k_all, k_high, k_low, sent_0, sent_1, picked, p_x, p_high, p_low, p_z, pz_high, pz_low,
    n_part, n_got, n_all, t_high, t_low, d_part, d_core, d_got, d_sum, d_out,
    one_send, one_recv, two_send, two_recv, three_send, three_recv, local_sem, k_send, k_recv,
    z_send, z_recv, x_send, x_recv, n_send, n_recv, y_send, y_recv,
    c_send, c_recv, d_send, d_recv, o_send, o_recv,
):
    row, col = lax.axis_index("row"), lax.axis_index("col")
    x, y_lo = row % 4, row // 4
    core, z, y_hi = col % 2, (col // 2) % 4, col // 8
    y, place = y_hi * 2 + y_lo, col % 8

    def at(y_hi_, z_, core_, y_lo_, x_):
        return (y_lo_ * 4 + x_, y_hi_ * 8 + z_ * 2 + core_)

    def on_x(k):
        return (y_lo * 4 + (x + k) % 4, col)

    def on_y(k):
        there = (y + k) % 4
        return at(there // 2, z, core, there % 2, x)

    def on_z(k):
        return (row, y_hi * 8 + ((z + k) % 4) * 2 + core)

    other_core = (row, y_hi * 8 + z * 2 + 1 - core)
    stays = jnp.logical_and(y_hi == y_lo, y_hi == core)

    def remote(src, dst, send, recv, device):
        return pltpu.make_async_remote_copy(
            src_ref=src, dst_ref=dst, send_sem=send, recv_sem=recv, device_id=device, device_id_type=MESH
        )

    barrier = pltpu.get_barrier_semaphore()

    def greet(device):
        pl.semaphore_signal(barrier, inc=1, device_id=device, device_id_type=MESH)

    @pl.loop(1, 16)
    def _(k):
        greet((row, (col + k) % 16))

    for k in (1, 2, 3):
        greet(on_x(k))
    for k in (1, 3):
        greet(on_y(k))

    @pl.when(jnp.logical_not(stays))
    def _():
        greet(at(core, z, y_lo, y_hi, x))

    pl.semaphore_wait(barrier, 21 - stays.astype(jnp.int32))

    sent = (sent_0, sent_1)

    def piece(to, e):
        return f_ref.at[:, to % 8, :, pl.ds(pl.multiple_of((to // 8) * 256 + e * 128, 128), 128)]

    def first(e, k):
        to = (col + k) % 16
        return remote(piece(to, e), sent[e].at[pl.ds(col * 7, 7)], one_send.at[e, k], one_recv.at[e, k], (row, to))

    def first_here(e):
        return pltpu.make_async_copy(piece(col, e), sent[e].at[pl.ds(col * 7, 7)], local_sem.at[e])

    for e in range(2):

        @pl.loop(1, 16)
        def _(k):
            first(e, k).start()

        first_here(e).start()

    def k_copy(kind, half):
        rows = pl.ds(half * 224, 224)
        return remote(
            k_ref.at[rows], k_all.at[y, rows], k_send.at[kind, half], k_recv.at[kind, half], on_y(1 if kind == UP else 3)
        )

    def k_pass(kind):
        rows = pl.ds(0, 224) if kind == HALF_UP else pl.ds(224, 224)
        ref = k_all.at[(y + (3 if kind == HALF_UP else 1)) % 4, rows]
        return remote(ref, ref, k_send.at[kind, 0], k_recv.at[kind, 0], on_y(1 if kind == HALF_UP else 3))

    k_copy(UP, 0).start()
    k_copy(DOWN, 1).start()
    k_copy(UP, 1).start()
    k_copy(DOWN, 0).start()

    def take_k(there, ref):
        for side in range(2):

            @pl.when(there % 2 == side)
            def _():
                columns = slice(side * 896, (side + 1) * 896)
                k_high[there // 2, :, columns], k_low[there // 2, :, columns] = split(ref[...])

    take_k(y, k_ref)

    def second(e, k):
        to = (x + 4 - k) % 4
        i = (k + 3) % 4
        src = picked.at[e, :, pl.ds(to * 14, 14)]
        dst = p_x.at[e, i // 2, i % 2, :, :, z, core]
        if k == 0:
            return pltpu.make_async_copy(src, dst, local_sem.at[2 + e])
        return remote(src, dst, two_send.at[e, k], two_recv.at[e, k], on_x(4 - k))

    def third(e, k):
        to = (place + k) % 8
        src = picked.at[e, :, pl.ds(to * 7, 7)]
        dst = p_z.at[e, x, :, :, place]
        return remote(src, dst, three_send.at[e, k], three_recv.at[e, k], (row, y_hi * 8 + to))

    def third_here(e):
        src = picked.at[e, :, pl.ds(place * 7, 7)]
        return pltpu.make_async_copy(src, p_z.at[e, x, :, :, place], local_sem.at[4 + e])

    for e in range(2):
        first_here(e).wait()

        @pl.loop(1, 16)
        def _(k):
            first(e, k).wait_recv()

        for j in range(28):
            picked[e, j // 14, (j % 14) * 4 : (j % 14) * 4 + 4] = sent[e][pl.ds(inv_ref[j] * 4, 4)]
        for k in (1, 2, 3, 0):
            second(e, k).start()

        @pl.loop(1, 8)
        def _(k):
            third(e, k).start()

        third_here(e).start()

    def z_copy(kind, r):
        def rows(there, chunk=slice(None)):
            return p_x.at[r // 2, r % 2, :, chunk, :, there, core]

        if kind == CORE:
            ref, to = p_x.at[r // 2, r % 2, :, :, :, :, core], other_core
        else:
            ref, to = {
                UP: (rows(z), on_z(1)),
                DOWN: (rows(z), on_z(3)),
                HALF_UP: (rows((z + 3) % 4, 0), on_z(1)),
                HALF_DOWN: (rows((z + 1) % 4, 1), on_z(3)),
            }[kind]
        return remote(ref, ref, z_send.at[kind, r], z_recv.at[kind, r], to)

    def x_copy(kind, e):
        def block(there, half=slice(None)):
            return p_z.at[e, there, half]

        ref, to = {
            UP: (block(x), on_x(1)),
            DOWN: (block(x), on_x(3)),
            HALF_UP: (block((x + 3) % 4, 0), on_x(1)),
            HALF_DOWN: (block((x + 1) % 4, 1), on_x(3)),
        }[kind]
        return remote(ref, ref, x_send.at[kind, e], x_recv.at[kind, e], to)

    def pass_on(copy, r):
        copy(UP, r).wait_recv()
        copy(HALF_UP, r).start()
        copy(DOWN, r).wait_recv()
        copy(HALF_DOWN, r).start()

    def third_done(e):
        third_here(e).wait()

        @pl.loop(1, 8)
        def _(k):
            third(e, k).wait_recv()

    for e in range(2):
        second(e, 0).wait()
        for k in (1, 2, 3):
            second(e, k).wait_recv()
        for p in range(2):
            z_copy(UP, 2 * e + p).start()
            z_copy(DOWN, 2 * e + p).start()
        third_done(e)
        if e == 0:
            x_copy(UP, 0).start()
            x_copy(DOWN, 0).start()

    k_copy(UP, 0).wait_recv()
    k_pass(HALF_UP).start()
    k_copy(DOWN, 1).wait_recv()
    k_pass(HALF_DOWN).start()

    def core_start(r):
        z_copy(HALF_UP, r).wait_recv()
        z_copy(HALF_DOWN, r).wait_recv()
        z_copy(CORE, r).start()

    pass_on(z_copy, 0)
    pass_on(z_copy, 1)
    core_start(0)
    k_copy(UP, 1).wait_recv()
    k_copy(DOWN, 0).wait_recv()
    take_k((y + 3) % 4, k_all.at[(y + 3) % 4])
    take_k((y + 1) % 4, k_all.at[(y + 1) % 4])
    pass_on(x_copy, 0)

    def n_copy(e, i, side):
        src = n_part.at[2 * e + i // 2, side, :, pl.ds((i % 2) * 128, 128)]
        return remote(src, n_got.at[i, e, side], n_send.at[i, e, side], n_recv.at[i, e, side], on_x(i + 1))

    def n_unit(r, side):
        e, p = r // 2, r % 2

        @pl.loop(0, 14)
        def _(k):
            for half in range(2):
                rows = pl.ds(pl.multiple_of(half * 896 + k * 64, 64), 64)
                for i in range(2):
                    columns = slice(i * 128, (i + 1) * 128)
                    p_high[rows, columns], p_low[rows, columns] = split(p_x[e, p, i, half, k].reshape(64, 128))

        n_part[r, side] = three(k_high[side], k_low[side], p_high[...], p_low[...])

        @pl.when(p == 0)
        def _():
            n_copy(e, 0, side).start()
            n_copy(e, 1, side).start()

        @pl.when(p == 1)
        def _():
            n_copy(e, 2, side).start()

    @pl.loop(0, 4)
    def _(r):
        @pl.when(r < 2)
        def _():
            pass_on(z_copy, r + 2)

        @pl.when(r < 3)
        def _():
            core_start(r + 1)

        z_copy(CORE, r).wait_recv()
        n_unit(r, y_hi)

    k_pass(HALF_UP).wait_recv()
    k_pass(HALF_DOWN).wait_recv()
    take_k((y + 2) % 4, k_all.at[(y + 2) % 4])

    @pl.loop(0, 4)
    def _(r):
        n_unit(r, 1 - y_hi)

    x_copy(UP, 1).start()
    x_copy(DOWN, 1).start()

    def y_copy(e, k):
        ref = n_all.at[e, y]
        return remote(ref, ref, y_send.at[e, k], y_recv.at[e, k], on_y(k))

    for e in range(2):
        for side in range(2):
            for i in range(3):
                n_copy(e, i, side).wait_recv()
            n_all[e, y, side * 448 : (side + 1) * 448] = n_part[2 * e + 1, side, :, 128:256] + (
                n_got[0, e, side] + n_got[1, e, side] + n_got[2, e, side]
            )
        for k in (1, 3, 2):
            y_copy(e, k).start()
        if e == 0:
            pass_on(x_copy, 1)

    for e in range(2):
        x_copy(HALF_UP, e).wait_recv()
        x_copy(HALF_DOWN, e).wait_recv()

    @pl.loop(0, 4)
    def _(there):
        for half in range(2):
            rows = slice(half * 448, (half + 1) * 448)
            for e in range(2):
                columns = slice(e * 128, (e + 1) * 128)
                pz_high[there, rows, columns], pz_low[there, rows, columns] = split(p_z[e, there, half].reshape(448, 128))

    def c_copy(e):
        return remote(d_part.at[e, 1 - core], d_core.at[e], c_send.at[e], c_recv.at[e], other_core)

    def d_copy(e, k):
        return remote(d_part.at[e, core, (z + k) % 4], d_got.at[e, k - 1], d_send.at[e, k - 1], d_recv.at[e, k - 1], on_z(k))

    @pl.loop(0, 2)
    def _(e):
        for k in (1, 3, 2):
            y_copy(e, k).wait_recv()
        for low in range(2):
            for high in range(2):
                for k in range(7):
                    rows = slice(k * 128, (k + 1) * 128)
                    lines = slice(high * 128, (high + 1) * 128)
                    t_high[low, lines, rows], t_low[low, lines, rows] = split(n_all[e, 2 * high + low, rows].T)

        @pl.loop(0, 2)
        def _(turn):
            low = (core + 1 + turn) % 2

            @pl.loop(0, 4)
            def _(there):
                d_part[e, low, there] = three(t_high[low], t_low[low], pz_high[there], pz_low[there])

            @pl.when(turn == 0)
            def _():
                c_copy(e).start()

        c_copy(e).wait_recv()

        @pl.loop(0, 4)
        def _(there):
            d_part[e, core, there] += d_core[e, there]

        for k in (1, 3, 2):
            d_copy(e, k).start()

    def o_copy(e):
        return remote(d_sum.at[e], d_out.at[e], o_send.at[e], o_recv.at[e], at(y_lo, z, y_hi, core, x))

    for e in range(2):
        for k in (1, 3, 2):
            d_copy(e, k).wait_recv()
        d_sum[e] = d_part[e, core, z] + (d_got[e, 0] + d_got[e, 1] + d_got[e, 2])

        @pl.when(stays)
        def _():
            pltpu.make_async_copy(d_sum.at[e], d_out.at[e], o_recv.at[e]).start()

        @pl.when(jnp.logical_not(stays))
        def _():
            o_copy(e).start()

    for e in range(2):
        for half in range(2):
            n_ref[:, half * 256 + e * 128 : half * 256 + (e + 1) * 128] = n_all[
                e, half * 2 + y_lo, pl.ds(pl.multiple_of(y_hi * 448, 64), 448)
            ]

    for e in range(2):
        pltpu.make_async_copy(d_sum.at[e], d_out.at[e], o_recv.at[e]).wait()
        d_ref[0, e] = d_out[e, 0:128]
        d_ref[1, e] = d_out[e, 128:256]

    for e in range(2):

        @pl.loop(1, 16)
        def _(k):
            first(e, k).wait_send()

        @pl.loop(1, 8)
        def _(k):
            third(e, k).wait_send()

        for k in (1, 2, 3):
            second(e, k).wait_send()
            y_copy(e, k).wait_send()
            d_copy(e, k).wait_send()
        for kind in range(4):
            x_copy(kind, e).wait_send()
        for i in range(3):
            for side in range(2):
                n_copy(e, i, side).wait_send()
        c_copy(e).wait_send()

        @pl.when(jnp.logical_not(stays))
        def _():
            o_copy(e).wait_send()

    for half in range(2):
        k_copy(UP, half).wait_send()
        k_copy(DOWN, half).wait_send()
    k_pass(HALF_UP).wait_send()
    k_pass(HALF_DOWN).wait_send()

    @pl.loop(0, 4)
    def _(r):
        for kind in range(5):
            z_copy(kind, r).wait_send()


def on_device(known_inverse, factor_panel, diag_base, ancestor_map):
    blocks = jnp.arange(28, dtype=jnp.int32)
    inverse = jnp.sum(jnp.where(ancestor_map[None, :] == blocks[:, None], blocks[None, :], 0), axis=1)
    vmem = pl.BlockSpec(memory_space=pltpu.VMEM)
    dma = pltpu.SemaphoreType.DMA
    product, reduced = pl.pallas_call(
        kernel,
        out_shape=(jax.ShapeDtypeStruct((448, 512), F32), jax.ShapeDtypeStruct((2, 2, 128, 256), F32)),
        in_specs=[pl.BlockSpec(memory_space=pltpu.SMEM), vmem, vmem],
        out_specs=(vmem, vmem),
        scratch_shapes=[
            pltpu.VMEM((4, 448, 896), F32),
            pltpu.VMEM((2, 448, 1792), BF),
            pltpu.VMEM((2, 448, 1792), BF),
            pltpu.VMEM((112, 8, 128), F32),
            pltpu.VMEM((112, 8, 128), F32),
            pltpu.VMEM((2, 2, 56, 8, 128), F32),
            pltpu.VMEM((2, 2, 2, 2, 14, 4, 2, 8, 128), F32),
            pltpu.VMEM((1792, 256), BF),
            pltpu.VMEM((1792, 256), BF),
            pltpu.VMEM((2, 4, 2, 7, 8, 8, 128), F32),
            pltpu.VMEM((4, 896, 256), BF),
            pltpu.VMEM((4, 896, 256), BF),
            pltpu.VMEM((4, 2, 448, 256), F32),
            pltpu.VMEM((3, 2, 2, 448, 128), F32),
            pltpu.VMEM((2, 4, 896, 128), F32),
            pltpu.VMEM((2, 256, 896), BF),
            pltpu.VMEM((2, 256, 896), BF),
            pltpu.VMEM((2, 2, 4, 256, 256), F32),
            pltpu.VMEM((2, 4, 256, 256), F32),
            pltpu.VMEM((2, 3, 256, 256), F32),
            pltpu.VMEM((2, 256, 256), F32),
            pltpu.VMEM((2, 256, 256), F32),
            dma((2, 16)), dma((2, 16)), dma((2, 4)), dma((2, 4)), dma((2, 8)), dma((2, 8)), dma((6,)), dma((4, 2)), dma((4, 2)),
            dma((5, 4)), dma((5, 4)), dma((4, 2)), dma((4, 2)), dma((3, 2, 2)), dma((3, 2, 2)), dma((2, 4)), dma((2, 4)),
            dma((2,)), dma((2,)), dma((2, 3)), dma((2, 3)), dma((2,)), dma((2,)),
        ],
        compiler_params=pltpu.CompilerParams(collective_id=0, has_side_effects=True, vmem_limit_bytes=60 << 20),
        cost_estimate=pl.CostEstimate(
            flops=6 * (448 * 1792 * 2048 + 256 * 1792 * 2048), bytes_accessed=4 << 20, transcendentals=0
        ),
        name="selected_inverse",
    )(inverse, known_inverse, factor_panel.reshape(7, 8, 8, 512))
    return (-product, diag_base + reduced.reshape(512, 256))


def solution(mesh):
    placed = (P("col", "row"), P("col", "row"), P("row", "col"), P())
    return jax.shard_map(
        on_device,
        mesh=mesh,
        in_specs=placed,
        out_specs=(P("col", "row"), P("row", "col")),
        check_vma=False,
    )
```

```python
import jax
import jax.numpy as jnp
from jax import lax
from jax.experimental import pallas as pl
from jax.experimental.pallas import tpu as pltpu
from jax.sharding import PartitionSpec as P

MESH = pl.DeviceIdType.MESH
BF = jnp.bfloat16
F32 = jnp.float32

UP, DOWN, HALF_UP, HALF_DOWN, CORE = range(5)


def split(value):
    high = value.astype(BF)
    return high, (value - high.astype(F32)).astype(BF)


def three(a_high, a_low, b_high, b_low):
    def dot(a, b):
        return jnp.dot(a, b, preferred_element_type=F32)

    return dot(a_high, b_high) + (dot(a_high, b_low) + dot(a_low, b_high))


def kernel(
    inv_ref, k_ref, f_ref, n_ref, d_ref,
    k_all, k_high, k_low, sent_0, sent_1, picked, p_x, p_high, p_low, p_z, pz_high, pz_low,
    n_part, n_far, n_got, n_all, t_high, t_low, d_part, d_core, d_got, d_sum, d_out,
    one_send, one_recv, two_send, two_recv, three_send, three_recv, local_sem, k_send, k_recv,
    z_send, z_recv, x_send, x_recv, n_send, n_recv, y_send, y_recv,
    c_send, c_recv, d_send, d_recv, o_send, o_recv,
):
    row, col = lax.axis_index("row"), lax.axis_index("col")
    x, y_lo = row % 4, row // 4
    core, z, y_hi = col % 2, (col // 2) % 4, col // 8
    y, place = y_hi * 2 + y_lo, col % 8

    def at(y_hi_, z_, core_, y_lo_, x_):
        return (y_lo_ * 4 + x_, y_hi_ * 8 + z_ * 2 + core_)

    def on_x(k):
        return (y_lo * 4 + (x + k) % 4, col)

    def on_y(k):
        there = (y + k) % 4
        return at(there // 2, z, core, there % 2, x)

    def on_z(k):
        return (row, y_hi * 8 + ((z + k) % 4) * 2 + core)

    other_core = (row, y_hi * 8 + z * 2 + 1 - core)
    stays = jnp.logical_and(y_hi == y_lo, y_hi == core)

    def remote(src, dst, send, recv, device):
        return pltpu.make_async_remote_copy(
            src_ref=src, dst_ref=dst, send_sem=send, recv_sem=recv, device_id=device, device_id_type=MESH
        )

    barrier = pltpu.get_barrier_semaphore()

    def greet(device):
        pl.semaphore_signal(barrier, inc=1, device_id=device, device_id_type=MESH)

    @pl.loop(1, 16)
    def _(k):
        greet((row, (col + k) % 16))

    for k in (1, 2, 3):
        greet(on_x(k))
    for k in (1, 3):
        greet(on_y(k))

    @pl.when(jnp.logical_not(stays))
    def _():
        greet(at(core, z, y_lo, y_hi, x))

    pl.semaphore_wait(barrier, 21 - stays.astype(jnp.int32))

    sent = (sent_0, sent_1)

    def piece(to, e):
        return f_ref.at[:, to % 8, :, pl.ds(pl.multiple_of((to // 8) * 256 + e * 128, 128), 128)]

    def first(e, k):
        to = (col + k) % 16
        return remote(piece(to, e), sent[e].at[pl.ds(col * 7, 7)], one_send.at[e, k], one_recv.at[e, k], (row, to))

    def first_here(e):
        return pltpu.make_async_copy(piece(col, e), sent[e].at[pl.ds(col * 7, 7)], local_sem.at[e])

    for e in range(2):

        @pl.loop(1, 16)
        def _(k):
            first(e, k).start()

        first_here(e).start()

    def k_copy(kind, half):
        rows = pl.ds(half * 224, 224)
        return remote(
            k_ref.at[rows], k_all.at[y, rows], k_send.at[kind, half], k_recv.at[kind, half], on_y(1 if kind == UP else 3)
        )

    def k_pass(kind):
        rows = pl.ds(0, 224) if kind == HALF_UP else pl.ds(224, 224)
        ref = k_all.at[(y + (3 if kind == HALF_UP else 1)) % 4, rows]
        return remote(ref, ref, k_send.at[kind, 0], k_recv.at[kind, 0], on_y(1 if kind == HALF_UP else 3))

    k_copy(UP, 0).start()
    k_copy(DOWN, 1).start()

    def take_k(there, ref):
        k_high[there], k_low[there] = split(ref[...])

    take_k(y, k_ref)

    def second(e, k):
        to = (x + 4 - k) % 4
        i = (k + 3) % 4
        src = picked.at[e, :, pl.ds(to * 14, 14)]
        dst = p_x.at[e, i // 2, i % 2, :, :, z, core]
        if k == 0:
            return pltpu.make_async_copy(src, dst, local_sem.at[2 + e])
        return remote(src, dst, two_send.at[e, k], two_recv.at[e, k], on_x(4 - k))

    def third(e, k):
        to = (place + k) % 8
        src = picked.at[e, :, pl.ds(to * 7, 7)]
        dst = p_z.at[e, x, :, :, place]
        return remote(src, dst, three_send.at[e, k], three_recv.at[e, k], (row, y_hi * 8 + to))

    def third_here(e):
        src = picked.at[e, :, pl.ds(place * 7, 7)]
        return pltpu.make_async_copy(src, p_z.at[e, x, :, :, place], local_sem.at[4 + e])

    for e in range(2):
        first_here(e).wait()

        @pl.loop(1, 16)
        def _(k):
            first(e, k).wait_recv()

        for j in range(28):
            picked[e, j // 14, (j % 14) * 4 : (j % 14) * 4 + 4] = sent[e][pl.ds(inv_ref[j] * 4, 4)]
        for k in (1, 2, 3, 0):
            second(e, k).start()

        @pl.loop(1, 8)
        def _(k):
            third(e, k).start()

        third_here(e).start()
        if e == 0:
            k_copy(UP, 1).start()
            k_copy(DOWN, 0).start()

    def z_copy(kind, r):
        def rows(there, chunk=slice(None)):
            return p_x.at[r // 2, r % 2, :, chunk, :, there, core]

        if kind == CORE:
            ref, to = p_x.at[r // 2, r % 2, :, :, :, :, core], other_core
        else:
            ref, to = {
                UP: (rows(z), on_z(1)),
                DOWN: (rows(z), on_z(3)),
                HALF_UP: (rows((z + 3) % 4, 0), on_z(1)),
                HALF_DOWN: (rows((z + 1) % 4, 1), on_z(3)),
            }[kind]
        return remote(ref, ref, z_send.at[kind, r], z_recv.at[kind, r], to)

    def x_copy(kind, e):
        def block(there, half=slice(None)):
            return p_z.at[e, there, half]

        ref, to = {
            UP: (block(x), on_x(1)),
            DOWN: (block(x), on_x(3)),
            HALF_UP: (block((x + 3) % 4, 0), on_x(1)),
            HALF_DOWN: (block((x + 1) % 4, 1), on_x(3)),
        }[kind]
        return remote(ref, ref, x_send.at[kind, e], x_recv.at[kind, e], to)

    def pass_on(copy, r):
        copy(UP, r).wait_recv()
        copy(HALF_UP, r).start()
        copy(DOWN, r).wait_recv()
        copy(HALF_DOWN, r).start()

    def third_done(e):
        third_here(e).wait()

        @pl.loop(1, 8)
        def _(k):
            third(e, k).wait_recv()

    for e in range(2):
        second(e, 0).wait()
        for k in (1, 2, 3):
            second(e, k).wait_recv()
        for p in range(2):
            z_copy(UP, 2 * e + p).start()
            z_copy(DOWN, 2 * e + p).start()
        third_done(e)
        x_copy(UP, e).start()
        x_copy(DOWN, e).start()
        if e == 0:
            k_copy(UP, 0).wait_recv()
            k_pass(HALF_UP).start()
            k_copy(DOWN, 1).wait_recv()
            k_pass(HALF_DOWN).start()

    def core_start(r):
        z_copy(HALF_UP, r).wait_recv()
        z_copy(HALF_DOWN, r).wait_recv()
        z_copy(CORE, r).start()

    pass_on(z_copy, 0)
    pass_on(z_copy, 1)
    core_start(0)
    pass_on(z_copy, 2)
    core_start(1)
    pass_on(x_copy, 0)
    pass_on(z_copy, 3)
    k_copy(UP, 1).wait_recv()
    k_copy(DOWN, 0).wait_recv()
    take_k((y + 3) % 4, k_all.at[(y + 3) % 4])
    take_k((y + 1) % 4, k_all.at[(y + 1) % 4])
    pass_on(x_copy, 1)

    def n_copy(kind, e, side):
        src, dst = {
            HALF_UP: (n_part.at[e, 1, side, pl.ds(0, 224)], n_far.at[0, e, side]),
            HALF_DOWN: (n_part.at[e, 1, side, pl.ds(224, 224)], n_far.at[1, e, side]),
            UP: (n_part.at[e, 0, side], n_got.at[0, e, side]),
            DOWN: (n_part.at[e, 2, side], n_got.at[1, e, side]),
        }[kind]
        to = on_x(1 if kind in (UP, HALF_UP) else 3)
        return remote(src, dst, n_send.at[kind, e, side], n_recv.at[kind, e, side], to)

    def n_passed(r, side):
        e = r // 2

        @pl.when(r % 2 == 0)
        def _():
            n_copy(HALF_UP, e, side).start()
            n_copy(HALF_DOWN, e, side).start()

        @pl.when(r % 2 == 1)
        def _():
            n_copy(HALF_UP, e, side).wait_recv()
            n_part[e, 0, side, 0:224] += n_far[0, e, side]
            n_copy(UP, e, side).start()
            n_copy(HALF_DOWN, e, side).wait_recv()
            n_part[e, 2, side, 224:448] += n_far[1, e, side]
            n_copy(DOWN, e, side).start()

    def take_p(r, half):
        @pl.loop(0, 7)
        def _(k):
            rows = pl.ds(pl.multiple_of(k * 128, 128), 128)
            for i in range(2):
                columns = slice(i * 128, (i + 1) * 128)
                p_high[half, rows, columns], p_low[half, rows, columns] = split(
                    p_x[r // 2, r % 2, i, half, pl.ds(2 * k, 2)].reshape(128, 128)
                )

    def n_dots(there, half):
        return three(k_high[there], k_low[there], p_high[half], p_low[half])

    def n_put(r, side, value, add):
        for i in range(2):
            columns = value[:, i * 128 : (i + 1) * 128]
            n_part[r // 2, 2 * (r % 2) + i, side] = columns + n_part[r // 2, 2 * (r % 2) + i, side] if add else columns

    theirs = 1 - y_hi

    @pl.loop(0, 4)
    def _(r):
        z_copy(CORE, r).wait_recv()

        @pl.when(r < 2)
        def _():
            core_start(r + 2)

        take_p(r, 0)
        take_p(r, 1)
        n_put(r, y_hi, n_dots(y, y_lo) + n_dots(y_hi * 2 + 1 - y_lo, 1 - y_lo), False)
        n_passed(r, y_hi)
        n_put(r, theirs, n_dots(theirs * 2 + 1 - y_lo, 1 - y_lo), False)

    def y_copy(kind, e, s):
        there = (y + {UP: 0, DOWN: 0, HALF_UP: 3, HALF_DOWN: 1}[kind]) % 4
        start = ((there // 2 + s) % 2) * 448 + (224 if kind == HALF_DOWN else 0)
        size = 448 if kind in (UP, DOWN) else 224
        ref = n_all.at[e, there, pl.ds(pl.multiple_of(start, 32), size)]
        to = on_y(1 if kind in (UP, HALF_UP) else 3)
        return remote(ref, ref, y_send.at[kind, e, s], y_recv.at[kind, e, s], to)

    def y_start(e, s):
        side = (y_hi + s) % 2
        n_copy(UP, e, side).wait_recv()
        n_copy(DOWN, e, side).wait_recv()
        rows = pl.ds(pl.multiple_of(side * 448, 64), 448)
        n_all[e, y, rows] = n_part[e, 3, side] + (n_got[0, e, side] + n_got[1, e, side])
        y_copy(UP, e, s).start()
        y_copy(DOWN, e, s).start()

    def y_pass(e, s):
        y_copy(UP, e, s).wait_recv()
        y_copy(HALF_UP, e, s).start()
        y_copy(DOWN, e, s).wait_recv()
        y_copy(HALF_DOWN, e, s).start()

    y_start(0, 0)
    y_start(1, 0)
    k_pass(HALF_UP).wait_recv()
    k_pass(HALF_DOWN).wait_recv()
    take_k((y + 2) % 4, k_all.at[(y + 2) % 4])

    @pl.loop(0, 4)
    def _(r):
        take_p(r, y_lo)
        n_put(r, theirs, n_dots(theirs * 2 + y_lo, y_lo), True)
        n_passed(r, theirs)

    y_pass(0, 0)
    y_start(0, 1)
    y_pass(1, 0)
    y_start(1, 1)

    for e in range(2):
        x_copy(HALF_UP, e).wait_recv()
        x_copy(HALF_DOWN, e).wait_recv()

    @pl.loop(0, 4)
    def _(there):
        for half in range(2):
            rows = slice(half * 448, (half + 1) * 448)
            for e in range(2):
                columns = slice(e * 128, (e + 1) * 128)
                pz_high[there, rows, columns], pz_low[there, rows, columns] = split(p_z[e, there, half].reshape(448, 128))

    y_pass(0, 1)
    y_pass(1, 1)

    def c_copy(e, k):
        there = (z + k) % 4
        return remote(d_part.at[e, 1 - core, there], d_core.at[e, there], c_send.at[e, k], c_recv.at[e, k], other_core)

    def d_copy(e, k):
        return remote(d_part.at[e, core, (z + k) % 4], d_got.at[e, k], d_send.at[e, k], d_recv.at[e, k], on_z(k))

    def over_z(e, k):
        there = (z + k) % 4
        c_copy(e, k).wait_recv()
        d_part[e, core, there] += d_core[e, there]

        @pl.when(k != 0)
        def _():
            d_copy(e, k).start()

    @pl.loop(0, 2)
    def _(e):
        for kind in (HALF_UP, HALF_DOWN):
            for s in range(2):
                y_copy(kind, e, s).wait_recv()
        for low in range(2):
            for high in range(2):
                for k in range(7):
                    rows = slice(k * 128, (k + 1) * 128)
                    lines = slice(high * 128, (high + 1) * 128)
                    t_high[low, lines, rows], t_low[low, lines, rows] = split(n_all[e, 2 * high + low, rows].T)

        @pl.loop(0, 4)
        def _(j):
            k = (j + 1) % 4
            there = (z + k) % 4

            @pl.loop(0, 2)
            def _(turn):
                low = (core + 1 + turn) % 2
                d_part[e, low, there] = three(t_high[low], t_low[low], pz_high[there], pz_low[there])

                @pl.when(turn == 0)
                def _():
                    c_copy(e, k).start()

            @pl.when(j > 0)
            def _():
                over_z(e, j)

        over_z(e, 0)

    def o_copy(e):
        return remote(d_sum.at[e], d_out.at[e], o_send.at[e], o_recv.at[e], at(y_lo, z, y_hi, core, x))

    for e in range(2):
        for k in (1, 3, 2):
            d_copy(e, k).wait_recv()
        d_sum[e] = d_part[e, core, z] + (d_got[e, 1] + d_got[e, 2] + d_got[e, 3])

        @pl.when(stays)
        def _():
            pltpu.make_async_copy(d_sum.at[e], d_out.at[e], o_recv.at[e]).start()

        @pl.when(jnp.logical_not(stays))
        def _():
            o_copy(e).start()

    for e in range(2):
        for half in range(2):
            n_ref[:, half * 256 + e * 128 : half * 256 + (e + 1) * 128] = n_all[
                e, half * 2 + y_lo, pl.ds(pl.multiple_of(y_hi * 448, 64), 448)
            ]

    for e in range(2):
        pltpu.make_async_copy(d_sum.at[e], d_out.at[e], o_recv.at[e]).wait()
        d_ref[0, e] = d_out[e, 0:128]
        d_ref[1, e] = d_out[e, 128:256]

    for e in range(2):

        @pl.loop(1, 16)
        def _(k):
            first(e, k).wait_send()

        @pl.loop(1, 8)
        def _(k):
            third(e, k).wait_send()

        for k in (1, 2, 3):
            second(e, k).wait_send()
            d_copy(e, k).wait_send()
        for kind in range(4):
            x_copy(kind, e).wait_send()
            c_copy(e, kind).wait_send()
            for side in range(2):
                n_copy(kind, e, side).wait_send()
                y_copy(kind, e, side).wait_send()

        @pl.when(jnp.logical_not(stays))
        def _():
            o_copy(e).wait_send()

    for half in range(2):
        k_copy(UP, half).wait_send()
        k_copy(DOWN, half).wait_send()
    k_pass(HALF_UP).wait_send()
    k_pass(HALF_DOWN).wait_send()

    @pl.loop(0, 4)
    def _(r):
        for kind in range(5):
            z_copy(kind, r).wait_send()


def on_device(known_inverse, factor_panel, diag_base, ancestor_map):
    blocks = jnp.arange(28, dtype=jnp.int32)
    inverse = jnp.sum(jnp.where(ancestor_map[None, :] == blocks[:, None], blocks[None, :], 0), axis=1)
    vmem = pl.BlockSpec(memory_space=pltpu.VMEM)
    dma = pltpu.SemaphoreType.DMA
    product, reduced = pl.pallas_call(
        kernel,
        out_shape=(jax.ShapeDtypeStruct((448, 512), F32), jax.ShapeDtypeStruct((2, 2, 128, 256), F32)),
        in_specs=[pl.BlockSpec(memory_space=pltpu.SMEM), vmem, vmem],
        out_specs=(vmem, vmem),
        scratch_shapes=[
            pltpu.VMEM((4, 448, 896), F32),
            pltpu.VMEM((4, 448, 896), BF),
            pltpu.VMEM((4, 448, 896), BF),
            pltpu.VMEM((112, 8, 128), F32),
            pltpu.VMEM((112, 8, 128), F32),
            pltpu.VMEM((2, 2, 56, 8, 128), F32),
            pltpu.VMEM((2, 2, 2, 2, 14, 4, 2, 8, 128), F32),
            pltpu.VMEM((2, 896, 256), BF),
            pltpu.VMEM((2, 896, 256), BF),
            pltpu.VMEM((2, 4, 2, 7, 8, 8, 128), F32),
            pltpu.VMEM((4, 896, 256), BF),
            pltpu.VMEM((4, 896, 256), BF),
            pltpu.VMEM((2, 4, 2, 448, 128), F32),
            pltpu.VMEM((2, 2, 2, 224, 128), F32),
            pltpu.VMEM((2, 2, 2, 448, 128), F32),
            pltpu.VMEM((2, 4, 896, 128), F32),
            pltpu.VMEM((2, 256, 896), BF),
            pltpu.VMEM((2, 256, 896), BF),
            pltpu.VMEM((2, 2, 4, 256, 256), F32),
            pltpu.VMEM((2, 4, 256, 256), F32),
            pltpu.VMEM((2, 4, 256, 256), F32),
            pltpu.VMEM((2, 256, 256), F32),
            pltpu.VMEM((2, 256, 256), F32),
            dma((2, 16)), dma((2, 16)), dma((2, 4)), dma((2, 4)), dma((2, 8)), dma((2, 8)), dma((6,)), dma((4, 2)), dma((4, 2)),
            dma((5, 4)), dma((5, 4)), dma((4, 2)), dma((4, 2)), dma((4, 2, 2)), dma((4, 2, 2)), dma((4, 2, 2)), dma((4, 2, 2)),
            dma((2, 4)), dma((2, 4)), dma((2, 4)), dma((2, 4)), dma((2,)), dma((2,)),
        ],
        compiler_params=pltpu.CompilerParams(collective_id=0, has_side_effects=True, vmem_limit_bytes=60 << 20),
        cost_estimate=pl.CostEstimate(
            flops=6 * (448 * 1792 * 2048 + 256 * 1792 * 2048), bytes_accessed=4 << 20, transcendentals=0
        ),
        name="selected_inverse",
    )(inverse, known_inverse, factor_panel.reshape(7, 8, 8, 512))
    return (-product, diag_base + reduced.reshape(512, 256))


def solution(mesh):
    placed = (P("col", "row"), P("col", "row"), P("row", "col"), P())
    return jax.shard_map(
        on_device,
        mesh=mesh,
        in_specs=placed,
        out_specs=(P("col", "row"), P("row", "col")),
        check_vma=False,
    )
```

```python
import jax
import jax.numpy as jnp
from jax import lax
from jax.experimental import pallas as pl
from jax.experimental.pallas import tpu as pltpu
from jax.sharding import PartitionSpec as P

MESH = pl.DeviceIdType.MESH
BF = jnp.bfloat16
F32 = jnp.float32

UP, DOWN, HALF_UP, HALF_DOWN, CORE = range(5)


def split(value):
    high = value.astype(BF)
    return high, (value - high.astype(F32)).astype(BF)


def three(a_high, a_low, b_high, b_low):
    def dot(a, b):
        return jnp.dot(a, b, preferred_element_type=F32)

    return dot(a_high, b_high) + (dot(a_high, b_low) + dot(a_low, b_high))


def kernel(
    inv_ref, k_ref, f_ref, n_ref, d_ref,
    k_all, k_high, k_low, sent_0, sent_1, picked, p_x, p_high, p_low, p_z, pz_high, pz_low,
    n_part, n_far, n_got, n_all, t_high, t_low, d_part, d_core, d_far, d_got, d_sum, d_out,
    one_send, one_recv, two_send, two_recv, three_send, three_recv, local_sem, k_send, k_recv,
    z_send, z_recv, x_send, x_recv, n_send, n_recv, y_send, y_recv,
    c_send, c_recv, d_send, d_recv, o_send, o_recv,
):
    row, col = lax.axis_index("row"), lax.axis_index("col")
    x, y_lo = row % 4, row // 4
    core, z, y_hi = col % 2, (col // 2) % 4, col // 8
    y, place = y_hi * 2 + y_lo, col % 8

    def at(y_hi_, z_, core_, y_lo_, x_):
        return (y_lo_ * 4 + x_, y_hi_ * 8 + z_ * 2 + core_)

    def on_x(k):
        return (y_lo * 4 + (x + k) % 4, col)

    def on_y(k):
        there = (y + k) % 4
        return at(there // 2, z, core, there % 2, x)

    def on_z(k):
        return (row, y_hi * 8 + ((z + k) % 4) * 2 + core)

    other_core = (row, y_hi * 8 + z * 2 + 1 - core)
    stays = jnp.logical_and(y_hi == y_lo, y_hi == core)

    def remote(src, dst, send, recv, device):
        return pltpu.make_async_remote_copy(
            src_ref=src, dst_ref=dst, send_sem=send, recv_sem=recv, device_id=device, device_id_type=MESH
        )

    barrier = pltpu.get_barrier_semaphore()

    def greet(device):
        pl.semaphore_signal(barrier, inc=1, device_id=device, device_id_type=MESH)

    @pl.loop(1, 16)
    def _(k):
        greet((row, (col + k) % 16))

    for k in (1, 2, 3):
        greet(on_x(k))
    for k in (1, 3):
        greet(on_y(k))

    @pl.when(jnp.logical_not(stays))
    def _():
        greet(at(core, z, y_lo, y_hi, x))

    pl.semaphore_wait(barrier, 21 - stays.astype(jnp.int32))

    sent = (sent_0, sent_1)

    def piece(to, e):
        return f_ref.at[:, to % 8, :, pl.ds(pl.multiple_of((to // 8) * 256 + e * 128, 128), 128)]

    def first(e, k):
        to = (col + k) % 16
        return remote(piece(to, e), sent[e].at[pl.ds(col * 7, 7)], one_send.at[e, k], one_recv.at[e, k], (row, to))

    def first_here(e):
        return pltpu.make_async_copy(piece(col, e), sent[e].at[pl.ds(col * 7, 7)], local_sem.at[e])

    for e in range(2):

        @pl.loop(1, 16)
        def _(k):
            first(e, k).start()

        first_here(e).start()

    def k_copy(kind, half):
        rows = pl.ds(half * 224, 224)
        return remote(
            k_ref.at[rows], k_all.at[y, rows], k_send.at[kind, half], k_recv.at[kind, half], on_y(1 if kind == UP else 3)
        )

    def k_pass(kind):
        rows = pl.ds(0, 224) if kind == HALF_UP else pl.ds(224, 224)
        ref = k_all.at[(y + (3 if kind == HALF_UP else 1)) % 4, rows]
        return remote(ref, ref, k_send.at[kind, 0], k_recv.at[kind, 0], on_y(1 if kind == HALF_UP else 3))

    k_copy(UP, 0).start()
    k_copy(DOWN, 1).start()

    def take_k(there, ref):
        k_high[there], k_low[there] = split(ref[...])

    take_k(y, k_ref)

    def second(e, k):
        to = (x + 4 - k) % 4
        i = (k + 3) % 4
        src = picked.at[e, :, pl.ds(to * 14, 14)]
        dst = p_x.at[e, i // 2, i % 2, :, :, z, core]
        if k == 0:
            return pltpu.make_async_copy(src, dst, local_sem.at[2 + e])
        return remote(src, dst, two_send.at[e, k], two_recv.at[e, k], on_x(4 - k))

    def third(e, k):
        to = (place + k) % 8
        src = picked.at[e, :, pl.ds(to * 7, 7)]
        dst = p_z.at[e, x, :, :, place]
        return remote(src, dst, three_send.at[e, k], three_recv.at[e, k], (row, y_hi * 8 + to))

    def third_here(e):
        src = picked.at[e, :, pl.ds(place * 7, 7)]
        return pltpu.make_async_copy(src, p_z.at[e, x, :, :, place], local_sem.at[4 + e])

    for e in range(2):
        first_here(e).wait()

        @pl.loop(1, 16)
        def _(k):
            first(e, k).wait_recv()

        for j in range(28):
            picked[e, j // 14, (j % 14) * 4 : (j % 14) * 4 + 4] = sent[e][pl.ds(inv_ref[j] * 4, 4)]
        for k in (1, 2, 3, 0):
            second(e, k).start()

        @pl.loop(1, 8)
        def _(k):
            third(e, k).start()

        third_here(e).start()
        if e == 0:
            k_copy(UP, 1).start()
            k_copy(DOWN, 0).start()

    def z_copy(kind, r):
        def rows(there, chunk=slice(None)):
            return p_x.at[r // 2, r % 2, :, chunk, :, there, core]

        if kind == CORE:
            ref, to = p_x.at[r // 2, r % 2, :, :, :, :, core], other_core
        else:
            ref, to = {
                UP: (rows(z), on_z(1)),
                DOWN: (rows(z), on_z(3)),
                HALF_UP: (rows((z + 3) % 4, 0), on_z(1)),
                HALF_DOWN: (rows((z + 1) % 4, 1), on_z(3)),
            }[kind]
        return remote(ref, ref, z_send.at[kind, r], z_recv.at[kind, r], to)

    def x_copy(kind, e):
        def block(there, half=slice(None)):
            return p_z.at[e, there, half]

        ref, to = {
            UP: (block(x), on_x(1)),
            DOWN: (block(x), on_x(3)),
            HALF_UP: (block((x + 3) % 4, 0), on_x(1)),
            HALF_DOWN: (block((x + 1) % 4, 1), on_x(3)),
        }[kind]
        return remote(ref, ref, x_send.at[kind, e], x_recv.at[kind, e], to)

    def pass_on(copy, r):
        copy(UP, r).wait_recv()
        copy(HALF_UP, r).start()
        copy(DOWN, r).wait_recv()
        copy(HALF_DOWN, r).start()

    def third_done(e):
        third_here(e).wait()

        @pl.loop(1, 8)
        def _(k):
            third(e, k).wait_recv()

    for e in range(2):
        second(e, 0).wait()
        for k in (1, 2, 3):
            second(e, k).wait_recv()
        for p in range(2):
            z_copy(UP, 2 * e + p).start()
            z_copy(DOWN, 2 * e + p).start()
        third_done(e)
        x_copy(UP, e).start()
        x_copy(DOWN, e).start()

    def core_start(r):
        z_copy(HALF_UP, r).wait_recv()
        z_copy(HALF_DOWN, r).wait_recv()
        z_copy(CORE, r).start()

    pass_on(z_copy, 0)
    pass_on(z_copy, 1)
    core_start(0)
    pass_on(x_copy, 0)
    core_start(1)
    for half in range(2):
        k_copy(UP, half).wait_recv()
    k_pass(HALF_UP).start()
    for half in range(2):
        k_copy(DOWN, half).wait_recv()
    k_pass(HALF_DOWN).start()
    pass_on(z_copy, 2)
    pass_on(z_copy, 3)
    take_k((y + 3) % 4, k_all.at[(y + 3) % 4])
    take_k((y + 1) % 4, k_all.at[(y + 1) % 4])
    pass_on(x_copy, 1)

    def n_copy(kind, e, side):
        src, dst = {
            HALF_UP: (n_part.at[e, 1, side, pl.ds(0, 224)], n_far.at[0, e, side]),
            HALF_DOWN: (n_part.at[e, 1, side, pl.ds(224, 224)], n_far.at[1, e, side]),
            UP: (n_part.at[e, 0, side], n_got.at[0, e, side]),
            DOWN: (n_part.at[e, 2, side], n_got.at[1, e, side]),
        }[kind]
        to = on_x(1 if kind in (UP, HALF_UP) else 3)
        return remote(src, dst, n_send.at[kind, e, side], n_recv.at[kind, e, side], to)

    def n_far_start(e, side):
        n_copy(HALF_UP, e, side).start()
        n_copy(HALF_DOWN, e, side).start()

    def n_near_start(e, side):
        n_copy(HALF_UP, e, side).wait_recv()
        n_part[e, 0, side, 0:224] += n_far[0, e, side]
        n_copy(UP, e, side).start()
        n_copy(HALF_DOWN, e, side).wait_recv()
        n_part[e, 2, side, 224:448] += n_far[1, e, side]
        n_copy(DOWN, e, side).start()

    def take_p(r, half):
        @pl.loop(0, 7)
        def _(k):
            rows = pl.ds(pl.multiple_of(k * 128, 128), 128)
            for i in range(2):
                columns = slice(i * 128, (i + 1) * 128)
                p_high[half, rows, columns], p_low[half, rows, columns] = split(
                    p_x[r // 2, r % 2, i, half, pl.ds(2 * k, 2)].reshape(128, 128)
                )

    def n_dots(there, half):
        return three(k_high[there], k_low[there], p_high[half], p_low[half])

    def n_put(r, side, value, add):
        for i in range(2):
            columns = value[:, i * 128 : (i + 1) * 128]
            n_part[r // 2, 2 * (r % 2) + i, side] = columns + n_part[r // 2, 2 * (r % 2) + i, side] if add else columns

    theirs = 1 - y_hi

    @pl.loop(0, 4)
    def _(r):
        z_copy(CORE, r).wait_recv()

        @pl.when(r < 2)
        def _():
            core_start(r + 2)

        take_p(r, 0)
        take_p(r, 1)
        n_put(r, y_hi, n_dots(y, y_lo) + n_dots(y_hi * 2 + 1 - y_lo, 1 - y_lo), False)

        @pl.when(r % 2 == 0)
        def _():
            n_far_start(r // 2, y_hi)

        n_put(r, theirs, n_dots(theirs * 2 + 1 - y_lo, 1 - y_lo), False)

        @pl.when(r % 2 == 1)
        def _():
            n_near_start(r // 2, y_hi)

    def y_copy(kind, e, s):
        there = (y + {UP: 0, DOWN: 0, HALF_UP: 3, HALF_DOWN: 1}[kind]) % 4
        start = ((there // 2 + s) % 2) * 448 + (224 if kind == HALF_DOWN else 0)
        size = 448 if kind in (UP, DOWN) else 224
        ref = n_all.at[e, there, pl.ds(pl.multiple_of(start, 32), size)]
        to = on_y(1 if kind in (UP, HALF_UP) else 3)
        return remote(ref, ref, y_send.at[kind, e, s], y_recv.at[kind, e, s], to)

    def y_start(e, s):
        side = (y_hi + s) % 2
        n_copy(UP, e, side).wait_recv()
        n_copy(DOWN, e, side).wait_recv()
        rows = pl.ds(pl.multiple_of(side * 448, 64), 448)
        n_all[e, y, rows] = n_part[e, 3, side] + (n_got[0, e, side] + n_got[1, e, side])
        y_copy(UP, e, s).start()
        y_copy(DOWN, e, s).start()

    def y_pass(e, s):
        y_copy(UP, e, s).wait_recv()
        y_copy(HALF_UP, e, s).start()
        y_copy(DOWN, e, s).wait_recv()
        y_copy(HALF_DOWN, e, s).start()

    y_start(0, 0)
    y_start(1, 0)
    k_pass(HALF_UP).wait_recv()
    k_pass(HALF_DOWN).wait_recv()
    take_k((y + 2) % 4, k_all.at[(y + 2) % 4])

    @pl.loop(0, 4)
    def _(t):
        r = (t % 2) * 2 + t // 2
        take_p(r, y_lo)
        n_put(r, theirs, n_dots(theirs * 2 + y_lo, y_lo), True)

        @pl.when(t < 2)
        def _():
            n_far_start(t, theirs)

        @pl.when(t >= 2)
        def _():
            n_near_start(t - 2, theirs)

    y_pass(0, 0)
    y_start(0, 1)
    y_pass(1, 0)
    y_start(1, 1)

    for e in range(2):
        x_copy(HALF_UP, e).wait_recv()
        x_copy(HALF_DOWN, e).wait_recv()

    @pl.loop(0, 4)
    def _(there):
        for half in range(2):
            rows = slice(half * 448, (half + 1) * 448)
            for e in range(2):
                columns = slice(e * 128, (e + 1) * 128)
                pz_high[there, rows, columns], pz_low[there, rows, columns] = split(p_z[e, there, half].reshape(448, 128))

    def c_copy(e, k):
        there = (z + k) % 4
        return remote(d_part.at[e, 1 - core, there], d_core.at[e, there], c_send.at[e, k], c_recv.at[e, k], other_core)

    def d_copy(kind, e):
        src, dst = {
            HALF_UP: (d_part.at[e, core, (z + 2) % 4, pl.ds(0, 128)], d_far.at[0, e]),
            HALF_DOWN: (d_part.at[e, core, (z + 2) % 4, pl.ds(128, 128)], d_far.at[1, e]),
            UP: (d_part.at[e, core, (z + 1) % 4], d_got.at[0, e]),
            DOWN: (d_part.at[e, core, (z + 3) % 4], d_got.at[1, e]),
        }[kind]
        return remote(src, dst, d_send.at[kind, e], d_recv.at[kind, e], on_z(1 if kind in (UP, HALF_UP) else 3))

    def d_cores(e, k):
        there = (z + k) % 4
        c_copy(e, k).wait_recv()
        d_part[e, core, there] += d_core[e, there]

    def d_far_start(e):
        d_cores(e, 2)
        d_copy(HALF_UP, e).start()
        d_copy(HALF_DOWN, e).start()

    def d_near_start(e):
        d_copy(HALF_UP, e).wait_recv()
        d_part[e, core, (z + 1) % 4, 0:128] += d_far[0, e]
        d_copy(UP, e).start()
        d_copy(HALF_DOWN, e).wait_recv()
        d_part[e, core, (z + 3) % 4, 128:256] += d_far[1, e]
        d_copy(DOWN, e).start()

    @pl.loop(0, 2)
    def _(e):
        y_pass(e, 1)
        for kind in (HALF_UP, HALF_DOWN):
            for s in range(2):
                y_copy(kind, e, s).wait_recv()
        for low in range(2):
            for high in range(2):
                for k in range(7):
                    rows = slice(k * 128, (k + 1) * 128)
                    lines = slice(high * 128, (high + 1) * 128)
                    t_high[low, lines, rows], t_low[low, lines, rows] = split(n_all[e, 2 * high + low, rows].T)

        @pl.loop(0, 4)
        def _(j):
            k = (j + 2) % 4
            there = (z + k) % 4

            @pl.loop(0, 2)
            def _(turn):
                low = (core + 1 + turn) % 2
                d_part[e, low, there] = three(t_high[low], t_low[low], pz_high[there], pz_low[there])

                @pl.when(turn == 0)
                def _():
                    c_copy(e, k).start()

            @pl.when(j == 1)
            def _():
                d_far_start(e)

        d_cores(e, 3)
        d_cores(e, 1)
        d_near_start(e)
        d_cores(e, 0)

    def o_copy(e):
        return remote(d_sum.at[e], d_out.at[e], o_send.at[e], o_recv.at[e], at(y_lo, z, y_hi, core, x))

    for e in range(2):
        d_copy(UP, e).wait_recv()
        d_copy(DOWN, e).wait_recv()
        d_sum[e] = d_part[e, core, z] + (d_got[0, e] + d_got[1, e])

        @pl.when(stays)
        def _():
            pltpu.make_async_copy(d_sum.at[e], d_out.at[e], o_recv.at[e]).start()

        @pl.when(jnp.logical_not(stays))
        def _():
            o_copy(e).start()

    for e in range(2):
        for half in range(2):
            n_ref[:, half * 256 + e * 128 : half * 256 + (e + 1) * 128] = n_all[
                e, half * 2 + y_lo, pl.ds(pl.multiple_of(y_hi * 448, 64), 448)
            ]

    for e in range(2):
        pltpu.make_async_copy(d_sum.at[e], d_out.at[e], o_recv.at[e]).wait()
        d_ref[0, e] = d_out[e, 0:128]
        d_ref[1, e] = d_out[e, 128:256]

    for e in range(2):

        @pl.loop(1, 16)
        def _(k):
            first(e, k).wait_send()

        @pl.loop(1, 8)
        def _(k):
            third(e, k).wait_send()

        for k in (1, 2, 3):
            second(e, k).wait_send()
        for kind in range(4):
            x_copy(kind, e).wait_send()
            c_copy(e, kind).wait_send()
            d_copy(kind, e).wait_send()
            for side in range(2):
                n_copy(kind, e, side).wait_send()
                y_copy(kind, e, side).wait_send()

        @pl.when(jnp.logical_not(stays))
        def _():
            o_copy(e).wait_send()

    for half in range(2):
        k_copy(UP, half).wait_send()
        k_copy(DOWN, half).wait_send()
    k_pass(HALF_UP).wait_send()
    k_pass(HALF_DOWN).wait_send()

    @pl.loop(0, 4)
    def _(r):
        for kind in range(5):
            z_copy(kind, r).wait_send()


def on_device(known_inverse, factor_panel, diag_base, ancestor_map):
    blocks = jnp.arange(28, dtype=jnp.int32)
    inverse = jnp.sum(jnp.where(ancestor_map[None, :] == blocks[:, None], blocks[None, :], 0), axis=1)
    vmem = pl.BlockSpec(memory_space=pltpu.VMEM)
    dma = pltpu.SemaphoreType.DMA
    product, reduced = pl.pallas_call(
        kernel,
        out_shape=(jax.ShapeDtypeStruct((448, 512), F32), jax.ShapeDtypeStruct((2, 2, 128, 256), F32)),
        in_specs=[pl.BlockSpec(memory_space=pltpu.SMEM), vmem, vmem],
        out_specs=(vmem, vmem),
        scratch_shapes=[
            pltpu.VMEM((4, 448, 896), F32),
            pltpu.VMEM((4, 448, 896), BF),
            pltpu.VMEM((4, 448, 896), BF),
            pltpu.VMEM((112, 8, 128), F32),
            pltpu.VMEM((112, 8, 128), F32),
            pltpu.VMEM((2, 2, 56, 8, 128), F32),
            pltpu.VMEM((2, 2, 2, 2, 14, 4, 2, 8, 128), F32),
            pltpu.VMEM((2, 896, 256), BF),
            pltpu.VMEM((2, 896, 256), BF),
            pltpu.VMEM((2, 4, 2, 7, 8, 8, 128), F32),
            pltpu.VMEM((4, 896, 256), BF),
            pltpu.VMEM((4, 896, 256), BF),
            pltpu.VMEM((2, 4, 2, 448, 128), F32),
            pltpu.VMEM((2, 2, 2, 224, 128), F32),
            pltpu.VMEM((2, 2, 2, 448, 128), F32),
            pltpu.VMEM((2, 4, 896, 128), F32),
            pltpu.VMEM((2, 256, 896), BF),
            pltpu.VMEM((2, 256, 896), BF),
            pltpu.VMEM((2, 2, 4, 256, 256), F32),
            pltpu.VMEM((2, 4, 256, 256), F32),
            pltpu.VMEM((2, 2, 128, 256), F32),
            pltpu.VMEM((2, 2, 256, 256), F32),
            pltpu.VMEM((2, 256, 256), F32),
            pltpu.VMEM((2, 256, 256), F32),
            dma((2, 16)), dma((2, 16)), dma((2, 4)), dma((2, 4)), dma((2, 8)), dma((2, 8)), dma((6,)), dma((4, 2)), dma((4, 2)),
            dma((5, 4)), dma((5, 4)), dma((4, 2)), dma((4, 2)), dma((4, 2, 2)), dma((4, 2, 2)), dma((4, 2, 2)), dma((4, 2, 2)),
            dma((2, 4)), dma((2, 4)), dma((4, 2)), dma((4, 2)), dma((2,)), dma((2,)),
        ],
        compiler_params=pltpu.CompilerParams(collective_id=0, has_side_effects=True, vmem_limit_bytes=60 << 20),
        cost_estimate=pl.CostEstimate(
            flops=6 * (448 * 1792 * 2048 + 256 * 1792 * 2048), bytes_accessed=4 << 20, transcendentals=0
        ),
        name="selected_inverse",
    )(inverse, known_inverse, factor_panel.reshape(7, 8, 8, 512))
    return (-product, diag_base + reduced.reshape(512, 256))


def solution(mesh):
    placed = (P("col", "row"), P("col", "row"), P("row", "col"), P())
    return jax.shard_map(
        on_device,
        mesh=mesh,
        in_specs=placed,
        out_specs=(P("col", "row"), P("row", "col")),
        check_vma=False,
    )
```

```python
import jax
import jax.numpy as jnp
from jax import lax
from jax.experimental import pallas as pl
from jax.experimental.pallas import tpu as pltpu
from jax.sharding import PartitionSpec as P

MESH = pl.DeviceIdType.MESH
BF = jnp.bfloat16
F32 = jnp.float32

UP, DOWN, HALF_UP, HALF_DOWN, CORE = range(5)


def split(value):
    high = value.astype(BF)
    return high, (value - high.astype(F32)).astype(BF)


def three(a_high, a_low, b_high, b_low):
    def dot(a, b):
        return jnp.dot(a, b, preferred_element_type=F32)

    return dot(a_high, b_high) + (dot(a_high, b_low) + dot(a_low, b_high))


def kernel(
    inv_ref, k_ref, f_ref, n_ref, d_ref,
    k_all, k_high, k_low, sent_0, sent_1, picked, p_x, p_high, p_low, p_z, pz_high, pz_low,
    n_part, n_far, n_got, n_all, t_high, t_low, d_part, d_core, d_far, d_got, d_sum, d_out,
    one_send, one_recv, two_send, two_recv, three_send, three_recv, local_sem, k_send, k_recv,
    z_send, z_recv, x_send, x_recv, n_send, n_recv, y_send, y_recv,
    c_send, c_recv, d_send, d_recv, o_send, o_recv,
):
    row, col = lax.axis_index("row"), lax.axis_index("col")
    x, y_lo = row % 4, row // 4
    core, z, y_hi = col % 2, (col // 2) % 4, col // 8
    y, place = y_hi * 2 + y_lo, col % 8

    def at(y_hi_, z_, core_, y_lo_, x_):
        return (y_lo_ * 4 + x_, y_hi_ * 8 + z_ * 2 + core_)

    def on_x(k):
        return (y_lo * 4 + (x + k) % 4, col)

    def on_y(k):
        there = (y + k) % 4
        return at(there // 2, z, core, there % 2, x)

    def on_z(k):
        return (row, y_hi * 8 + ((z + k) % 4) * 2 + core)

    other_core = (row, y_hi * 8 + z * 2 + 1 - core)
    stays = jnp.logical_and(y_hi == y_lo, y_hi == core)

    def remote(src, dst, send, recv, device):
        return pltpu.make_async_remote_copy(
            src_ref=src, dst_ref=dst, send_sem=send, recv_sem=recv, device_id=device, device_id_type=MESH
        )

    barrier = pltpu.get_barrier_semaphore()

    def greet(device):
        pl.semaphore_signal(barrier, inc=1, device_id=device, device_id_type=MESH)

    @pl.loop(1, 16)
    def _(k):
        greet((row, (col + k) % 16))

    for k in (1, 2, 3):
        greet(on_x(k))
    for k in (1, 3):
        greet(on_y(k))

    @pl.when(jnp.logical_not(stays))
    def _():
        greet(at(core, z, y_lo, y_hi, x))

    pl.semaphore_wait(barrier, 21 - stays.astype(jnp.int32))

    sent = (sent_0, sent_1)

    def piece(to, e):
        return f_ref.at[:, to % 8, :, pl.ds(pl.multiple_of((to // 8) * 256 + e * 128, 128), 128)]

    def first(e, k):
        to = (col + k) % 16
        return remote(piece(to, e), sent[e].at[pl.ds(col * 7, 7)], one_send.at[e, k], one_recv.at[e, k], (row, to))

    def first_here(e):
        return pltpu.make_async_copy(piece(col, e), sent[e].at[pl.ds(col * 7, 7)], local_sem.at[e])

    for e in range(2):

        @pl.loop(1, 16)
        def _(k):
            first(e, k).start()

        first_here(e).start()

    def k_copy(kind, half):
        rows = pl.ds(half * 224, 224)
        return remote(
            k_ref.at[rows], k_all.at[y, rows], k_send.at[kind, half], k_recv.at[kind, half], on_y(1 if kind == UP else 3)
        )

    def k_pass(kind):
        rows = pl.ds(0, 224) if kind == HALF_UP else pl.ds(224, 224)
        ref = k_all.at[(y + (3 if kind == HALF_UP else 1)) % 4, rows]
        return remote(ref, ref, k_send.at[kind, 0], k_recv.at[kind, 0], on_y(1 if kind == HALF_UP else 3))

    k_copy(UP, 0).start()
    k_copy(DOWN, 1).start()

    def take_k(there, ref):
        k_high[there], k_low[there] = split(ref[...])

    take_k(y, k_ref)

    def second(e, k):
        to = (x + 4 - k) % 4
        i = (k + 3) % 4
        src = picked.at[e, :, pl.ds(to * 14, 14)]
        dst = p_x.at[e, i // 2, i % 2, :, :, z, core]
        if k == 0:
            return pltpu.make_async_copy(src, dst, local_sem.at[2 + e])
        return remote(src, dst, two_send.at[e, k], two_recv.at[e, k], on_x(4 - k))

    def third(e, k):
        to = (place + k) % 8
        src = picked.at[e, :, pl.ds(to * 7, 7)]
        dst = p_z.at[e, x, :, :, place]
        return remote(src, dst, three_send.at[e, k], three_recv.at[e, k], (row, y_hi * 8 + to))

    def third_here(e):
        src = picked.at[e, :, pl.ds(place * 7, 7)]
        return pltpu.make_async_copy(src, p_z.at[e, x, :, :, place], local_sem.at[4 + e])

    for e in range(2):
        first_here(e).wait()

        @pl.loop(1, 16)
        def _(k):
            first(e, k).wait_recv()

        for j in range(28):
            picked[e, j // 14, (j % 14) * 4 : (j % 14) * 4 + 4] = sent[e][pl.ds(inv_ref[j] * 4, 4)]
        for k in (1, 2, 3, 0):
            second(e, k).start()

        @pl.loop(1, 8)
        def _(k):
            third(e, k).start()

        third_here(e).start()
        if e == 0:
            k_copy(UP, 1).start()
            k_copy(DOWN, 0).start()

    def z_copy(kind, r):
        def rows(there, chunk=slice(None)):
            return p_x.at[r // 2, r % 2, :, chunk, :, there, core]

        if kind == CORE:
            ref, to = p_x.at[r // 2, r % 2, :, :, :, :, core], other_core
        else:
            ref, to = {
                UP: (rows(z), on_z(1)),
                DOWN: (rows(z), on_z(3)),
                HALF_UP: (rows((z + 3) % 4, 0), on_z(1)),
                HALF_DOWN: (rows((z + 1) % 4, 1), on_z(3)),
            }[kind]
        return remote(ref, ref, z_send.at[kind, r], z_recv.at[kind, r], to)

    def x_copy(kind, e):
        def block(there, half=slice(None)):
            return p_z.at[e, there, half]

        ref, to = {
            UP: (block(x), on_x(1)),
            DOWN: (block(x), on_x(3)),
            HALF_UP: (block((x + 3) % 4, 0), on_x(1)),
            HALF_DOWN: (block((x + 1) % 4, 1), on_x(3)),
        }[kind]
        return remote(ref, ref, x_send.at[kind, e], x_recv.at[kind, e], to)

    def pass_on(copy, r):
        copy(UP, r).wait_recv()
        copy(HALF_UP, r).start()
        copy(DOWN, r).wait_recv()
        copy(HALF_DOWN, r).start()

    def third_done(e):
        third_here(e).wait()

        @pl.loop(1, 8)
        def _(k):
            third(e, k).wait_recv()

    for e in range(2):
        second(e, 0).wait()
        for k in (1, 2, 3):
            second(e, k).wait_recv()
        for p in range(2):
            z_copy(UP, 2 * e + p).start()
            z_copy(DOWN, 2 * e + p).start()
        third_done(e)
        x_copy(UP, e).start()
        x_copy(DOWN, e).start()

    def core_start(r):
        z_copy(HALF_UP, r).wait_recv()
        z_copy(HALF_DOWN, r).wait_recv()
        z_copy(CORE, r).start()

    pass_on(z_copy, 0)
    pass_on(z_copy, 1)
    core_start(0)
    pass_on(x_copy, 0)
    core_start(1)
    for half in range(2):
        k_copy(UP, half).wait_recv()
    k_pass(HALF_UP).start()
    for half in range(2):
        k_copy(DOWN, half).wait_recv()
    k_pass(HALF_DOWN).start()
    pass_on(z_copy, 2)
    pass_on(z_copy, 3)
    take_k((y + 3) % 4, k_all.at[(y + 3) % 4])
    take_k((y + 1) % 4, k_all.at[(y + 1) % 4])
    pass_on(x_copy, 1)

    def n_copy(kind, e, side):
        src, dst = {
            HALF_UP: (n_part.at[e, 1, side, pl.ds(0, 224)], n_far.at[0, e, side]),
            HALF_DOWN: (n_part.at[e, 1, side, pl.ds(224, 224)], n_far.at[1, e, side]),
            UP: (n_part.at[e, 0, side], n_got.at[0, e, side]),
            DOWN: (n_part.at[e, 2, side], n_got.at[1, e, side]),
        }[kind]
        to = on_x(1 if kind in (UP, HALF_UP) else 3)
        return remote(src, dst, n_send.at[kind, e, side], n_recv.at[kind, e, side], to)

    def n_far_start(e, side):
        n_copy(HALF_UP, e, side).start()
        n_copy(HALF_DOWN, e, side).start()

    def n_near_start(e, side):
        n_copy(HALF_UP, e, side).wait_recv()
        n_part[e, 0, side, 0:224] += n_far[0, e, side]
        n_copy(UP, e, side).start()
        n_copy(HALF_DOWN, e, side).wait_recv()
        n_part[e, 2, side, 224:448] += n_far[1, e, side]
        n_copy(DOWN, e, side).start()

    def take_p(r, half):
        @pl.loop(0, 7)
        def _(k):
            rows = pl.ds(pl.multiple_of(k * 128, 128), 128)
            for i in range(2):
                columns = slice(i * 128, (i + 1) * 128)
                p_high[half, rows, columns], p_low[half, rows, columns] = split(
                    p_x[r // 2, r % 2, i, half, pl.ds(2 * k, 2)].reshape(128, 128)
                )

    def n_dots(there, half):
        return three(k_high[there], k_low[there], p_high[half], p_low[half])

    def n_put(r, side, value, add):
        for i in range(2):
            columns = value[:, i * 128 : (i + 1) * 128]
            n_part[r // 2, 2 * (r % 2) + i, side] = columns + n_part[r // 2, 2 * (r % 2) + i, side] if add else columns

    theirs = 1 - y_hi

    @pl.loop(0, 4)
    def _(r):
        z_copy(CORE, r).wait_recv()

        @pl.when(r < 2)
        def _():
            core_start(r + 2)

        take_p(r, 0)
        take_p(r, 1)
        n_put(r, y_hi, n_dots(y, y_lo) + n_dots(y_hi * 2 + 1 - y_lo, 1 - y_lo), False)

        @pl.when(r % 2 == 0)
        def _():
            n_far_start(r // 2, y_hi)

        n_put(r, theirs, n_dots(theirs * 2 + 1 - y_lo, 1 - y_lo), False)

        @pl.when(r % 2 == 1)
        def _():
            n_near_start(r // 2, y_hi)

    def y_copy(kind, e, s):
        there = (y + {UP: 0, DOWN: 0, HALF_UP: 3, HALF_DOWN: 1}[kind]) % 4
        start = ((there // 2 + s) % 2) * 448 + (224 if kind == HALF_DOWN else 0)
        size = 448 if kind in (UP, DOWN) else 224
        ref = n_all.at[e, there, pl.ds(pl.multiple_of(start, 32), size)]
        to = on_y(1 if kind in (UP, HALF_UP) else 3)
        return remote(ref, ref, y_send.at[kind, e, s], y_recv.at[kind, e, s], to)

    def y_start(e, s):
        side = (y_hi + s) % 2
        n_copy(UP, e, side).wait_recv()
        n_copy(DOWN, e, side).wait_recv()
        rows = pl.ds(pl.multiple_of(side * 448, 64), 448)
        n_all[e, y, rows] = n_part[e, 3, side] + (n_got[0, e, side] + n_got[1, e, side])
        y_copy(UP, e, s).start()
        y_copy(DOWN, e, s).start()

    def y_pass(e, s):
        y_copy(UP, e, s).wait_recv()
        y_copy(HALF_UP, e, s).start()
        y_copy(DOWN, e, s).wait_recv()
        y_copy(HALF_DOWN, e, s).start()

    y_start(0, 0)
    k_pass(HALF_UP).wait_recv()
    k_pass(HALF_DOWN).wait_recv()
    take_k((y + 2) % 4, k_all.at[(y + 2) % 4])

    @pl.loop(0, 4)
    def _(r):
        take_p(r, y_lo)
        n_put(r, theirs, n_dots(theirs * 2 + y_lo, y_lo), True)

        @pl.when(r % 2 == 0)
        def _():
            n_far_start(r // 2, theirs)

        @pl.when(r % 2 == 1)
        def _():
            n_near_start(r // 2, theirs)

    y_start(1, 0)
    y_pass(0, 0)

    for e in range(2):
        x_copy(HALF_UP, e).wait_recv()
        x_copy(HALF_DOWN, e).wait_recv()

    @pl.loop(0, 4)
    def _(there):
        for half in range(2):
            rows = slice(half * 448, (half + 1) * 448)
            for e in range(2):
                columns = slice(e * 128, (e + 1) * 128)
                pz_high[there, rows, columns], pz_low[there, rows, columns] = split(p_z[e, there, half].reshape(448, 128))

    y_start(0, 1)
    y_pass(1, 0)
    y_start(1, 1)
    y_pass(0, 1)

    def c_copy(e, k):
        there = (z + k) % 4
        return remote(d_part.at[e, 1 - core, there], d_core.at[e, there], c_send.at[e, k], c_recv.at[e, k], other_core)

    def d_copy(kind, e):
        src, dst = {
            HALF_UP: (d_part.at[e, core, (z + 2) % 4, pl.ds(0, 128)], d_far.at[0, e]),
            HALF_DOWN: (d_part.at[e, core, (z + 2) % 4, pl.ds(128, 128)], d_far.at[1, e]),
            UP: (d_part.at[e, core, (z + 1) % 4], d_got.at[0, e]),
            DOWN: (d_part.at[e, core, (z + 3) % 4], d_got.at[1, e]),
        }[kind]
        return remote(src, dst, d_send.at[kind, e], d_recv.at[kind, e], on_z(1 if kind in (UP, HALF_UP) else 3))

    def d_cores(e, k):
        there = (z + k) % 4
        c_copy(e, k).wait_recv()
        d_part[e, core, there] += d_core[e, there]

    def d_far_start(e):
        d_cores(e, 2)
        d_copy(HALF_UP, e).start()
        d_copy(HALF_DOWN, e).start()

    def d_near_start(e):
        d_copy(HALF_UP, e).wait_recv()
        d_part[e, core, (z + 1) % 4, 0:128] += d_far[0, e]
        d_copy(UP, e).start()
        d_copy(HALF_DOWN, e).wait_recv()
        d_part[e, core, (z + 3) % 4, 128:256] += d_far[1, e]
        d_copy(DOWN, e).start()

    @pl.loop(0, 2)
    def _(e):
        for kind in (HALF_UP, HALF_DOWN):
            for s in range(2):
                y_copy(kind, e, s).wait_recv()
        for low in range(2):
            for high in range(2):
                for k in range(7):
                    rows = slice(k * 128, (k + 1) * 128)
                    lines = slice(high * 128, (high + 1) * 128)
                    t_high[low, lines, rows], t_low[low, lines, rows] = split(n_all[e, 2 * high + low, rows].T)

        @pl.loop(0, 4)
        def _(j):
            k = (j + 2) % 4
            there = (z + k) % 4

            @pl.loop(0, 2)
            def _(turn):
                low = (core + 1 + turn) % 2
                d_part[e, low, there] = three(t_high[low], t_low[low], pz_high[there], pz_low[there])

                @pl.when(turn == 0)
                def _():
                    c_copy(e, k).start()

            @pl.when(j == 1)
            def _():
                d_far_start(e)

            @pl.when(jnp.logical_and(j == 1, e == 0))
            def _():
                y_pass(1, 1)

            @pl.when(jnp.logical_and(j == 0, e == 1))
            def _():
                d_near_start(0)

        d_cores(e, 3)
        d_cores(e, 1)
        d_cores(e, 0)

    d_near_start(1)

    def o_copy(e):
        return remote(d_sum.at[e], d_out.at[e], o_send.at[e], o_recv.at[e], at(y_lo, z, y_hi, core, x))

    for e in range(2):
        d_copy(UP, e).wait_recv()
        d_copy(DOWN, e).wait_recv()
        d_sum[e] = d_part[e, core, z] + (d_got[0, e] + d_got[1, e])

        @pl.when(stays)
        def _():
            pltpu.make_async_copy(d_sum.at[e], d_out.at[e], o_recv.at[e]).start()

        @pl.when(jnp.logical_not(stays))
        def _():
            o_copy(e).start()

    for e in range(2):
        for half in range(2):
            n_ref[:, half * 256 + e * 128 : half * 256 + (e + 1) * 128] = n_all[
                e, half * 2 + y_lo, pl.ds(pl.multiple_of(y_hi * 448, 64), 448)
            ]

    for e in range(2):
        pltpu.make_async_copy(d_sum.at[e], d_out.at[e], o_recv.at[e]).wait()
        d_ref[0, e] = d_out[e, 0:128]
        d_ref[1, e] = d_out[e, 128:256]

    for e in range(2):

        @pl.loop(1, 16)
        def _(k):
            first(e, k).wait_send()

        @pl.loop(1, 8)
        def _(k):
            third(e, k).wait_send()

        for k in (1, 2, 3):
            second(e, k).wait_send()
        for kind in range(4):
            x_copy(kind, e).wait_send()
            c_copy(e, kind).wait_send()
            d_copy(kind, e).wait_send()
            for side in range(2):
                n_copy(kind, e, side).wait_send()
                y_copy(kind, e, side).wait_send()

        @pl.when(jnp.logical_not(stays))
        def _():
            o_copy(e).wait_send()

    for half in range(2):
        k_copy(UP, half).wait_send()
        k_copy(DOWN, half).wait_send()
    k_pass(HALF_UP).wait_send()
    k_pass(HALF_DOWN).wait_send()

    @pl.loop(0, 4)
    def _(r):
        for kind in range(5):
            z_copy(kind, r).wait_send()


def on_device(known_inverse, factor_panel, diag_base, ancestor_map):
    blocks = jnp.arange(28, dtype=jnp.int32)
    inverse = jnp.sum(jnp.where(ancestor_map[None, :] == blocks[:, None], blocks[None, :], 0), axis=1)
    vmem = pl.BlockSpec(memory_space=pltpu.VMEM)
    dma = pltpu.SemaphoreType.DMA
    product, reduced = pl.pallas_call(
        kernel,
        out_shape=(jax.ShapeDtypeStruct((448, 512), F32), jax.ShapeDtypeStruct((2, 2, 128, 256), F32)),
        in_specs=[pl.BlockSpec(memory_space=pltpu.SMEM), vmem, vmem],
        out_specs=(vmem, vmem),
        scratch_shapes=[
            pltpu.VMEM((4, 448, 896), F32),
            pltpu.VMEM((4, 448, 896), BF),
            pltpu.VMEM((4, 448, 896), BF),
            pltpu.VMEM((112, 8, 128), F32),
            pltpu.VMEM((112, 8, 128), F32),
            pltpu.VMEM((2, 2, 56, 8, 128), F32),
            pltpu.VMEM((2, 2, 2, 2, 14, 4, 2, 8, 128), F32),
            pltpu.VMEM((2, 896, 256), BF),
            pltpu.VMEM((2, 896, 256), BF),
            pltpu.VMEM((2, 4, 2, 7, 8, 8, 128), F32),
            pltpu.VMEM((4, 896, 256), BF),
            pltpu.VMEM((4, 896, 256), BF),
            pltpu.VMEM((2, 4, 2, 448, 128), F32),
            pltpu.VMEM((2, 2, 2, 224, 128), F32),
            pltpu.VMEM((2, 2, 2, 448, 128), F32),
            pltpu.VMEM((2, 4, 896, 128), F32),
            pltpu.VMEM((2, 256, 896), BF),
            pltpu.VMEM((2, 256, 896), BF),
            pltpu.VMEM((2, 2, 4, 256, 256), F32),
            pltpu.VMEM((2, 4, 256, 256), F32),
            pltpu.VMEM((2, 2, 128, 256), F32),
            pltpu.VMEM((2, 2, 256, 256), F32),
            pltpu.VMEM((2, 256, 256), F32),
            pltpu.VMEM((2, 256, 256), F32),
            dma((2, 16)), dma((2, 16)), dma((2, 4)), dma((2, 4)), dma((2, 8)), dma((2, 8)), dma((6,)), dma((4, 2)), dma((4, 2)),
            dma((5, 4)), dma((5, 4)), dma((4, 2)), dma((4, 2)), dma((4, 2, 2)), dma((4, 2, 2)), dma((4, 2, 2)), dma((4, 2, 2)),
            dma((2, 4)), dma((2, 4)), dma((4, 2)), dma((4, 2)), dma((2,)), dma((2,)),
        ],
        compiler_params=pltpu.CompilerParams(collective_id=0, has_side_effects=True, vmem_limit_bytes=60 << 20),
        cost_estimate=pl.CostEstimate(
            flops=6 * (448 * 1792 * 2048 + 256 * 1792 * 2048), bytes_accessed=4 << 20, transcendentals=0
        ),
        name="selected_inverse",
    )(inverse, known_inverse, factor_panel.reshape(7, 8, 8, 512))
    return (-product, diag_base + reduced.reshape(512, 256))


def solution(mesh):
    placed = (P("col", "row"), P("col", "row"), P("row", "col"), P())
    return jax.shard_map(
        on_device,
        mesh=mesh,
        in_specs=placed,
        out_specs=(P("col", "row"), P("row", "col")),
        check_vma=False,
    )
```

```python
import jax
import jax.numpy as jnp
from jax import lax
from jax.experimental import pallas as pl
from jax.experimental.pallas import tpu as pltpu
from jax.sharding import PartitionSpec as P

MESH = pl.DeviceIdType.MESH
BF = jnp.bfloat16
F32 = jnp.float32

UP, DOWN, HALF_UP, HALF_DOWN, CORE = range(5)


def split(value):
    high = value.astype(BF)
    return high, (value - high.astype(F32)).astype(BF)


def three(a_high, a_low, b_high, b_low):
    def dot(a, b):
        return jnp.dot(a, b, preferred_element_type=F32)

    return dot(a_high, b_high) + (dot(a_high, b_low) + dot(a_low, b_high))


def kernel(
    inv_ref, k_ref, f_ref, n_ref, d_ref,
    k_all, k_high, k_low, sent_0, sent_1, picked, p_x, p_high, p_low, p_z, pz_high, pz_low,
    n_part, n_far, n_got, n_all, t_high, t_low, d_part, d_core, d_far, d_got, d_sum,
    one_send, one_recv, two_send, two_recv, three_send, three_recv, local_sem, k_send, k_recv,
    z_send, z_recv, x_send, x_recv, n_send, n_recv, y_send, y_recv,
    c_send, c_recv, d_send, d_recv, out_sem, o_send, o_recv,
):
    row, col = lax.axis_index("row"), lax.axis_index("col")
    x, y_lo = row % 4, row // 4
    core, z, y_hi = col % 2, (col // 2) % 4, col // 8
    y, place = y_hi * 2 + y_lo, col % 8

    def at(y_hi_, z_, core_, y_lo_, x_):
        return (y_lo_ * 4 + x_, y_hi_ * 8 + z_ * 2 + core_)

    def on_x(k):
        return (y_lo * 4 + (x + k) % 4, col)

    def on_y(k):
        there = (y + k) % 4
        return at(there // 2, z, core, there % 2, x)

    def on_z(k):
        return (row, y_hi * 8 + ((z + k) % 4) * 2 + core)

    other_core = (row, y_hi * 8 + z * 2 + 1 - core)
    stays = jnp.logical_and(y_hi == y_lo, y_hi == core)

    def remote(src, dst, send, recv, device):
        return pltpu.make_async_remote_copy(
            src_ref=src, dst_ref=dst, send_sem=send, recv_sem=recv, device_id=device, device_id_type=MESH
        )

    barrier = pltpu.get_barrier_semaphore()

    def greet(device):
        pl.semaphore_signal(barrier, inc=1, device_id=device, device_id_type=MESH)

    @pl.loop(1, 16)
    def _(k):
        greet((row, (col + k) % 16))

    for k in (1, 2, 3):
        greet(on_x(k))
    for k in (1, 3):
        greet(on_y(k))

    @pl.when(jnp.logical_not(stays))
    def _():
        greet(at(core, z, y_lo, y_hi, x))

    pl.semaphore_wait(barrier, 21 - stays.astype(jnp.int32))

    sent = (sent_0, sent_1)

    def piece(to, e):
        return f_ref.at[:, to % 8, :, pl.ds(pl.multiple_of((to // 8) * 256 + e * 128, 128), 128)]

    def first(e, k):
        to = (col + k) % 16
        return remote(piece(to, e), sent[e].at[pl.ds(col * 7, 7)], one_send.at[e, k], one_recv.at[e, k], (row, to))

    def first_here(e):
        return pltpu.make_async_copy(piece(col, e), sent[e].at[pl.ds(col * 7, 7)], local_sem.at[e])

    for e in range(2):

        @pl.loop(1, 16)
        def _(k):
            first(e, k).start()

        first_here(e).start()

    def k_copy(kind, half):
        rows = pl.ds(half * 224, 224)
        return remote(
            k_ref.at[rows], k_all.at[y, rows], k_send.at[kind, half], k_recv.at[kind, half], on_y(1 if kind == UP else 3)
        )

    def k_pass(kind):
        rows = pl.ds(0, 224) if kind == HALF_UP else pl.ds(224, 224)
        ref = k_all.at[(y + (3 if kind == HALF_UP else 1)) % 4, rows]
        return remote(ref, ref, k_send.at[kind, 0], k_recv.at[kind, 0], on_y(1 if kind == HALF_UP else 3))

    k_copy(UP, 0).start()
    k_copy(DOWN, 1).start()

    def take_k(there, ref):
        k_high[there], k_low[there] = split(ref[...])

    k_here = pltpu.make_async_copy(k_ref, k_all.at[y], local_sem.at[6])
    k_here.start()
    k_here.wait()
    take_k(y, k_all.at[y])

    def second(e, k):
        to = (x + 4 - k) % 4
        i = (k + 3) % 4
        src = picked.at[e, :, pl.ds(to * 14, 14)]
        dst = p_x.at[e, i // 2, i % 2, :, :, z, core]
        if k == 0:
            return pltpu.make_async_copy(src, dst, local_sem.at[2 + e])
        return remote(src, dst, two_send.at[e, k], two_recv.at[e, k], on_x(4 - k))

    def third(e, k):
        to = (place + k) % 8
        src = picked.at[e, :, pl.ds(to * 7, 7)]
        dst = p_z.at[e, x, :, :, place]
        return remote(src, dst, three_send.at[e, k], three_recv.at[e, k], (row, y_hi * 8 + to))

    def third_here(e):
        src = picked.at[e, :, pl.ds(place * 7, 7)]
        return pltpu.make_async_copy(src, p_z.at[e, x, :, :, place], local_sem.at[4 + e])

    for e in range(2):
        first_here(e).wait()

        @pl.loop(1, 16)
        def _(k):
            first(e, k).wait_recv()

        for j in range(28):
            picked[e, j // 14, (j % 14) * 4 : (j % 14) * 4 + 4] = sent[e][pl.ds(inv_ref[j] * 4, 4)]
        for k in (1, 2, 3, 0):
            second(e, k).start()

        @pl.loop(1, 8)
        def _(k):
            third(e, k).start()

        third_here(e).start()
        if e == 0:
            k_copy(UP, 1).start()
            k_copy(DOWN, 0).start()

    def z_copy(kind, r):
        def rows(there, chunk=slice(None)):
            return p_x.at[r // 2, r % 2, :, chunk, :, there, core]

        if kind == CORE:
            ref, to = p_x.at[r // 2, r % 2, :, :, :, :, core], other_core
        else:
            ref, to = {
                UP: (rows(z), on_z(1)),
                DOWN: (rows(z), on_z(3)),
                HALF_UP: (rows((z + 3) % 4, 0), on_z(1)),
                HALF_DOWN: (rows((z + 1) % 4, 1), on_z(3)),
            }[kind]
        return remote(ref, ref, z_send.at[kind, r], z_recv.at[kind, r], to)

    def x_copy(kind, e):
        def block(there, half=slice(None)):
            return p_z.at[e, there, half]

        ref, to = {
            UP: (block(x), on_x(1)),
            DOWN: (block(x), on_x(3)),
            HALF_UP: (block((x + 3) % 4, 0), on_x(1)),
            HALF_DOWN: (block((x + 1) % 4, 1), on_x(3)),
        }[kind]
        return remote(ref, ref, x_send.at[kind, e], x_recv.at[kind, e], to)

    def pass_on(copy, r):
        copy(UP, r).wait_recv()
        copy(HALF_UP, r).start()
        copy(DOWN, r).wait_recv()
        copy(HALF_DOWN, r).start()

    def z_start(e):
        for p in range(2):
            z_copy(UP, 2 * e + p).start()
            z_copy(DOWN, 2 * e + p).start()

    def x_start(e):
        x_copy(UP, e).start()
        x_copy(DOWN, e).start()

    def third_done(e):
        third_here(e).wait()

        @pl.loop(1, 8)
        def _(k):
            third(e, k).wait_recv()

    for e in range(2):
        second(e, 0).wait()
        for k in (1, 2, 3):
            second(e, k).wait_recv()
        if e == 0:
            z_start(0)
        third_done(e)
        if e == 0:
            x_start(0)

    def core_start(r):
        z_copy(HALF_UP, r).wait_recv()
        z_copy(HALF_DOWN, r).wait_recv()
        z_copy(CORE, r).start()

    pass_on(z_copy, 0)
    pass_on(z_copy, 1)
    z_start(1)
    x_start(1)
    pass_on(x_copy, 0)
    core_start(0)
    core_start(1)
    pass_on(z_copy, 2)

    def n_copy(kind, e, side):
        src, dst = {
            HALF_UP: (n_part.at[e, 1, side, pl.ds(0, 224)], n_far.at[0, e, side]),
            HALF_DOWN: (n_part.at[e, 1, side, pl.ds(224, 224)], n_far.at[1, e, side]),
            UP: (n_part.at[e, 0, side], n_got.at[0, e, side]),
            DOWN: (n_part.at[e, 2, side], n_got.at[1, e, side]),
        }[kind]
        to = on_x(1 if kind in (UP, HALF_UP) else 3)
        return remote(src, dst, n_send.at[kind, e, side], n_recv.at[kind, e, side], to)

    def n_far_start(e, side):
        n_copy(HALF_UP, e, side).start()
        n_copy(HALF_DOWN, e, side).start()

    def n_near_start(e, side):
        n_copy(HALF_UP, e, side).wait_recv()
        n_part[e, 0, side, 0:224] += n_far[0, e, side]
        n_copy(UP, e, side).start()
        n_copy(HALF_DOWN, e, side).wait_recv()
        n_part[e, 2, side, 224:448] += n_far[1, e, side]
        n_copy(DOWN, e, side).start()

    def take_p(r):
        for half in range(2):

            @pl.loop(0, 7)
            def _(k):
                rows = pl.ds(pl.multiple_of(k * 128, 128), 128)
                for i in range(2):
                    columns = slice(i * 128, (i + 1) * 128)
                    p_high[r, half, rows, columns], p_low[r, half, rows, columns] = split(
                        p_x[r // 2, r % 2, i, half, pl.ds(2 * k, 2)].reshape(128, 128)
                    )

    def n_dots(r, side, half, add):
        there = side * 2 + half
        value = three(k_high[there], k_low[there], p_high[r, half], p_low[r, half])
        for i in range(2):
            columns = value[:, i * 128 : (i + 1) * 128]
            n_part[r // 2, 2 * (r % 2) + i, side] = columns + n_part[r // 2, 2 * (r % 2) + i, side] if add else columns

    def n_first(r):
        z_copy(CORE, r).wait_recv()
        take_p(r)
        n_dots(r, y_hi, y_lo, False)

    theirs = 1 - y_hi

    @pl.loop(0, 2)
    def _(r):
        n_first(r)

    pass_on(z_copy, 3)
    for half in range(2):
        k_copy(UP, half).wait_recv()
    k_pass(HALF_UP).start()
    for half in range(2):
        k_copy(DOWN, half).wait_recv()
    k_pass(HALF_DOWN).start()
    take_k((y + 3) % 4, k_all.at[(y + 3) % 4])
    take_k((y + 1) % 4, k_all.at[(y + 1) % 4])
    core_start(2)
    pass_on(x_copy, 1)

    @pl.loop(0, 4)
    def _(r):
        @pl.when(r >= 2)
        def _():
            n_first(r)

        n_dots(r, y_hi, 1 - y_lo, True)

        @pl.when(r % 2 == 0)
        def _():
            n_far_start(r // 2, y_hi)

        @pl.when(r == 0)
        def _():
            core_start(3)

        n_dots(r, theirs, 1 - y_lo, False)

        @pl.when(r % 2 == 1)
        def _():
            n_near_start(r // 2, y_hi)

    def y_copy(kind, e, s):
        there = (y + {UP: 0, DOWN: 0, HALF_UP: 3, HALF_DOWN: 1}[kind]) % 4
        start = ((there // 2 + s) % 2) * 448 + (224 if kind == HALF_DOWN else 0)
        size = 448 if kind in (UP, DOWN) else 224
        ref = n_all.at[e, there, pl.ds(pl.multiple_of(start, 32), size)]
        to = on_y(1 if kind in (UP, HALF_UP) else 3)
        return remote(ref, ref, y_send.at[kind, e, s], y_recv.at[kind, e, s], to)

    def y_start(e, s):
        side = (y_hi + s) % 2
        n_copy(UP, e, side).wait_recv()
        n_copy(DOWN, e, side).wait_recv()
        rows = pl.ds(pl.multiple_of(side * 448, 64), 448)
        n_all[e, y, rows] = n_part[e, 3, side] + (n_got[0, e, side] + n_got[1, e, side])
        y_copy(UP, e, s).start()
        y_copy(DOWN, e, s).start()

    def y_pass(e, s):
        y_copy(UP, e, s).wait_recv()
        y_copy(HALF_UP, e, s).start()
        y_copy(DOWN, e, s).wait_recv()
        y_copy(HALF_DOWN, e, s).start()

    y_start(0, 0)
    k_pass(HALF_UP).wait_recv()
    k_pass(HALF_DOWN).wait_recv()
    take_k((y + 2) % 4, k_all.at[(y + 2) % 4])

    @pl.loop(0, 4)
    def _(t):
        n_dots((t % 2) * 2 + t // 2, theirs, y_lo, True)

        @pl.when(t < 2)
        def _():
            n_far_start(t, theirs)

        @pl.when(t >= 2)
        def _():
            n_near_start(t - 2, theirs)

    y_start(1, 0)
    y_pass(0, 0)

    def take_z(e):
        x_copy(HALF_UP, e).wait_recv()
        x_copy(HALF_DOWN, e).wait_recv()

        @pl.loop(0, 4)
        def _(there):
            for half in range(2):
                rows, columns = slice(half * 448, (half + 1) * 448), slice(e * 128, (e + 1) * 128)
                pz_high[there, rows, columns], pz_low[there, rows, columns] = split(p_z[e, there, half].reshape(448, 128))

    take_z(0)
    take_z(1)
    y_start(0, 1)
    y_pass(1, 0)
    y_start(1, 1)
    y_pass(0, 1)
    y_pass(1, 1)

    def c_copy(e, k):
        there = (z + k) % 4
        return remote(d_part.at[e, 1 - core, there], d_core.at[e, there], c_send.at[e, k], c_recv.at[e, k], other_core)

    def d_copy(kind, e):
        src, dst = {
            HALF_UP: (d_part.at[e, core, (z + 2) % 4, pl.ds(0, 128)], d_far.at[0, e]),
            HALF_DOWN: (d_part.at[e, core, (z + 2) % 4, pl.ds(128, 128)], d_far.at[1, e]),
            UP: (d_part.at[e, core, (z + 1) % 4], d_got.at[0, e]),
            DOWN: (d_part.at[e, core, (z + 3) % 4], d_got.at[1, e]),
        }[kind]
        return remote(src, dst, d_send.at[kind, e], d_recv.at[kind, e], on_z(1 if kind in (UP, HALF_UP) else 3))

    def d_cores(e, k):
        there = (z + k) % 4
        c_copy(e, k).wait_recv()
        d_part[e, core, there] += d_core[e, there]

    def d_far_start(e):
        d_cores(e, 2)
        d_copy(HALF_UP, e).start()
        d_copy(HALF_DOWN, e).start()

    def d_near_start(e):
        d_copy(HALF_UP, e).wait_recv()
        d_part[e, core, (z + 1) % 4, 0:128] += d_far[0, e]
        d_copy(UP, e).start()
        d_copy(HALF_DOWN, e).wait_recv()
        d_part[e, core, (z + 3) % 4, 128:256] += d_far[1, e]
        d_copy(DOWN, e).start()

    def n_out(e, half):
        src = n_all.at[e, half * 2 + y_lo, pl.ds(pl.multiple_of(y_hi * 448, 64), 448)]
        columns = pl.ds(pl.multiple_of(half * 256 + e * 128, 128), 128)
        return pltpu.make_async_copy(src, n_ref.at[:, columns], out_sem.at[e, half])

    @pl.loop(0, 2)
    def _(e):
        for kind in (HALF_UP, HALF_DOWN):
            for s in range(2):
                y_copy(kind, e, s).wait_recv()
        for half in range(2):
            n_out(e, half).start()
        for low in range(2):
            for high in range(2):
                for k in range(7):
                    rows = slice(k * 128, (k + 1) * 128)
                    lines = slice(high * 128, (high + 1) * 128)
                    t_high[low, lines, rows], t_low[low, lines, rows] = split(n_all[e, 2 * high + low, rows].T)

        @pl.loop(0, 4)
        def _(j):
            k = (j + 2) % 4
            there = (z + k) % 4

            @pl.loop(0, 2)
            def _(turn):
                low = (core + 1 + turn) % 2
                d_part[e, low, there] = three(t_high[low], t_low[low], pz_high[there], pz_low[there])

                @pl.when(turn == 0)
                def _():
                    c_copy(e, k).start()

            @pl.when(j == 1)
            def _():
                d_far_start(e)

            @pl.when(jnp.logical_and(j == 0, e == 1))
            def _():
                d_near_start(0)

        d_cores(e, 3)
        d_cores(e, 1)
        d_cores(e, 0)

    d_near_start(1)

    def o_copy(e):
        return remote(d_sum.at[e], d_ref.at[:, e], o_send.at[e], o_recv.at[e], at(y_lo, z, y_hi, core, x))

    def o_here(e):
        return pltpu.make_async_copy(d_sum.at[e], d_ref.at[:, e], o_recv.at[e])

    for e in range(2):
        d_copy(UP, e).wait_recv()
        d_copy(DOWN, e).wait_recv()
        d_sum[e] = (d_part[e, core, z] + (d_got[0, e] + d_got[1, e])).reshape(2, 128, 256)

        @pl.when(stays)
        def _():
            o_here(e).start()

        @pl.when(jnp.logical_not(stays))
        def _():
            o_copy(e).start()

    for e in range(2):

        @pl.loop(1, 16)
        def _(k):
            first(e, k).wait_send()

        @pl.loop(1, 8)
        def _(k):
            third(e, k).wait_send()

        for k in (1, 2, 3):
            second(e, k).wait_send()
        for kind in range(4):
            x_copy(kind, e).wait_send()
            c_copy(e, kind).wait_send()
            d_copy(kind, e).wait_send()
            for side in range(2):
                n_copy(kind, e, side).wait_send()
                y_copy(kind, e, side).wait_send()

        @pl.when(jnp.logical_not(stays))
        def _():
            o_copy(e).wait_send()

    for half in range(2):
        k_copy(UP, half).wait_send()
        k_copy(DOWN, half).wait_send()
    k_pass(HALF_UP).wait_send()
    k_pass(HALF_DOWN).wait_send()

    @pl.loop(0, 4)
    def _(r):
        for kind in range(5):
            z_copy(kind, r).wait_send()

    for e in range(2):
        for half in range(2):
            n_out(e, half).wait()
        o_here(e).wait()


def on_device(known_inverse, factor_panel, diag_base, ancestor_map):
    blocks = jnp.arange(28, dtype=jnp.int32)
    inverse = jnp.sum(jnp.where(ancestor_map[None, :] == blocks[:, None], blocks[None, :], 0), axis=1)
    whole = pl.BlockSpec(memory_space=pl.ANY)
    dma = pltpu.SemaphoreType.DMA
    product, reduced = pl.pallas_call(
        kernel,
        out_shape=(jax.ShapeDtypeStruct((448, 512), F32), jax.ShapeDtypeStruct((2, 2, 128, 256), F32)),
        in_specs=[pl.BlockSpec(memory_space=pltpu.SMEM), whole, whole],
        out_specs=(whole, whole),
        scratch_shapes=[
            pltpu.VMEM((4, 448, 896), F32),
            pltpu.VMEM((4, 448, 896), BF),
            pltpu.VMEM((4, 448, 896), BF),
            pltpu.VMEM((112, 8, 128), F32),
            pltpu.VMEM((112, 8, 128), F32),
            pltpu.VMEM((2, 2, 56, 8, 128), F32),
            pltpu.VMEM((2, 2, 2, 2, 14, 4, 2, 8, 128), F32),
            pltpu.VMEM((4, 2, 896, 256), BF),
            pltpu.VMEM((4, 2, 896, 256), BF),
            pltpu.VMEM((2, 4, 2, 7, 8, 8, 128), F32),
            pltpu.VMEM((4, 896, 256), BF),
            pltpu.VMEM((4, 896, 256), BF),
            pltpu.VMEM((2, 4, 2, 448, 128), F32),
            pltpu.VMEM((2, 2, 2, 224, 128), F32),
            pltpu.VMEM((2, 2, 2, 448, 128), F32),
            pltpu.VMEM((2, 4, 896, 128), F32),
            pltpu.VMEM((2, 256, 896), BF),
            pltpu.VMEM((2, 256, 896), BF),
            pltpu.VMEM((2, 2, 4, 256, 256), F32),
            pltpu.VMEM((2, 4, 256, 256), F32),
            pltpu.VMEM((2, 2, 128, 256), F32),
            pltpu.VMEM((2, 2, 256, 256), F32),
            pltpu.VMEM((2, 2, 128, 256), F32),
            dma((2, 16)), dma((2, 16)), dma((2, 4)), dma((2, 4)), dma((2, 8)), dma((2, 8)), dma((7,)), dma((4, 2)), dma((4, 2)),
            dma((5, 4)), dma((5, 4)), dma((4, 2)), dma((4, 2)), dma((4, 2, 2)), dma((4, 2, 2)), dma((4, 2, 2)), dma((4, 2, 2)),
            dma((2, 4)), dma((2, 4)), dma((4, 2)), dma((4, 2)), dma((2, 2)), dma((2,)), dma((2,)),
        ],
        compiler_params=pltpu.CompilerParams(collective_id=0, has_side_effects=True, vmem_limit_bytes=60 << 20),
        cost_estimate=pl.CostEstimate(
            flops=6 * (448 * 1792 * 2048 + 256 * 1792 * 2048), bytes_accessed=4 << 20, transcendentals=0
        ),
        name="selected_inverse",
    )(inverse, known_inverse, factor_panel.reshape(7, 8, 8, 512))
    return (-product, diag_base + reduced.reshape(512, 256))


def solution(mesh):
    placed = (P("col", "row"), P("col", "row"), P("row", "col"), P())
    return jax.shard_map(
        on_device,
        mesh=mesh,
        in_specs=placed,
        out_specs=(P("col", "row"), P("row", "col")),
        check_vma=False,
    )
```

```python
import jax
import jax.numpy as jnp
from jax import lax
from jax.experimental import pallas as pl
from jax.experimental.pallas import tpu as pltpu
from jax.sharding import PartitionSpec as P

MESH = pl.DeviceIdType.MESH
BF = jnp.bfloat16
F32 = jnp.float32

UP, DOWN, HALF_UP, HALF_DOWN, CORE = range(5)
FREE_UP, FREE_DOWN = 4, 5


def split(value):
    high = value.astype(BF)
    return high, (value - high.astype(F32)).astype(BF)


def three(a_high, a_low, b_high, b_low):
    def dot(a, b):
        return jnp.dot(a, b, preferred_element_type=F32)

    return dot(a_high, b_high) + (dot(a_high, b_low) + dot(a_low, b_high))


def kernel(
    inv_ref, k_ref, f_ref, n_ref, d_ref,
    k_all, k_high, k_low, sent_0, sent_1, picked, p_x, p_high, p_low, p_z, pz_high, pz_low,
    n_part, n_far, n_got, n_all, t_high, t_low, d_part, d_core, d_far, d_got, d_sum,
    one_send, one_recv, two_send, two_recv, three_send, three_recv, local_sem, k_send, k_recv,
    z_send, z_recv, x_send, x_recv, n_send, n_recv, y_send, y_recv,
    c_send, c_recv, d_send, d_recv, out_sem, o_send, o_recv,
):
    row, col = lax.axis_index("row"), lax.axis_index("col")
    x, y_lo = row % 4, row // 4
    core, z, y_hi = col % 2, (col // 2) % 4, col // 8
    y, place = y_hi * 2 + y_lo, col % 8

    def at(y_hi_, z_, core_, y_lo_, x_):
        return (y_lo_ * 4 + x_, y_hi_ * 8 + z_ * 2 + core_)

    def on_x(k):
        return (y_lo * 4 + (x + k) % 4, col)

    def on_y(k):
        there = (y + k) % 4
        return at(there // 2, z, core, there % 2, x)

    def on_z(k):
        return (row, y_hi * 8 + ((z + k) % 4) * 2 + core)

    other_core = (row, y_hi * 8 + z * 2 + 1 - core)
    stays = jnp.logical_and(y_hi == y_lo, y_hi == core)

    def remote(src, dst, send, recv, device):
        return pltpu.make_async_remote_copy(
            src_ref=src, dst_ref=dst, send_sem=send, recv_sem=recv, device_id=device, device_id_type=MESH
        )

    barrier = pltpu.get_barrier_semaphore()

    def greet(device):
        pl.semaphore_signal(barrier, inc=1, device_id=device, device_id_type=MESH)

    @pl.loop(1, 16)
    def _(k):
        greet((row, (col + k) % 16))

    for k in (1, 2, 3):
        greet(on_x(k))
    for k in (1, 3):
        greet(on_y(k))

    @pl.when(jnp.logical_not(stays))
    def _():
        greet(at(core, z, y_lo, y_hi, x))

    pl.semaphore_wait(barrier, 21 - stays.astype(jnp.int32))

    sent = (sent_0, sent_1)

    def piece(to, e):
        return f_ref.at[:, to % 8, :, pl.ds(pl.multiple_of((to // 8) * 256 + e * 128, 128), 128)]

    def first(e, k):
        to = (col + k) % 16
        return remote(piece(to, e), sent[e].at[pl.ds(col * 7, 7)], one_send.at[e, k], one_recv.at[e, k], (row, to))

    def first_here(e):
        return pltpu.make_async_copy(piece(col, e), sent[e].at[pl.ds(col * 7, 7)], local_sem.at[e])

    for e in range(2):

        @pl.loop(1, 16)
        def _(k):
            first(e, k).start()

        first_here(e).start()

    def k_copy(kind, half):
        rows = pl.ds(half * 224, 224)
        return remote(
            k_ref.at[rows], k_all.at[y, rows], k_send.at[kind, half], k_recv.at[kind, half], on_y(1 if kind == UP else 3)
        )

    def k_pass(kind):
        rows = pl.ds(0, 224) if kind == HALF_UP else pl.ds(224, 224)
        ref = k_all.at[(y + (3 if kind == HALF_UP else 1)) % 4, rows]
        return remote(ref, ref, k_send.at[kind, 0], k_recv.at[kind, 0], on_y(1 if kind == HALF_UP else 3))

    k_copy(UP, 0).start()
    k_copy(DOWN, 1).start()

    def take_k(there, ref):
        k_high[there], k_low[there] = split(ref[...])

    k_here = pltpu.make_async_copy(k_ref, k_all.at[y], local_sem.at[6])
    k_here.start()
    k_here.wait()
    take_k(y, k_all.at[y])

    def second(e, k):
        to = (x + 4 - k) % 4
        i = (k + 3) % 4
        src = picked.at[e, :, pl.ds(to * 14, 14)]
        dst = p_x.at[e, i // 2, i % 2, :, :, z, core]
        if k == 0:
            return pltpu.make_async_copy(src, dst, local_sem.at[2 + e])
        return remote(src, dst, two_send.at[e, k], two_recv.at[e, k], on_x(4 - k))

    def third(e, k):
        to = (place + k) % 8
        src = picked.at[e, :, pl.ds(to * 7, 7)]
        dst = p_z.at[e, x, :, :, place]
        return remote(src, dst, three_send.at[e, k], three_recv.at[e, k], (row, y_hi * 8 + to))

    def third_here(e):
        src = picked.at[e, :, pl.ds(place * 7, 7)]
        return pltpu.make_async_copy(src, p_z.at[e, x, :, :, place], local_sem.at[4 + e])

    def third_start(e):
        @pl.loop(1, 8)
        def _(k):
            third(e, k).start()

        third_here(e).start()

    for e in range(2):
        first_here(e).wait()

        @pl.loop(1, 16)
        def _(k):
            first(e, k).wait_recv()

        for j in range(28):
            picked[e, j // 14, (j % 14) * 4 : (j % 14) * 4 + 4] = sent[e][pl.ds(inv_ref[j] * 4, 4)]
        for k in (1, 2, 3, 0):
            second(e, k).start()
        if e == 0:
            third_start(0)
            k_copy(UP, 1).start()
            k_copy(DOWN, 0).start()

    def z_copy(kind, r):
        def rows(there, chunk=slice(None)):
            return p_x.at[r // 2, r % 2, :, chunk, :, there, core]

        if kind == CORE:
            ref, to = p_x.at[r // 2, r % 2, :, :, :, :, core], other_core
        else:
            ref, to = {
                UP: (rows(z), on_z(1)),
                DOWN: (rows(z), on_z(3)),
                HALF_UP: (rows((z + 3) % 4, 0), on_z(1)),
                HALF_DOWN: (rows((z + 1) % 4, 1), on_z(3)),
            }[kind]
        return remote(ref, ref, z_send.at[kind, r], z_recv.at[kind, r], to)

    def x_copy(kind, e):
        def block(there, half=slice(None)):
            return p_z.at[e, there, half]

        ref, to = {
            UP: (block(x), on_x(1)),
            DOWN: (block(x), on_x(3)),
            HALF_UP: (block((x + 3) % 4, 0), on_x(1)),
            HALF_DOWN: (block((x + 1) % 4, 1), on_x(3)),
        }[kind]
        return remote(ref, ref, x_send.at[kind, e], x_recv.at[kind, e], to)

    def pass_on(copy, r):
        copy(UP, r).wait_recv()
        copy(HALF_UP, r).start()
        copy(DOWN, r).wait_recv()
        copy(HALF_DOWN, r).start()

    def z_start(e):
        for p in range(2):
            z_copy(UP, 2 * e + p).start()
            z_copy(DOWN, 2 * e + p).start()

    def x_start(e):
        x_copy(UP, e).start()
        x_copy(DOWN, e).start()

    def third_done(e):
        third_here(e).wait()

        @pl.loop(1, 8)
        def _(k):
            third(e, k).wait_recv()

    def second_done(e):
        second(e, 0).wait()
        for k in (1, 2, 3):
            second(e, k).wait_recv()

    second_done(0)
    z_start(0)
    third_start(1)
    third_done(0)
    x_start(0)
    second_done(1)
    pass_on(z_copy, 0)
    pass_on(z_copy, 1)
    z_start(1)
    third_done(1)
    x_start(1)

    def core_start(r):
        z_copy(HALF_UP, r).wait_recv()
        z_copy(HALF_DOWN, r).wait_recv()
        z_copy(CORE, r).start()

    pass_on(x_copy, 0)
    core_start(0)
    core_start(1)

    def n_copy(kind, e, side):
        low, high = pl.ds(0, 224), pl.ds(224, 224)
        src, dst = {
            HALF_UP: (n_part.at[e, 1, side, low], n_far.at[0, e, side]),
            HALF_DOWN: (n_part.at[e, 1, side, high], n_far.at[1, e, side]),
            UP: (n_part.at[e, 0, side, low], n_got.at[0, e, side, low]),
            DOWN: (n_part.at[e, 2, side, high], n_got.at[1, e, side, high]),
            FREE_UP: (n_part.at[e, 0, side, high], n_got.at[0, e, side, high]),
            FREE_DOWN: (n_part.at[e, 2, side, low], n_got.at[1, e, side, low]),
        }[kind]
        to = on_x(1 if kind in (UP, HALF_UP, FREE_UP) else 3)
        return remote(src, dst, n_send.at[kind, e, side], n_recv.at[kind, e, side], to)

    def n_far_start(e, side):
        n_copy(HALF_UP, e, side).start()
        n_copy(HALF_DOWN, e, side).start()

    def n_free_start(e, side):
        n_copy(FREE_UP, e, side).start()
        n_copy(FREE_DOWN, e, side).start()

    def n_near_start(e, side):
        n_copy(HALF_UP, e, side).wait_recv()
        n_part[e, 0, side, 0:224] += n_far[0, e, side]
        n_copy(UP, e, side).start()
        n_copy(HALF_DOWN, e, side).wait_recv()
        n_part[e, 2, side, 224:448] += n_far[1, e, side]
        n_copy(DOWN, e, side).start()

    def take_p(r):
        for half in range(2):

            @pl.loop(0, 7)
            def _(k):
                rows = pl.ds(pl.multiple_of(k * 128, 128), 128)
                for i in range(2):
                    columns = slice(i * 128, (i + 1) * 128)
                    p_high[r, half, rows, columns], p_low[r, half, rows, columns] = split(
                        p_x[r // 2, r % 2, i, half, pl.ds(2 * k, 2)].reshape(128, 128)
                    )

    def n_dots(r, side, half, add):
        there = side * 2 + half
        value = three(k_high[there], k_low[there], p_high[r, half], p_low[r, half])

        @pl.when(add)
        def _():
            for i in range(2):
                n_part[r // 2, 2 * (r % 2) + i, side] += value[:, i * 128 : (i + 1) * 128]

        @pl.when(jnp.logical_not(add))
        def _():
            for i in range(2):
                n_part[r // 2, 2 * (r % 2) + i, side] = value[:, i * 128 : (i + 1) * 128]

    def n_first(r):
        z_copy(CORE, r).wait_recv()
        take_p(r)

    theirs = 1 - y_hi

    @pl.loop(0, 2)
    def _(r):
        n_first(r)
        n_dots(r, y_hi, y_lo, r < 0)

    pass_on(z_copy, 2)
    for half in range(2):
        k_copy(UP, half).wait_recv()
    k_pass(HALF_UP).start()
    for half in range(2):
        k_copy(DOWN, half).wait_recv()
    k_pass(HALF_DOWN).start()
    pass_on(x_copy, 1)
    pass_on(z_copy, 3)
    take_k((y + 3) % 4, k_all.at[(y + 3) % 4])
    take_k((y + 1) % 4, k_all.at[(y + 1) % 4])
    core_start(2)

    def y_copy(kind, e, s):
        there = (y + {UP: 0, DOWN: 0, HALF_UP: 3, HALF_DOWN: 1}[kind]) % 4
        start = ((there // 2 + s) % 2) * 448 + (224 if kind == HALF_DOWN else 0)
        size = 448 if kind in (UP, DOWN) else 224
        ref = n_all.at[e, there, pl.ds(pl.multiple_of(start, 32), size)]
        to = on_y(1 if kind in (UP, HALF_UP) else 3)
        return remote(ref, ref, y_send.at[kind, e, s], y_recv.at[kind, e, s], to)

    def y_start(e, s):
        side = (y_hi + s) % 2
        for kind in (UP, DOWN, FREE_UP, FREE_DOWN):
            n_copy(kind, e, side).wait_recv()
        rows = pl.ds(pl.multiple_of(side * 448, 64), 448)
        n_all[e, y, rows] = n_part[e, 3, side] + (n_got[0, e, side] + n_got[1, e, side])
        y_copy(UP, e, s).start()
        y_copy(DOWN, e, s).start()

    def y_pass(e, s):
        y_copy(UP, e, s).wait_recv()
        y_copy(HALF_UP, e, s).start()
        y_copy(DOWN, e, s).wait_recv()
        y_copy(HALF_DOWN, e, s).start()

    @pl.loop(0, 10)
    def _(q):
        def after(step, action, *args):
            @pl.when(q == step)
            def _():
                action(*args)

        after(2, n_first, 2)
        after(4, n_first, 3)
        own_block = jnp.logical_or(q == 2, q == 4)
        add = jnp.logical_or(q < 2, jnp.logical_or(q == 3, q == 5))
        r = jnp.where(q < 2, q, jnp.where(q < 6, q // 2 + 1, q - 6))
        n_dots(r, jnp.where(q < 6, y_hi, theirs), jnp.where(own_block, y_lo, 1 - y_lo), add)
        after(0, n_far_start, 0, y_hi)
        after(1, n_free_start, 0, y_hi)
        after(1, core_start, 3)
        after(3, n_far_start, 1, y_hi)
        after(3, n_near_start, 0, y_hi)
        after(5, n_free_start, 1, y_hi)
        after(6, n_near_start, 1, y_hi)
        after(8, y_start, 0, 0)

    k_pass(HALF_UP).wait_recv()
    k_pass(HALF_DOWN).wait_recv()
    take_k((y + 2) % 4, k_all.at[(y + 2) % 4])

    @pl.loop(0, 4)
    def _(t):
        n_dots(t, theirs, y_lo, t >= 0)

        @pl.when(t == 0)
        def _():
            n_far_start(0, theirs)

        @pl.when(t == 1)
        def _():
            n_free_start(0, theirs)
            y_start(1, 0)

        @pl.when(t == 2)
        def _():
            n_near_start(0, theirs)
            n_far_start(1, theirs)

        @pl.when(t == 3)
        def _():
            n_free_start(1, theirs)

    y_pass(0, 0)

    def take_z(e):
        x_copy(HALF_UP, e).wait_recv()
        x_copy(HALF_DOWN, e).wait_recv()

        @pl.loop(0, 4)
        def _(there):
            for half in range(2):
                rows, columns = slice(half * 448, (half + 1) * 448), slice(e * 128, (e + 1) * 128)
                pz_high[there, rows, columns], pz_low[there, rows, columns] = split(p_z[e, there, half].reshape(448, 128))

    take_z(0)
    take_z(1)
    y_start(0, 1)
    n_near_start(1, theirs)
    y_pass(1, 0)
    y_start(1, 1)
    y_pass(0, 1)
    y_pass(1, 1)

    def c_copy(e, k):
        there = (z + k) % 4
        return remote(d_part.at[e, there, 1 - core], d_core.at[e, there], c_send.at[e, k], c_recv.at[e, k], other_core)

    def d_copy(kind, e):
        low, high = pl.ds(0, 128), pl.ds(128, 128)
        src, dst = {
            HALF_UP: (d_part.at[e, (z + 2) % 4, core, low], d_far.at[0, e]),
            HALF_DOWN: (d_part.at[e, (z + 2) % 4, core, high], d_far.at[1, e]),
            UP: (d_part.at[e, (z + 1) % 4, core, low], d_got.at[0, e, low]),
            DOWN: (d_part.at[e, (z + 3) % 4, core, high], d_got.at[1, e, high]),
            FREE_UP: (d_part.at[e, (z + 1) % 4, core, high], d_got.at[0, e, high]),
            FREE_DOWN: (d_part.at[e, (z + 3) % 4, core, low], d_got.at[1, e, low]),
        }[kind]
        to = on_z(1 if kind in (UP, HALF_UP, FREE_UP) else 3)
        return remote(src, dst, d_send.at[kind, e], d_recv.at[kind, e], to)

    def d_cores(e, k):
        there = (z + k) % 4
        c_copy(e, k).wait_recv()
        d_part[e, there, core] += d_core[e, there]

    def d_far_start(e):
        d_cores(e, 2)
        d_copy(HALF_UP, e).start()
        d_copy(HALF_DOWN, e).start()

    def d_near_start(e):
        d_copy(HALF_UP, e).wait_recv()
        d_part[e, (z + 1) % 4, core, 0:128] += d_far[0, e]
        d_copy(UP, e).start()
        d_copy(HALF_DOWN, e).wait_recv()
        d_part[e, (z + 3) % 4, core, 128:256] += d_far[1, e]
        d_copy(DOWN, e).start()

    def n_out(e, half):
        src = n_all.at[e, half * 2 + y_lo, pl.ds(pl.multiple_of(y_hi * 448, 64), 448)]
        columns = pl.ds(pl.multiple_of(half * 256 + e * 128, 128), 128)
        return pltpu.make_async_copy(src, n_ref.at[:, columns], out_sem.at[e, half])

    @pl.loop(0, 2)
    def _(e):
        for kind in (HALF_UP, HALF_DOWN):
            for s in range(2):
                y_copy(kind, e, s).wait_recv()
        for half in range(2):
            n_out(e, half).start()
        for low in range(2):
            for high in range(2):
                for k in range(7):
                    rows = slice(k * 128, (k + 1) * 128)
                    lines = slice((low * 2 + high) * 128, (low * 2 + high + 1) * 128)
                    t_high[lines, rows], t_low[lines, rows] = split(n_all[e, 2 * high + low, rows].T)

        @pl.loop(0, 4)
        def _(j):
            k = jnp.where(j == 0, 2, jnp.where(j == 1, 1, jnp.where(j == 2, 3, 0)))
            there = (z + k) % 4
            d_part[e, there] = three(t_high[...], t_low[...], pz_high[there], pz_low[there]).reshape(2, 256, 256)
            c_copy(e, k).start()

            @pl.when(jnp.logical_and(j == 0, e == 1))
            def _():
                d_near_start(0)

            @pl.when(j == 1)
            def _():
                d_far_start(e)

            @pl.when(j == 2)
            def _():
                d_cores(e, 1)
                d_copy(FREE_UP, e).start()

            @pl.when(j == 3)
            def _():
                d_cores(e, 3)
                d_copy(FREE_DOWN, e).start()

        d_cores(e, 0)

    d_near_start(1)

    def o_copy(e):
        return remote(d_sum.at[e], d_ref.at[:, e], o_send.at[e], o_recv.at[e], at(y_lo, z, y_hi, core, x))

    def o_here(e):
        return pltpu.make_async_copy(d_sum.at[e], d_ref.at[:, e], o_recv.at[e])

    for e in range(2):
        for kind in (UP, DOWN, FREE_UP, FREE_DOWN):
            d_copy(kind, e).wait_recv()
        d_sum[e] = (d_part[e, z, core] + (d_got[0, e] + d_got[1, e])).reshape(2, 128, 256)

        @pl.when(stays)
        def _():
            o_here(e).start()

        @pl.when(jnp.logical_not(stays))
        def _():
            o_copy(e).start()

    for e in range(2):

        @pl.loop(1, 16)
        def _(k):
            first(e, k).wait_send()

        @pl.loop(1, 8)
        def _(k):
            third(e, k).wait_send()

        for k in (1, 2, 3):
            second(e, k).wait_send()
        for kind in range(4):
            x_copy(kind, e).wait_send()
            c_copy(e, kind).wait_send()
            for side in range(2):
                y_copy(kind, e, side).wait_send()
        for kind in range(6):
            d_copy(kind, e).wait_send()
            for side in range(2):
                n_copy(kind, e, side).wait_send()

        @pl.when(jnp.logical_not(stays))
        def _():
            o_copy(e).wait_send()

    for half in range(2):
        k_copy(UP, half).wait_send()
        k_copy(DOWN, half).wait_send()
    k_pass(HALF_UP).wait_send()
    k_pass(HALF_DOWN).wait_send()

    @pl.loop(0, 4)
    def _(r):
        for kind in range(5):
            z_copy(kind, r).wait_send()

    for e in range(2):
        for half in range(2):
            n_out(e, half).wait()
        o_here(e).wait()


def on_device(known_inverse, factor_panel, diag_base, ancestor_map):
    blocks = jnp.arange(28, dtype=jnp.int32)
    inverse = jnp.sum(jnp.where(ancestor_map[None, :] == blocks[:, None], blocks[None, :], 0), axis=1)
    whole = pl.BlockSpec(memory_space=pl.ANY)
    dma = pltpu.SemaphoreType.DMA
    product, reduced = pl.pallas_call(
        kernel,
        out_shape=(jax.ShapeDtypeStruct((448, 512), F32), jax.ShapeDtypeStruct((2, 2, 128, 256), F32)),
        in_specs=[pl.BlockSpec(memory_space=pltpu.SMEM), whole, whole],
        out_specs=(whole, whole),
        scratch_shapes=[
            pltpu.VMEM((4, 448, 896), F32),
            pltpu.VMEM((4, 448, 896), BF),
            pltpu.VMEM((4, 448, 896), BF),
            pltpu.VMEM((112, 8, 128), F32),
            pltpu.VMEM((112, 8, 128), F32),
            pltpu.VMEM((2, 2, 56, 8, 128), F32),
            pltpu.VMEM((2, 2, 2, 2, 14, 4, 2, 8, 128), F32),
            pltpu.VMEM((4, 2, 896, 256), BF),
            pltpu.VMEM((4, 2, 896, 256), BF),
            pltpu.VMEM((2, 4, 2, 7, 8, 8, 128), F32),
            pltpu.VMEM((4, 896, 256), BF),
            pltpu.VMEM((4, 896, 256), BF),
            pltpu.VMEM((2, 4, 2, 448, 128), F32),
            pltpu.VMEM((2, 2, 2, 224, 128), F32),
            pltpu.VMEM((2, 2, 2, 448, 128), F32),
            pltpu.VMEM((2, 4, 896, 128), F32),
            pltpu.VMEM((512, 896), BF),
            pltpu.VMEM((512, 896), BF),
            pltpu.VMEM((2, 4, 2, 256, 256), F32),
            pltpu.VMEM((2, 4, 256, 256), F32),
            pltpu.VMEM((2, 2, 128, 256), F32),
            pltpu.VMEM((2, 2, 256, 256), F32),
            pltpu.VMEM((2, 2, 128, 256), F32),
            dma((2, 16)), dma((2, 16)), dma((2, 4)), dma((2, 4)), dma((2, 8)), dma((2, 8)), dma((7,)), dma((4, 2)), dma((4, 2)),
            dma((5, 4)), dma((5, 4)), dma((4, 2)), dma((4, 2)), dma((6, 2, 2)), dma((6, 2, 2)), dma((4, 2, 2)), dma((4, 2, 2)),
            dma((2, 4)), dma((2, 4)), dma((6, 2)), dma((6, 2)), dma((2, 2)), dma((2,)), dma((2,)),
        ],
        compiler_params=pltpu.CompilerParams(collective_id=0, has_side_effects=True, vmem_limit_bytes=60 << 20),
        cost_estimate=pl.CostEstimate(
            flops=6 * (448 * 1792 * 2048 + 256 * 1792 * 2048), bytes_accessed=4 << 20, transcendentals=0
        ),
        name="selected_inverse",
    )(inverse, known_inverse, factor_panel.reshape(7, 8, 8, 512))
    return (-product, diag_base + reduced.reshape(512, 256))


def solution(mesh):
    placed = (P("col", "row"), P("col", "row"), P("row", "col"), P())
    return jax.shard_map(
        on_device,
        mesh=mesh,
        in_specs=placed,
        out_specs=(P("col", "row"), P("row", "col")),
        check_vma=False,
    )
```

```python
import functools

import jax
import jax.numpy as jnp
from jax import lax
from jax.experimental import pallas as pl
from jax.experimental.pallas import tpu as pltpu
from jax.sharding import PartitionSpec as P

MESH = pl.DeviceIdType.MESH
BF = jnp.bfloat16
F32 = jnp.float32

UP, DOWN, HALF_UP, HALF_DOWN, CORE = range(5)
FREE_UP, FREE_DOWN = 4, 5


def split(value):
    high = value.astype(BF)
    return high, (value - high.astype(F32)).astype(BF)


def three(a_high, a_low, b_high, b_low):
    def dot(a, b):
        return jnp.dot(a, b, preferred_element_type=F32)

    return dot(a_high, b_high) + (dot(a_high, b_low) + dot(a_low, b_high))


def kernel(
    inv_ref, k_ref, f_ref, n_ref, d_ref,
    k_all, k_high, k_low, sent_0, sent_1, picked, p_x, p_high, p_low, p_z, pz_high, pz_low,
    n_part, n_far, n_got, n_all, t_high, t_low, d_part, d_core, d_far, d_got, d_sum,
    one_send, one_recv, two_send, two_recv, three_send, three_recv, local_sem, k_send, k_recv,
    z_send, z_recv, x_send, x_recv, n_send, n_recv, y_send, y_recv,
    c_send, c_recv, d_send, d_recv, out_sem, o_send, o_recv,
):
    row, col = lax.axis_index("row"), lax.axis_index("col")
    x, y_lo = row % 4, row // 4
    core, z, y_hi = col % 2, (col // 2) % 4, col // 8
    y, place = y_hi * 2 + y_lo, col % 8

    def at(y_hi_, z_, core_, y_lo_, x_):
        return (y_lo_ * 4 + x_, y_hi_ * 8 + z_ * 2 + core_)

    def on_x(k):
        return (y_lo * 4 + (x + k) % 4, col)

    def on_y(k):
        there = (y + k) % 4
        return at(there // 2, z, core, there % 2, x)

    def on_z(k):
        return (row, y_hi * 8 + ((z + k) % 4) * 2 + core)

    other_core = (row, y_hi * 8 + z * 2 + 1 - core)
    stays = jnp.logical_and(y_hi == y_lo, y_hi == core)

    def remote(src, dst, send, recv, device):
        return pltpu.make_async_remote_copy(
            src_ref=src, dst_ref=dst, send_sem=send, recv_sem=recv, device_id=device, device_id_type=MESH
        )

    barrier = pltpu.get_barrier_semaphore()

    def greet(device):
        pl.semaphore_signal(barrier, inc=1, device_id=device, device_id_type=MESH)

    @pl.loop(1, 16)
    def _(k):
        greet((row, (col + k) % 16))

    for k in (1, 2, 3):
        greet(on_x(k))
    for k in (1, 3):
        greet(on_y(k))

    @pl.when(jnp.logical_not(stays))
    def _():
        greet(at(core, z, y_lo, y_hi, x))

    pl.semaphore_wait(barrier, 21 - stays.astype(jnp.int32))

    sent = (sent_0, sent_1)

    def piece(to, e):
        return f_ref.at[:, to % 8, :, pl.ds(pl.multiple_of((to // 8) * 256 + e * 128, 128), 128)]

    def first(e, k):
        to = (col + k) % 16
        return remote(piece(to, e), sent[e].at[pl.ds(col * 7, 7)], one_send.at[e, k], one_recv.at[e, k], (row, to))

    def first_here(e):
        return pltpu.make_async_copy(piece(col, e), sent[e].at[pl.ds(col * 7, 7)], local_sem.at[e])

    for e in range(2):

        @pl.loop(1, 16)
        def _(k):
            first(e, k).start()

        first_here(e).start()

    def k_copy(kind, half):
        rows = pl.ds(half * 224, 224)
        return remote(
            k_ref.at[rows], k_all.at[y, rows], k_send.at[kind, half], k_recv.at[kind, half], on_y(1 if kind == UP else 3)
        )

    def k_pass(kind):
        rows = pl.ds(0, 224) if kind == HALF_UP else pl.ds(224, 224)
        ref = k_all.at[(y + (3 if kind == HALF_UP else 1)) % 4, rows]
        return remote(ref, ref, k_send.at[kind, 0], k_recv.at[kind, 0], on_y(1 if kind == HALF_UP else 3))

    k_copy(UP, 0).start()
    k_copy(DOWN, 1).start()

    def take_k(there, ref):
        k_high[there], k_low[there] = split(ref[...])

    k_here = pltpu.make_async_copy(k_ref, k_all.at[y], local_sem.at[6])
    k_here.start()
    k_here.wait()
    take_k(y, k_all.at[y])

    def second(e, k):
        to = (x + 4 - k) % 4
        i = (k + 3) % 4
        src = picked.at[e, :, pl.ds(to * 14, 14)]
        dst = p_x.at[e, i // 2, i % 2, :, :, z, core]
        if k == 0:
            return pltpu.make_async_copy(src, dst, local_sem.at[2 + e])
        return remote(src, dst, two_send.at[e, k], two_recv.at[e, k], on_x(4 - k))

    def third(e, k):
        to = (place + k) % 8
        src = picked.at[e, :, pl.ds(to * 7, 7)]
        dst = p_z.at[e, x, :, :, place]
        return remote(src, dst, three_send.at[e, k], three_recv.at[e, k], (row, y_hi * 8 + to))

    def third_here(e):
        src = picked.at[e, :, pl.ds(place * 7, 7)]
        return pltpu.make_async_copy(src, p_z.at[e, x, :, :, place], local_sem.at[4 + e])

    def third_start(e):
        @pl.loop(1, 8)
        def _(k):
            third(e, k).start()

        third_here(e).start()

    for e in range(2):
        first_here(e).wait()

        @pl.loop(1, 16)
        def _(k):
            first(e, k).wait_recv()

        for j in range(28):
            picked[e, j // 14, (j % 14) * 4 : (j % 14) * 4 + 4] = sent[e][pl.ds(inv_ref[j] * 4, 4)]
        for k in (1, 2, 3, 0):
            second(e, k).start()
        if e == 0:
            third_start(0)
            k_copy(UP, 1).start()
            k_copy(DOWN, 0).start()

    def z_copy(kind, r):
        def rows(there, chunk=slice(None)):
            return p_x.at[r // 2, r % 2, :, chunk, :, there, core]

        if kind == CORE:
            ref, to = p_x.at[r // 2, r % 2, :, :, :, :, core], other_core
        else:
            ref, to = {
                UP: (rows(z), on_z(1)),
                DOWN: (rows(z), on_z(3)),
                HALF_UP: (rows((z + 3) % 4, 0), on_z(1)),
                HALF_DOWN: (rows((z + 1) % 4, 1), on_z(3)),
            }[kind]
        return remote(ref, ref, z_send.at[kind, r], z_recv.at[kind, r], to)

    def x_copy(kind, e):
        def block(there, half=slice(None)):
            return p_z.at[e, there, half]

        ref, to = {
            UP: (block(x), on_x(1)),
            DOWN: (block(x), on_x(3)),
            HALF_UP: (block((x + 3) % 4, 0), on_x(1)),
            HALF_DOWN: (block((x + 1) % 4, 1), on_x(3)),
        }[kind]
        return remote(ref, ref, x_send.at[kind, e], x_recv.at[kind, e], to)

    def pass_on(copy, r):
        copy(UP, r).wait_recv()
        copy(HALF_UP, r).start()
        copy(DOWN, r).wait_recv()
        copy(HALF_DOWN, r).start()

    def z_start(e):
        for p in range(2):
            z_copy(UP, 2 * e + p).start()
            z_copy(DOWN, 2 * e + p).start()

    def x_start(e):
        x_copy(UP, e).start()
        x_copy(DOWN, e).start()

    def third_done(e):
        third_here(e).wait()

        @pl.loop(1, 8)
        def _(k):
            third(e, k).wait_recv()

    def second_done(e):
        second(e, 0).wait()
        for k in (1, 2, 3):
            second(e, k).wait_recv()

    second_done(0)
    z_start(0)
    third_start(1)
    third_done(0)
    x_start(0)
    second_done(1)
    pass_on(z_copy, 0)
    pass_on(z_copy, 1)
    z_start(1)
    third_done(1)
    x_start(1)

    def core_start(r):
        z_copy(HALF_UP, r).wait_recv()
        z_copy(HALF_DOWN, r).wait_recv()
        z_copy(CORE, r).start()

    pass_on(x_copy, 0)
    core_start(0)
    core_start(1)

    def n_copy(kind, e, side):
        low, high = pl.ds(0, 224), pl.ds(224, 224)
        src, dst = {
            HALF_UP: (n_part.at[e, 1, side, low], n_far.at[0, e, side]),
            HALF_DOWN: (n_part.at[e, 1, side, high], n_far.at[1, e, side]),
            UP: (n_part.at[e, 0, side, low], n_got.at[0, e, side, low]),
            DOWN: (n_part.at[e, 2, side, high], n_got.at[1, e, side, high]),
            FREE_UP: (n_part.at[e, 0, side, high], n_got.at[0, e, side, high]),
            FREE_DOWN: (n_part.at[e, 2, side, low], n_got.at[1, e, side, low]),
        }[kind]
        to = on_x(1 if kind in (UP, HALF_UP, FREE_UP) else 3)
        return remote(src, dst, n_send.at[kind, e, side], n_recv.at[kind, e, side], to)

    def n_far_start(e, side):
        n_copy(HALF_UP, e, side).start()
        n_copy(HALF_DOWN, e, side).start()

    def n_free_start(e, side):
        n_copy(FREE_UP, e, side).start()
        n_copy(FREE_DOWN, e, side).start()

    def n_near_start(e, side):
        n_copy(HALF_UP, e, side).wait_recv()
        n_part[e, 0, side, 0:224] += n_far[0, e, side]
        n_copy(UP, e, side).start()
        n_copy(HALF_DOWN, e, side).wait_recv()
        n_part[e, 2, side, 224:448] += n_far[1, e, side]
        n_copy(DOWN, e, side).start()

    def take_p(r):
        for half in range(2):

            @pl.loop(0, 7)
            def _(k):
                rows = pl.ds(pl.multiple_of(k * 128, 128), 128)
                for i in range(2):
                    columns = slice(i * 128, (i + 1) * 128)
                    p_high[r, half, rows, columns], p_low[r, half, rows, columns] = split(
                        p_x[r // 2, r % 2, i, half, pl.ds(2 * k, 2)].reshape(128, 128)
                    )

    def n_dots(r, side, half, add):
        there = side * 2 + half
        value = three(k_high[there], k_low[there], p_high[r, half], p_low[r, half])

        @pl.when(add)
        def _():
            for i in range(2):
                n_part[r // 2, 2 * (r % 2) + i, side] += value[:, i * 128 : (i + 1) * 128]

        @pl.when(jnp.logical_not(add))
        def _():
            for i in range(2):
                n_part[r // 2, 2 * (r % 2) + i, side] = value[:, i * 128 : (i + 1) * 128]

    def n_first(r):
        z_copy(CORE, r).wait_recv()
        take_p(r)

    theirs = 1 - y_hi

    @pl.loop(0, 2)
    def _(r):
        n_first(r)
        n_dots(r, y_hi, y_lo, r < 0)

    pass_on(z_copy, 2)
    for half in range(2):
        k_copy(UP, half).wait_recv()
    k_pass(HALF_UP).start()
    for half in range(2):
        k_copy(DOWN, half).wait_recv()
    k_pass(HALF_DOWN).start()
    pass_on(x_copy, 1)
    pass_on(z_copy, 3)
    take_k((y + 3) % 4, k_all.at[(y + 3) % 4])
    take_k((y + 1) % 4, k_all.at[(y + 1) % 4])
    core_start(2)

    def y_copy(kind, e, s):
        there = (y + {UP: 0, DOWN: 0, HALF_UP: 3, HALF_DOWN: 1}[kind]) % 4
        start = ((there // 2 + s) % 2) * 448 + (224 if kind == HALF_DOWN else 0)
        size = 448 if kind in (UP, DOWN) else 224
        ref = n_all.at[e, there, pl.ds(pl.multiple_of(start, 32), size)]
        to = on_y(1 if kind in (UP, HALF_UP) else 3)
        return remote(ref, ref, y_send.at[kind, e, s], y_recv.at[kind, e, s], to)

    def y_start(e, s):
        side = (y_hi + s) % 2
        for kind in (UP, DOWN, FREE_UP, FREE_DOWN):
            n_copy(kind, e, side).wait_recv()
        rows = pl.ds(pl.multiple_of(side * 448, 64), 448)
        n_all[e, y, rows] = n_part[e, 3, side] + (n_got[0, e, side] + n_got[1, e, side])
        y_copy(UP, e, s).start()
        y_copy(DOWN, e, s).start()

    def y_pass(e, s):
        y_copy(UP, e, s).wait_recv()
        y_copy(HALF_UP, e, s).start()
        y_copy(DOWN, e, s).wait_recv()
        y_copy(HALF_DOWN, e, s).start()

    @pl.loop(0, 10)
    def _(q):
        def after(step, action, *args):
            @pl.when(q == step)
            def _():
                action(*args)

        def among(*steps):
            return functools.reduce(jnp.logical_or, [q == step for step in steps])

        after(3, n_first, 2)
        after(6, n_first, 3)
        partners = among(2, 5, 8, 9)
        own_block = among(3, 6)
        add = jnp.logical_not(jnp.logical_or(partners, own_block))
        r = jnp.where(
            partners,
            jnp.where(q == 2, 0, jnp.where(q == 5, 1, q - 6)),
            jnp.where(q < 2, q, jnp.where(q < 5, 2, 3)),
        )
        n_dots(r, jnp.where(partners, theirs, y_hi), jnp.where(own_block, y_lo, 1 - y_lo), add)
        after(0, n_far_start, 0, y_hi)
        after(1, n_free_start, 0, y_hi)
        after(1, core_start, 3)
        after(4, n_far_start, 1, y_hi)
        after(4, n_near_start, 0, y_hi)
        after(7, n_free_start, 1, y_hi)
        after(8, n_near_start, 1, y_hi)
        after(9, y_start, 0, 0)

    k_pass(HALF_UP).wait_recv()
    k_pass(HALF_DOWN).wait_recv()
    take_k((y + 2) % 4, k_all.at[(y + 2) % 4])

    @pl.loop(0, 4)
    def _(t):
        n_dots(t, theirs, y_lo, t >= 0)

        @pl.when(t == 0)
        def _():
            n_far_start(0, theirs)

        @pl.when(t == 1)
        def _():
            n_free_start(0, theirs)

        @pl.when(t == 2)
        def _():
            n_far_start(1, theirs)
            y_start(1, 0)
            n_near_start(0, theirs)

        @pl.when(t == 3)
        def _():
            n_free_start(1, theirs)

    y_pass(0, 0)

    def take_z(e):
        x_copy(HALF_UP, e).wait_recv()
        x_copy(HALF_DOWN, e).wait_recv()

        @pl.loop(0, 4)
        def _(there):
            for half in range(2):
                columns = slice(e * 128, (e + 1) * 128)
                pz_high[there, half, :, columns], pz_low[there, half, :, columns] = split(
                    p_z[e, there, half].reshape(448, 128)
                )

    take_z(0)
    take_z(1)
    n_near_start(1, theirs)
    y_pass(1, 0)
    y_start(0, 1)

    def c_copy(e, k):
        there = (z + k) % 4
        return remote(d_part.at[e, there, 1 - core], d_core.at[e, there], c_send.at[e, k], c_recv.at[e, k], other_core)

    def d_copy(kind, e):
        two, up_, down_ = ((z + k) % 4 for k in (2, 1, 3))
        src, dst = {
            HALF_UP: (d_part.at[e, two, core, 0], d_far.at[0, e]),
            HALF_DOWN: (d_part.at[e, two, core, 1], d_far.at[1, e]),
            UP: (d_part.at[e, up_, core, 0], d_got.at[0, e, 0]),
            DOWN: (d_part.at[e, down_, core, 1], d_got.at[1, e, 1]),
            FREE_UP: (d_part.at[e, up_, core, 1], d_got.at[0, e, 1]),
            FREE_DOWN: (d_part.at[e, down_, core, 0], d_got.at[1, e, 0]),
        }[kind]
        to = on_z(1 if kind in (UP, HALF_UP, FREE_UP) else 3)
        return remote(src, dst, d_send.at[kind, e], d_recv.at[kind, e], to)

    def d_cores(e, k):
        there = (z + k) % 4
        c_copy(e, k).wait_recv()
        d_part[e, there, core] += d_core[e, there]

    def d_far_start(e):
        d_cores(e, 2)
        d_copy(HALF_UP, e).start()
        d_copy(HALF_DOWN, e).start()

    def d_near_start(e):
        d_copy(HALF_UP, e).wait_recv()
        d_part[e, (z + 1) % 4, core, 0] += d_far[0, e]
        d_copy(UP, e).start()
        d_copy(HALF_DOWN, e).wait_recv()
        d_part[e, (z + 3) % 4, core, 1] += d_far[1, e]
        d_copy(DOWN, e).start()

    def n_out(e, half):
        src = n_all.at[e, half * 2 + y_lo, pl.ds(pl.multiple_of(y_hi * 448, 64), 448)]
        columns = pl.ds(pl.multiple_of(half * 256 + e * 128, 128), 128)
        return pltpu.make_async_copy(src, n_ref.at[:, columns], out_sem.at[e, half])

    def d_rows(e, s):
        for kind in (HALF_UP, HALF_DOWN):
            y_copy(kind, e, s).wait_recv()
        for high in range(2):
            for low in range(2):
                lines = slice(low * 128, (low + 1) * 128)
                for first_row, size in ((0, 128), (128, 128), (256, 128), (384, 64)):
                    start = (high + s) % 2 * 448 + first_row
                    value = n_all[e, 2 * high + low, start : start + size].T
                    columns = slice(first_row, first_row + size)
                    t_high[high, lines, columns], t_low[high, lines, columns] = split(value)

    def d_dots(s, there, high):
        side = (high + s) % 2
        return three(t_high[high], t_low[high], pz_high[there, side], pz_low[there, side])

    def d_early(e):
        d_rows(e, 0)

        @pl.loop(0, 8)
        def _(q):
            there, high = q // 2, q % 2
            d_part[e, there, :, high] = d_dots(0, there, high).reshape(2, 128, 256)

    def d_late(e):
        d_rows(e, 1)
        for half in range(2):
            n_out(e, half).start()

        @pl.loop(0, 4)
        def _(j):
            k = jnp.where(j == 0, 2, jnp.where(j == 1, 1, jnp.where(j == 2, 3, 0)))
            there = (z + k) % 4

            @pl.loop(0, 2)
            def _(high):
                d_part[e, there, :, high] += d_dots(1, there, high).reshape(2, 128, 256)

            c_copy(e, k).start()

            @pl.when(j == 1)
            def _():
                d_far_start(e)
                if e == 0:
                    y_pass(1, 1)

            @pl.when(j == 2)
            def _():
                d_cores(e, 1)
                d_copy(FREE_UP, e).start()

            @pl.when(j == 3)
            def _():
                d_cores(e, 3)
                d_copy(FREE_DOWN, e).start()

        d_cores(e, 0)

    d_early(0)
    y_pass(0, 1)
    y_start(1, 1)
    d_early(1)
    d_late(0)
    d_near_start(0)
    d_late(1)
    d_near_start(1)

    def o_copy(e):
        return remote(d_sum.at[e], d_ref.at[:, e], o_send.at[e], o_recv.at[e], at(y_lo, z, y_hi, core, x))

    def o_here(e):
        return pltpu.make_async_copy(d_sum.at[e], d_ref.at[:, e], o_recv.at[e])

    for e in range(2):
        for kind in (UP, DOWN, FREE_UP, FREE_DOWN):
            d_copy(kind, e).wait_recv()
        d_sum[e] = d_part[e, z, core] + (d_got[0, e] + d_got[1, e])

        @pl.when(stays)
        def _():
            o_here(e).start()

        @pl.when(jnp.logical_not(stays))
        def _():
            o_copy(e).start()

    for e in range(2):

        @pl.loop(1, 16)
        def _(k):
            first(e, k).wait_send()

        @pl.loop(1, 8)
        def _(k):
            third(e, k).wait_send()

        for k in (1, 2, 3):
            second(e, k).wait_send()
        for kind in range(4):
            x_copy(kind, e).wait_send()
            c_copy(e, kind).wait_send()
            for side in range(2):
                y_copy(kind, e, side).wait_send()
        for kind in range(6):
            d_copy(kind, e).wait_send()
            for side in range(2):
                n_copy(kind, e, side).wait_send()

        @pl.when(jnp.logical_not(stays))
        def _():
            o_copy(e).wait_send()

    for half in range(2):
        k_copy(UP, half).wait_send()
        k_copy(DOWN, half).wait_send()
    k_pass(HALF_UP).wait_send()
    k_pass(HALF_DOWN).wait_send()

    @pl.loop(0, 4)
    def _(r):
        for kind in range(5):
            z_copy(kind, r).wait_send()

    for e in range(2):
        for half in range(2):
            n_out(e, half).wait()
        o_here(e).wait()


def on_device(known_inverse, factor_panel, diag_base, ancestor_map):
    blocks = jnp.arange(28, dtype=jnp.int32)
    inverse = jnp.sum(jnp.where(ancestor_map[None, :] == blocks[:, None], blocks[None, :], 0), axis=1)
    whole = pl.BlockSpec(memory_space=pl.ANY)
    dma = pltpu.SemaphoreType.DMA
    product, reduced = pl.pallas_call(
        kernel,
        out_shape=(jax.ShapeDtypeStruct((448, 512), F32), jax.ShapeDtypeStruct((2, 2, 128, 256), F32)),
        in_specs=[pl.BlockSpec(memory_space=pltpu.SMEM), whole, whole],
        out_specs=(whole, whole),
        scratch_shapes=[
            pltpu.VMEM((4, 448, 896), F32),
            pltpu.VMEM((4, 448, 896), BF),
            pltpu.VMEM((4, 448, 896), BF),
            pltpu.VMEM((112, 8, 128), F32),
            pltpu.VMEM((112, 8, 128), F32),
            pltpu.VMEM((2, 2, 56, 8, 128), F32),
            pltpu.VMEM((2, 2, 2, 2, 14, 4, 2, 8, 128), F32),
            pltpu.VMEM((4, 2, 896, 256), BF),
            pltpu.VMEM((4, 2, 896, 256), BF),
            pltpu.VMEM((2, 4, 2, 7, 8, 8, 128), F32),
            pltpu.VMEM((4, 2, 448, 256), BF),
            pltpu.VMEM((4, 2, 448, 256), BF),
            pltpu.VMEM((2, 4, 2, 448, 128), F32),
            pltpu.VMEM((2, 2, 2, 224, 128), F32),
            pltpu.VMEM((2, 2, 2, 448, 128), F32),
            pltpu.VMEM((2, 4, 896, 128), F32),
            pltpu.VMEM((2, 256, 448), BF),
            pltpu.VMEM((2, 256, 448), BF),
            pltpu.VMEM((2, 4, 2, 2, 128, 256), F32),
            pltpu.VMEM((2, 4, 2, 128, 256), F32),
            pltpu.VMEM((2, 2, 128, 256), F32),
            pltpu.VMEM((2, 2, 2, 128, 256), F32),
            pltpu.VMEM((2, 2, 128, 256), F32),
            dma((2, 16)), dma((2, 16)), dma((2, 4)), dma((2, 4)), dma((2, 8)), dma((2, 8)), dma((7,)), dma((4, 2)), dma((4, 2)),
            dma((5, 4)), dma((5, 4)), dma((4, 2)), dma((4, 2)), dma((6, 2, 2)), dma((6, 2, 2)), dma((4, 2, 2)), dma((4, 2, 2)),
            dma((2, 4)), dma((2, 4)), dma((6, 2)), dma((6, 2)), dma((2, 2)), dma((2,)), dma((2,)),
        ],
        compiler_params=pltpu.CompilerParams(collective_id=0, has_side_effects=True, vmem_limit_bytes=60 << 20),
        cost_estimate=pl.CostEstimate(
            flops=6 * (448 * 1792 * 2048 + 256 * 1792 * 2048), bytes_accessed=4 << 20, transcendentals=0
        ),
        name="selected_inverse",
    )(inverse, known_inverse, factor_panel.reshape(7, 8, 8, 512))
    return (-product, diag_base + reduced.reshape(512, 256))


def solution(mesh):
    placed = (P("col", "row"), P("col", "row"), P("row", "col"), P())
    return jax.shard_map(
        on_device,
        mesh=mesh,
        in_specs=placed,
        out_specs=(P("col", "row"), P("row", "col")),
        check_vma=False,
    )
```

```python
import functools

import jax
import jax.numpy as jnp
from jax import lax
from jax.experimental import pallas as pl
from jax.experimental.pallas import tpu as pltpu
from jax.sharding import PartitionSpec as P

MESH = pl.DeviceIdType.MESH
BF = jnp.bfloat16
F32 = jnp.float32

UP, DOWN, HALF_UP, HALF_DOWN, CORE = range(5)
FREE_UP, FREE_DOWN = 4, 5


def split(value):
    high = value.astype(BF)
    return high, (value - high.astype(F32)).astype(BF)


def three(a_high, a_low, b_high, b_low):
    def dot(a, b):
        return jnp.dot(a, b, preferred_element_type=F32)

    return dot(a_high, b_high) + (dot(a_high, b_low) + dot(a_low, b_high))


def kernel(
    map_ref, k_ref, f_ref, n_ref, d_ref,
    k_all, k_high, k_low, sent_0, sent_1, picked, p_x, p_high, p_low, p_z, pz_high, pz_low,
    n_part, n_far, n_got, n_all, t_high, t_low, d_part, d_core, d_far, d_got, d_sum,
    one_send, one_recv, two_send, two_recv, three_send, three_recv, local_sem, k_send, k_recv,
    z_send, z_recv, x_send, x_recv, n_send, n_recv, y_send, y_recv,
    c_send, c_recv, d_send, d_recv, out_sem, o_send, o_recv,
):
    row, col = lax.axis_index("row"), lax.axis_index("col")
    x, y_lo = row % 4, row // 4
    core, z, y_hi = col % 2, (col // 2) % 4, col // 8
    y, place = y_hi * 2 + y_lo, col % 8

    def at(y_hi_, z_, core_, y_lo_, x_):
        return (y_lo_ * 4 + x_, y_hi_ * 8 + z_ * 2 + core_)

    def on_x(k):
        return (y_lo * 4 + (x + k) % 4, col)

    def on_y(k):
        there = (y + k) % 4
        return at(there // 2, z, core, there % 2, x)

    def on_z(k):
        return (row, y_hi * 8 + ((z + k) % 4) * 2 + core)

    other_core = (row, y_hi * 8 + z * 2 + 1 - core)
    stays = jnp.logical_and(y_hi == y_lo, y_hi == core)

    def remote(src, dst, send, recv, device):
        return pltpu.make_async_remote_copy(
            src_ref=src, dst_ref=dst, send_sem=send, recv_sem=recv, device_id=device, device_id_type=MESH
        )

    barrier = pltpu.get_barrier_semaphore()

    def greet(device):
        pl.semaphore_signal(barrier, inc=1, device_id=device, device_id_type=MESH)

    @pl.loop(1, 16)
    def _(k):
        greet((row, (col + k) % 16))

    for k in (1, 2, 3):
        greet(on_x(k))
    for k in (1, 3):
        greet(on_y(k))

    @pl.when(jnp.logical_not(stays))
    def _():
        greet(at(core, z, y_lo, y_hi, x))

    pl.semaphore_wait(barrier, 21 - stays.astype(jnp.int32))

    sent = (sent_0, sent_1)

    def piece(to, e):
        return f_ref.at[:, to % 8, :, pl.ds(pl.multiple_of((to // 8) * 256 + e * 128, 128), 128)]

    def first(e, k):
        to = (col + k) % 16
        return remote(piece(to, e), sent[e].at[pl.ds(col * 7, 7)], one_send.at[e, k], one_recv.at[e, k], (row, to))

    def first_here(e):
        return pltpu.make_async_copy(piece(col, e), sent[e].at[pl.ds(col * 7, 7)], local_sem.at[e])

    for e in range(2):

        @pl.loop(1, 16)
        def _(k):
            first(e, k).start()

        first_here(e).start()

    def k_copy(kind, half):
        rows = pl.ds(half * 224, 224)
        return remote(
            k_ref.at[rows], k_all.at[y, rows], k_send.at[kind, half], k_recv.at[kind, half], on_y(1 if kind == UP else 3)
        )

    def k_pass(kind):
        rows = pl.ds(0, 224) if kind == HALF_UP else pl.ds(224, 224)
        ref = k_all.at[(y + (3 if kind == HALF_UP else 1)) % 4, rows]
        return remote(ref, ref, k_send.at[kind, 0], k_recv.at[kind, 0], on_y(1 if kind == HALF_UP else 3))

    k_copy(UP, 0).start()
    k_copy(DOWN, 1).start()

    def take_k(there, ref):
        k_high[there], k_low[there] = split(ref[...])

    k_here = pltpu.make_async_copy(k_ref, k_all.at[y], local_sem.at[6])
    k_here.start()
    k_here.wait()
    take_k(y, k_all.at[y])

    def second(e, k):
        to = (x + 4 - k) % 4
        i = (k + 3) % 4
        src = picked.at[e, :, pl.ds(to * 14, 14)]
        dst = p_x.at[e, i // 2, i % 2, :, :, z, core]
        if k == 0:
            return pltpu.make_async_copy(src, dst, local_sem.at[2 + e])
        return remote(src, dst, two_send.at[e, k], two_recv.at[e, k], on_x(4 - k))

    def third(e, k):
        to = (place + k) % 8
        src = picked.at[e, :, pl.ds(to * 7, 7)]
        dst = p_z.at[e, x, :, :, place]
        return remote(src, dst, three_send.at[e, k], three_recv.at[e, k], (row, y_hi * 8 + to))

    def third_here(e):
        src = picked.at[e, :, pl.ds(place * 7, 7)]
        return pltpu.make_async_copy(src, p_z.at[e, x, :, :, place], local_sem.at[4 + e])

    stored = [map_ref[t] for t in range(28)]
    inverse = [functools.reduce(jnp.maximum, [jnp.where(stored[t] == j, t, 0) for t in range(1, 28)]) for j in range(28)]

    def third_start(e):
        @pl.loop(1, 8)
        def _(k):
            third(e, k).start()

        third_here(e).start()

    for e in range(2):
        first_here(e).wait()

        @pl.loop(1, 16)
        def _(k):
            first(e, k).wait_recv()

        for j in range(28):
            picked[e, j // 14, (j % 14) * 4 : (j % 14) * 4 + 4] = sent[e][pl.ds(inverse[j] * 4, 4)]
        for k in (1, 2, 3, 0):
            second(e, k).start()
        if e == 0:
            third_start(0)
            k_copy(UP, 1).start()
            k_copy(DOWN, 0).start()

    def z_copy(kind, r):
        def rows(there, chunk=slice(None)):
            return p_x.at[r // 2, r % 2, :, chunk, :, there, core]

        if kind == CORE:
            ref, to = p_x.at[r // 2, r % 2, :, :, :, :, core], other_core
        else:
            ref, to = {
                UP: (rows(z), on_z(1)),
                DOWN: (rows(z), on_z(3)),
                HALF_UP: (rows((z + 3) % 4, 0), on_z(1)),
                HALF_DOWN: (rows((z + 1) % 4, 1), on_z(3)),
            }[kind]
        return remote(ref, ref, z_send.at[kind, r], z_recv.at[kind, r], to)

    def x_copy(kind, e):
        def block(there, half=slice(None)):
            return p_z.at[e, there, half]

        ref, to = {
            UP: (block(x), on_x(1)),
            DOWN: (block(x), on_x(3)),
            HALF_UP: (block((x + 3) % 4, 0), on_x(1)),
            HALF_DOWN: (block((x + 1) % 4, 1), on_x(3)),
        }[kind]
        return remote(ref, ref, x_send.at[kind, e], x_recv.at[kind, e], to)

    def pass_on(copy, r):
        copy(UP, r).wait_recv()
        copy(HALF_UP, r).start()
        copy(DOWN, r).wait_recv()
        copy(HALF_DOWN, r).start()

    def z_start(e):
        for p in range(2):
            z_copy(UP, 2 * e + p).start()
            z_copy(DOWN, 2 * e + p).start()

    def x_start(e):
        x_copy(UP, e).start()
        x_copy(DOWN, e).start()

    def third_done(e):
        third_here(e).wait()

        @pl.loop(1, 8)
        def _(k):
            third(e, k).wait_recv()

    def second_done(e):
        second(e, 0).wait()
        for k in (1, 2, 3):
            second(e, k).wait_recv()

    second_done(0)
    z_start(0)
    third_start(1)
    third_done(0)
    x_start(0)
    second_done(1)
    pass_on(z_copy, 0)
    pass_on(z_copy, 1)
    z_start(1)
    third_done(1)
    x_start(1)

    def core_start(r):
        z_copy(HALF_UP, r).wait_recv()
        z_copy(HALF_DOWN, r).wait_recv()
        z_copy(CORE, r).start()

    pass_on(x_copy, 0)
    core_start(0)
    core_start(1)

    def n_copy(kind, e, side):
        low, high = pl.ds(0, 224), pl.ds(224, 224)
        src, dst = {
            HALF_UP: (n_part.at[e, 1, side, low], n_far.at[0, e, side]),
            HALF_DOWN: (n_part.at[e, 1, side, high], n_far.at[1, e, side]),
            UP: (n_part.at[e, 0, side, low], n_got.at[0, e, side, low]),
            DOWN: (n_part.at[e, 2, side, high], n_got.at[1, e, side, high]),
            FREE_UP: (n_part.at[e, 0, side, high], n_got.at[0, e, side, high]),
            FREE_DOWN: (n_part.at[e, 2, side, low], n_got.at[1, e, side, low]),
        }[kind]
        to = on_x(1 if kind in (UP, HALF_UP, FREE_UP) else 3)
        return remote(src, dst, n_send.at[kind, e, side], n_recv.at[kind, e, side], to)

    def n_far_start(e, side):
        n_copy(HALF_UP, e, side).start()
        n_copy(HALF_DOWN, e, side).start()

    def n_free_start(e, side):
        n_copy(FREE_UP, e, side).start()
        n_copy(FREE_DOWN, e, side).start()

    def n_near_start(e, side):
        n_copy(HALF_UP, e, side).wait_recv()
        n_part[e, 0, side, 0:224] += n_far[0, e, side]
        n_copy(UP, e, side).start()
        n_copy(HALF_DOWN, e, side).wait_recv()
        n_part[e, 2, side, 224:448] += n_far[1, e, side]
        n_copy(DOWN, e, side).start()

    def take_p(r):
        for half in range(2):

            @pl.loop(0, 7)
            def _(k):
                rows = pl.ds(pl.multiple_of(k * 128, 128), 128)
                for i in range(2):
                    columns = slice(i * 128, (i + 1) * 128)
                    p_high[r, half, rows, columns], p_low[r, half, rows, columns] = split(
                        p_x[r // 2, r % 2, i, half, pl.ds(2 * k, 2)].reshape(128, 128)
                    )

    def n_dots(r, side, half, add):
        there = side * 2 + half
        value = three(k_high[there], k_low[there], p_high[r, half], p_low[r, half])

        @pl.when(add)
        def _():
            for i in range(2):
                n_part[r // 2, 2 * (r % 2) + i, side] += value[:, i * 128 : (i + 1) * 128]

        @pl.when(jnp.logical_not(add))
        def _():
            for i in range(2):
                n_part[r // 2, 2 * (r % 2) + i, side] = value[:, i * 128 : (i + 1) * 128]

    def n_first(r):
        z_copy(CORE, r).wait_recv()
        take_p(r)

    theirs = 1 - y_hi

    @pl.loop(0, 2)
    def _(r):
        n_first(r)
        n_dots(r, y_hi, y_lo, r < 0)

    pass_on(z_copy, 2)
    for half in range(2):
        k_copy(UP, half).wait_recv()
    k_pass(HALF_UP).start()
    for half in range(2):
        k_copy(DOWN, half).wait_recv()
    k_pass(HALF_DOWN).start()
    pass_on(x_copy, 1)
    pass_on(z_copy, 3)
    take_k((y + 3) % 4, k_all.at[(y + 3) % 4])
    take_k((y + 1) % 4, k_all.at[(y + 1) % 4])
    core_start(2)

    def y_copy(kind, e, s):
        there = (y + {UP: 0, DOWN: 0, HALF_UP: 3, HALF_DOWN: 1}[kind]) % 4
        start = ((there // 2 + s) % 2) * 448 + (224 if kind == HALF_DOWN else 0)
        size = 448 if kind in (UP, DOWN) else 224
        ref = n_all.at[e, there, pl.ds(pl.multiple_of(start, 32), size)]
        to = on_y(1 if kind in (UP, HALF_UP) else 3)
        return remote(ref, ref, y_send.at[kind, e, s], y_recv.at[kind, e, s], to)

    def y_start(e, s):
        side = (y_hi + s) % 2
        for kind in (UP, DOWN, FREE_UP, FREE_DOWN):
            n_copy(kind, e, side).wait_recv()
        rows = pl.ds(pl.multiple_of(side * 448, 64), 448)
        n_all[e, y, rows] = n_part[e, 3, side] + (n_got[0, e, side] + n_got[1, e, side])
        y_copy(UP, e, s).start()
        y_copy(DOWN, e, s).start()

    def y_pass(e, s):
        y_copy(UP, e, s).wait_recv()
        y_copy(HALF_UP, e, s).start()
        y_copy(DOWN, e, s).wait_recv()
        y_copy(HALF_DOWN, e, s).start()

    @pl.loop(0, 10)
    def _(q):
        def after(step, action, *args):
            @pl.when(q == step)
            def _():
                action(*args)

        def among(*steps):
            return functools.reduce(jnp.logical_or, [q == step for step in steps])

        after(3, n_first, 2)
        after(6, n_first, 3)
        partners = among(2, 5, 8, 9)
        own_block = among(3, 6)
        add = jnp.logical_not(jnp.logical_or(partners, own_block))
        r = jnp.where(
            partners,
            jnp.where(q == 2, 0, jnp.where(q == 5, 1, q - 6)),
            jnp.where(q < 2, q, jnp.where(q < 5, 2, 3)),
        )
        n_dots(r, jnp.where(partners, theirs, y_hi), jnp.where(own_block, y_lo, 1 - y_lo), add)
        after(0, n_far_start, 0, y_hi)
        after(1, n_free_start, 0, y_hi)
        after(1, core_start, 3)
        after(4, n_far_start, 1, y_hi)
        after(4, n_near_start, 0, y_hi)
        after(7, n_free_start, 1, y_hi)
        after(8, n_near_start, 1, y_hi)
        after(9, y_start, 0, 0)

    k_pass(HALF_UP).wait_recv()
    k_pass(HALF_DOWN).wait_recv()
    take_k((y + 2) % 4, k_all.at[(y + 2) % 4])

    @pl.loop(0, 4)
    def _(t):
        n_dots(t, theirs, y_lo, t >= 0)

        @pl.when(t == 0)
        def _():
            n_far_start(0, theirs)

        @pl.when(t == 1)
        def _():
            n_free_start(0, theirs)

        @pl.when(t == 2)
        def _():
            y_start(1, 0)
            n_near_start(0, theirs)
            n_far_start(1, theirs)

        @pl.when(t == 3)
        def _():
            n_free_start(1, theirs)

    y_pass(0, 0)

    def take_z(e):
        x_copy(HALF_UP, e).wait_recv()
        x_copy(HALF_DOWN, e).wait_recv()

        @pl.loop(0, 4)
        def _(there):
            for half in range(2):
                columns = slice(e * 128, (e + 1) * 128)
                pz_high[there, half, :, columns], pz_low[there, half, :, columns] = split(
                    p_z[e, there, half].reshape(448, 128)
                )

    take_z(0)
    take_z(1)
    y_start(0, 1)
    n_near_start(1, theirs)
    y_pass(1, 0)

    def c_copy(e, k):
        there = (z + k) % 4
        return remote(d_part.at[e, there, 1 - core], d_core.at[e, there], c_send.at[e, k], c_recv.at[e, k], other_core)

    def d_copy(kind, e):
        two, up_, down_ = ((z + k) % 4 for k in (2, 1, 3))
        src, dst = {
            HALF_UP: (d_part.at[e, two, core, 0], d_far.at[0, e]),
            HALF_DOWN: (d_part.at[e, two, core, 1], d_far.at[1, e]),
            UP: (d_part.at[e, up_, core, 0], d_got.at[0, e, 0]),
            DOWN: (d_part.at[e, down_, core, 1], d_got.at[1, e, 1]),
            FREE_UP: (d_part.at[e, up_, core, 1], d_got.at[0, e, 1]),
            FREE_DOWN: (d_part.at[e, down_, core, 0], d_got.at[1, e, 0]),
        }[kind]
        to = on_z(1 if kind in (UP, HALF_UP, FREE_UP) else 3)
        return remote(src, dst, d_send.at[kind, e], d_recv.at[kind, e], to)

    def d_cores(e, k):
        there = (z + k) % 4
        c_copy(e, k).wait_recv()
        d_part[e, there, core] += d_core[e, there]

    def d_far_start(e):
        d_cores(e, 2)
        d_copy(HALF_UP, e).start()
        d_copy(HALF_DOWN, e).start()

    def d_near_start(e):
        d_copy(HALF_UP, e).wait_recv()
        d_part[e, (z + 1) % 4, core, 0] += d_far[0, e]
        d_copy(UP, e).start()
        d_copy(HALF_DOWN, e).wait_recv()
        d_part[e, (z + 3) % 4, core, 1] += d_far[1, e]
        d_copy(DOWN, e).start()

    def n_out(e, half):
        src = n_all.at[e, half * 2 + y_lo, pl.ds(pl.multiple_of(y_hi * 448, 64), 448)]
        columns = pl.ds(pl.multiple_of(half * 256 + e * 128, 128), 128)
        return pltpu.make_async_copy(src, n_ref.at[:, columns], out_sem.at[e, half])

    def d_rows(e, s):
        for kind in (HALF_UP, HALF_DOWN):
            y_copy(kind, e, s).wait_recv()
        for high in range(2):
            for low in range(2):
                lines = slice(low * 128, (low + 1) * 128)
                for first_row, size in ((0, 128), (128, 128), (256, 128), (384, 64)):
                    start = (high + s) % 2 * 448 + first_row
                    value = n_all[e, 2 * high + low, start : start + size].T
                    columns = slice(first_row, first_row + size)
                    t_high[high, lines, columns], t_low[high, lines, columns] = split(value)

    def d_dots(s, there, high):
        side = (high + s) % 2
        return three(t_high[high], t_low[high], pz_high[there, side], pz_low[there, side])

    def d_early(e):
        d_rows(e, 0)

        @pl.loop(0, 8)
        def _(q):
            there, high = q // 2, q % 2
            d_part[e, there, :, high] = d_dots(0, there, high).reshape(2, 128, 256)

    def d_late(e):
        d_rows(e, 1)
        for half in range(2):
            n_out(e, half).start()

        @pl.loop(0, 4)
        def _(j):
            k = jnp.where(j == 0, 2, jnp.where(j == 1, 1, jnp.where(j == 2, 3, 0)))
            there = (z + k) % 4

            @pl.loop(0, 2)
            def _(high):
                d_part[e, there, :, high] += d_dots(1, there, high).reshape(2, 128, 256)

            c_copy(e, k).start()

            @pl.when(j == 2)
            def _():
                d_far_start(e)

            @pl.when(j == 3)
            def _():
                d_cores(e, 1)
                d_copy(FREE_UP, e).start()
                if e == 0:
                    y_pass(1, 1)

        d_cores(e, 3)
        d_copy(FREE_DOWN, e).start()
        d_cores(e, 0)

    d_early(0)
    y_pass(0, 1)
    y_start(1, 1)
    d_early(1)
    d_late(0)
    d_near_start(0)
    d_late(1)

    def o_copy(e):
        return remote(d_sum.at[e], d_ref.at[:, e], o_send.at[e], o_recv.at[e], at(y_lo, z, y_hi, core, x))

    def o_here(e):
        return pltpu.make_async_copy(d_sum.at[e], d_ref.at[:, e], o_recv.at[e])

    def o_start(e):
        for kind in (UP, DOWN, FREE_UP, FREE_DOWN):
            d_copy(kind, e).wait_recv()
        d_sum[e] = d_part[e, z, core] + (d_got[0, e] + d_got[1, e])

        @pl.when(stays)
        def _():
            o_here(e).start()

        @pl.when(jnp.logical_not(stays))
        def _():
            o_copy(e).start()

    o_start(0)
    d_near_start(1)
    o_start(1)

    for e in range(2):

        @pl.loop(1, 16)
        def _(k):
            first(e, k).wait_send()

        @pl.loop(1, 8)
        def _(k):
            third(e, k).wait_send()

        for k in (1, 2, 3):
            second(e, k).wait_send()
        for kind in range(4):
            x_copy(kind, e).wait_send()
            c_copy(e, kind).wait_send()
            for side in range(2):
                y_copy(kind, e, side).wait_send()
        for kind in range(6):
            d_copy(kind, e).wait_send()
            for side in range(2):
                n_copy(kind, e, side).wait_send()

        @pl.when(jnp.logical_not(stays))
        def _():
            o_copy(e).wait_send()

    for half in range(2):
        k_copy(UP, half).wait_send()
        k_copy(DOWN, half).wait_send()
    k_pass(HALF_UP).wait_send()
    k_pass(HALF_DOWN).wait_send()

    @pl.loop(0, 4)
    def _(r):
        for kind in range(5):
            z_copy(kind, r).wait_send()

    for e in range(2):
        for half in range(2):
            n_out(e, half).wait()
        o_here(e).wait()


def on_device(known_inverse, factor_panel, diag_base, ancestor_map):
    whole = pl.BlockSpec(memory_space=pl.ANY)
    dma = pltpu.SemaphoreType.DMA
    product, reduced = pl.pallas_call(
        kernel,
        out_shape=(jax.ShapeDtypeStruct((448, 512), F32), jax.ShapeDtypeStruct((2, 2, 128, 256), F32)),
        in_specs=[pl.BlockSpec(memory_space=pltpu.SMEM), whole, whole],
        out_specs=(whole, whole),
        scratch_shapes=[
            pltpu.VMEM((4, 448, 896), F32),
            pltpu.VMEM((4, 448, 896), BF),
            pltpu.VMEM((4, 448, 896), BF),
            pltpu.VMEM((112, 8, 128), F32),
            pltpu.VMEM((112, 8, 128), F32),
            pltpu.VMEM((2, 2, 56, 8, 128), F32),
            pltpu.VMEM((2, 2, 2, 2, 14, 4, 2, 8, 128), F32),
            pltpu.VMEM((4, 2, 896, 256), BF),
            pltpu.VMEM((4, 2, 896, 256), BF),
            pltpu.VMEM((2, 4, 2, 7, 8, 8, 128), F32),
            pltpu.VMEM((4, 2, 448, 256), BF),
            pltpu.VMEM((4, 2, 448, 256), BF),
            pltpu.VMEM((2, 4, 2, 448, 128), F32),
            pltpu.VMEM((2, 2, 2, 224, 128), F32),
            pltpu.VMEM((2, 2, 2, 448, 128), F32),
            pltpu.VMEM((2, 4, 896, 128), F32),
            pltpu.VMEM((2, 256, 448), BF),
            pltpu.VMEM((2, 256, 448), BF),
            pltpu.VMEM((2, 4, 2, 2, 128, 256), F32),
            pltpu.VMEM((2, 4, 2, 128, 256), F32),
            pltpu.VMEM((2, 2, 128, 256), F32),
            pltpu.VMEM((2, 2, 2, 128, 256), F32),
            pltpu.VMEM((2, 2, 128, 256), F32),
            dma((2, 16)), dma((2, 16)), dma((2, 4)), dma((2, 4)), dma((2, 8)), dma((2, 8)), dma((7,)), dma((4, 2)), dma((4, 2)),
            dma((5, 4)), dma((5, 4)), dma((4, 2)), dma((4, 2)), dma((6, 2, 2)), dma((6, 2, 2)), dma((4, 2, 2)), dma((4, 2, 2)),
            dma((2, 4)), dma((2, 4)), dma((6, 2)), dma((6, 2)), dma((2, 2)), dma((2,)), dma((2,)),
        ],
        compiler_params=pltpu.CompilerParams(collective_id=0, has_side_effects=True, vmem_limit_bytes=60 << 20),
        cost_estimate=pl.CostEstimate(
            flops=6 * (448 * 1792 * 2048 + 256 * 1792 * 2048), bytes_accessed=4 << 20, transcendentals=0
        ),
        name="selected_inverse",
    )(ancestor_map, known_inverse, factor_panel.reshape(7, 8, 8, 512))
    return (-product, diag_base + reduced.reshape(512, 256))


def solution(mesh):
    placed = (P("col", "row"), P("col", "row"), P("row", "col"), P())
    return jax.shard_map(
        on_device,
        mesh=mesh,
        in_specs=placed,
        out_specs=(P("col", "row"), P("row", "col")),
        check_vma=False,
    )
```

```python
import functools

import jax
import jax.numpy as jnp
from jax import lax
from jax.experimental import pallas as pl
from jax.experimental.pallas import tpu as pltpu
from jax.sharding import PartitionSpec as P

MESH = pl.DeviceIdType.MESH
BF = jnp.bfloat16
F32 = jnp.float32

UP, DOWN, HALF_UP, HALF_DOWN, CORE = range(5)
FREE_UP, FREE_DOWN = 4, 5


def split(value):
    high = value.astype(BF)
    return high, (value - high.astype(F32)).astype(BF)


def three(a_high, a_low, b_high, b_low):
    def dot(a, b):
        return jnp.dot(a, b, preferred_element_type=F32)

    return dot(a_high, b_high) + (dot(a_high, b_low) + dot(a_low, b_high))


def kernel(
    map_ref, k_ref, f_ref, n_ref, d_ref,
    k_all, k_high, k_low, sent_0, sent_1, picked, p_x, p_high, p_low, p_z, pz_high, pz_low,
    n_part, n_far, n_got, n_all, t_high, t_low, d_part, d_core, d_far, d_got, d_sum,
    one_send, one_recv, two_send, two_recv, three_send, three_recv, local_sem, k_send, k_recv,
    z_send, z_recv, x_send, x_recv, n_send, n_recv, y_send, y_recv,
    c_send, c_recv, d_send, d_recv, out_sem, o_send, o_recv,
):
    row, col = lax.axis_index("row"), lax.axis_index("col")
    x, y_lo = row % 4, row // 4
    core, z, y_hi = col % 2, (col // 2) % 4, col // 8
    y, place = y_hi * 2 + y_lo, col % 8

    def at(y_hi_, z_, core_, y_lo_, x_):
        return (y_lo_ * 4 + x_, y_hi_ * 8 + z_ * 2 + core_)

    def on_x(k):
        return (y_lo * 4 + (x + k) % 4, col)

    def on_y(k):
        there = (y + k) % 4
        return at(there // 2, z, core, there % 2, x)

    def on_z(k):
        return (row, y_hi * 8 + ((z + k) % 4) * 2 + core)

    other_core = (row, y_hi * 8 + z * 2 + 1 - core)
    stays = jnp.logical_and(y_hi == y_lo, y_hi == core)

    def remote(src, dst, send, recv, device):
        return pltpu.make_async_remote_copy(
            src_ref=src, dst_ref=dst, send_sem=send, recv_sem=recv, device_id=device, device_id_type=MESH
        )

    barrier = pltpu.get_barrier_semaphore()

    def greet(device):
        pl.semaphore_signal(barrier, inc=1, device_id=device, device_id_type=MESH)

    @pl.loop(1, 16)
    def _(k):
        greet((row, (col + k) % 16))

    for k in (1, 2, 3):
        greet(on_x(k))
    for k in (1, 3):
        greet(on_y(k))

    @pl.when(jnp.logical_not(stays))
    def _():
        greet(at(core, z, y_lo, y_hi, x))

    pl.semaphore_wait(barrier, 21 - stays.astype(jnp.int32))

    sent = (sent_0, sent_1)

    def piece(to, e):
        return f_ref.at[:, to % 8, :, pl.ds(pl.multiple_of((to // 8) * 256 + e * 128, 128), 128)]

    def first(e, k):
        to = (col + k) % 16
        return remote(piece(to, e), sent[e].at[pl.ds(col * 7, 7)], one_send.at[e, k], one_recv.at[e, k], (row, to))

    def first_here(e):
        return pltpu.make_async_copy(piece(col, e), sent[e].at[pl.ds(col * 7, 7)], local_sem.at[e])

    for e in range(2):

        @pl.loop(1, 16)
        def _(k):
            first(e, k).start()

        first_here(e).start()

    def k_copy(kind, half):
        rows = pl.ds(half * 224, 224)
        return remote(
            k_ref.at[rows], k_all.at[y, rows], k_send.at[kind, half], k_recv.at[kind, half], on_y(1 if kind == UP else 3)
        )

    def k_pass(kind):
        rows = pl.ds(0, 224) if kind == HALF_UP else pl.ds(224, 224)
        ref = k_all.at[(y + (3 if kind == HALF_UP else 1)) % 4, rows]
        return remote(ref, ref, k_send.at[kind, 0], k_recv.at[kind, 0], on_y(1 if kind == HALF_UP else 3))

    k_copy(UP, 0).start()
    k_copy(DOWN, 1).start()

    def take_k(there, ref):
        k_high[there], k_low[there] = split(ref[...])

    k_here = pltpu.make_async_copy(k_ref, k_all.at[y], local_sem.at[6])
    k_here.start()
    k_here.wait()
    take_k(y, k_all.at[y])

    def second(e, k):
        to = (x + 4 - k) % 4
        i = (k + 3) % 4
        src = picked.at[e, :, pl.ds(to * 14, 14)]
        dst = p_x.at[e, i // 2, i % 2, :, :, z, core]
        if k == 0:
            return pltpu.make_async_copy(src, dst, local_sem.at[2 + e])
        return remote(src, dst, two_send.at[e, k], two_recv.at[e, k], on_x(4 - k))

    def third(e, k):
        to = (place + k) % 8
        src = picked.at[e, :, pl.ds(to * 7, 7)]
        dst = p_z.at[e, x, :, :, place]
        return remote(src, dst, three_send.at[e, k], three_recv.at[e, k], (row, y_hi * 8 + to))

    def third_here(e):
        src = picked.at[e, :, pl.ds(place * 7, 7)]
        return pltpu.make_async_copy(src, p_z.at[e, x, :, :, place], local_sem.at[4 + e])

    stored = [map_ref[t] for t in range(28)]
    inverse = [functools.reduce(jnp.maximum, [jnp.where(stored[t] == j, t, 0) for t in range(1, 28)]) for j in range(28)]

    def third_start(e):
        @pl.loop(1, 8)
        def _(k):
            third(e, k).start()

        third_here(e).start()

    for e in range(2):
        first_here(e).wait()

        @pl.loop(1, 16)
        def _(k):
            first(e, k).wait_recv()

        for j in range(28):
            picked[e, j // 14, (j % 14) * 4 : (j % 14) * 4 + 4] = sent[e][pl.ds(inverse[j] * 4, 4)]
        for k in (1, 2, 3, 0):
            second(e, k).start()
        if e == 0:
            third_start(0)
            k_copy(UP, 1).start()
            k_copy(DOWN, 0).start()

    def z_copy(kind, r):
        def rows(there, chunk=slice(None)):
            return p_x.at[r // 2, r % 2, :, chunk, :, there, core]

        if kind == CORE:
            ref, to = p_x.at[r // 2, r % 2, :, :, :, :, core], other_core
        else:
            ref, to = {
                UP: (rows(z), on_z(1)),
                DOWN: (rows(z), on_z(3)),
                HALF_UP: (rows((z + 3) % 4, 0), on_z(1)),
                HALF_DOWN: (rows((z + 1) % 4, 1), on_z(3)),
            }[kind]
        return remote(ref, ref, z_send.at[kind, r], z_recv.at[kind, r], to)

    def x_copy(kind, e):
        def block(there, half=slice(None)):
            return p_z.at[e, there, half]

        ref, to = {
            UP: (block(x), on_x(1)),
            DOWN: (block(x), on_x(3)),
            HALF_UP: (block((x + 3) % 4, 0), on_x(1)),
            HALF_DOWN: (block((x + 1) % 4, 1), on_x(3)),
        }[kind]
        return remote(ref, ref, x_send.at[kind, e], x_recv.at[kind, e], to)

    def pass_on(copy, r):
        copy(UP, r).wait_recv()
        copy(HALF_UP, r).start()
        copy(DOWN, r).wait_recv()
        copy(HALF_DOWN, r).start()

    def z_start(e):
        for p in range(2):
            z_copy(UP, 2 * e + p).start()
            z_copy(DOWN, 2 * e + p).start()

    def x_start(e):
        x_copy(UP, e).start()
        x_copy(DOWN, e).start()

    def third_done(e):
        third_here(e).wait()

        @pl.loop(1, 8)
        def _(k):
            third(e, k).wait_recv()

    def second_done(e):
        second(e, 0).wait()
        for k in (1, 2, 3):
            second(e, k).wait_recv()

    second_done(0)
    z_start(0)
    third_start(1)
    third_done(0)
    x_start(0)
    second_done(1)
    pass_on(z_copy, 0)
    pass_on(z_copy, 1)
    z_start(1)
    third_done(1)
    x_start(1)

    def core_start(r):
        z_copy(HALF_UP, r).wait_recv()
        z_copy(HALF_DOWN, r).wait_recv()
        z_copy(CORE, r).start()

    pass_on(x_copy, 0)
    core_start(0)
    core_start(1)

    def n_copy(kind, e, side):
        low, high = pl.ds(0, 224), pl.ds(224, 224)
        src, dst = {
            HALF_UP: (n_part.at[e, 1, side, low], n_far.at[0, e, side]),
            HALF_DOWN: (n_part.at[e, 1, side, high], n_far.at[1, e, side]),
            UP: (n_part.at[e, 0, side, low], n_got.at[0, e, side, low]),
            DOWN: (n_part.at[e, 2, side, high], n_got.at[1, e, side, high]),
            FREE_UP: (n_part.at[e, 0, side, high], n_got.at[0, e, side, high]),
            FREE_DOWN: (n_part.at[e, 2, side, low], n_got.at[1, e, side, low]),
        }[kind]
        to = on_x(1 if kind in (UP, HALF_UP, FREE_UP) else 3)
        return remote(src, dst, n_send.at[kind, e, side], n_recv.at[kind, e, side], to)

    def n_far_start(e, side):
        n_copy(HALF_UP, e, side).start()
        n_copy(HALF_DOWN, e, side).start()

    def n_free_start(e, side):
        n_copy(FREE_UP, e, side).start()
        n_copy(FREE_DOWN, e, side).start()

    def n_near_start(e, side):
        n_copy(HALF_UP, e, side).wait_recv()
        n_part[e, 0, side, 0:224] += n_far[0, e, side]
        n_copy(UP, e, side).start()
        n_copy(HALF_DOWN, e, side).wait_recv()
        n_part[e, 2, side, 224:448] += n_far[1, e, side]
        n_copy(DOWN, e, side).start()

    def take_p(r):
        for half in range(2):

            @pl.loop(0, 7)
            def _(k):
                rows = pl.ds(pl.multiple_of(k * 128, 128), 128)
                for i in range(2):
                    columns = slice(i * 128, (i + 1) * 128)
                    p_high[r, half, rows, columns], p_low[r, half, rows, columns] = split(
                        p_x[r // 2, r % 2, i, half, pl.ds(2 * k, 2)].reshape(128, 128)
                    )

    def n_dots(r, side, half, add):
        there = side * 2 + half
        value = three(k_high[there], k_low[there], p_high[r, half], p_low[r, half])

        @pl.when(add)
        def _():
            for i in range(2):
                n_part[r // 2, 2 * (r % 2) + i, side] += value[:, i * 128 : (i + 1) * 128]

        @pl.when(jnp.logical_not(add))
        def _():
            for i in range(2):
                n_part[r // 2, 2 * (r % 2) + i, side] = value[:, i * 128 : (i + 1) * 128]

    def n_first(r):
        z_copy(CORE, r).wait_recv()
        take_p(r)

    theirs = 1 - y_hi

    @pl.loop(0, 2)
    def _(r):
        n_first(r)
        n_dots(r, y_hi, y_lo, r < 0)

    k_copy(UP, 0).wait_recv()
    k_pass(HALF_UP).start()
    k_copy(DOWN, 1).wait_recv()
    k_pass(HALF_DOWN).start()
    pass_on(z_copy, 2)
    pass_on(x_copy, 1)
    k_copy(UP, 1).wait_recv()
    k_copy(DOWN, 0).wait_recv()
    take_k((y + 3) % 4, k_all.at[(y + 3) % 4])
    take_k((y + 1) % 4, k_all.at[(y + 1) % 4])

    def y_copy(kind, e, s):
        there = (y + {UP: 0, DOWN: 0, HALF_UP: 3, HALF_DOWN: 1}[kind]) % 4
        start = ((there // 2 + s) % 2) * 448 + (224 if kind == HALF_DOWN else 0)
        size = 448 if kind in (UP, DOWN) else 224
        ref = n_all.at[e, there, pl.ds(pl.multiple_of(start, 32), size)]
        to = on_y(1 if kind in (UP, HALF_UP) else 3)
        return remote(ref, ref, y_send.at[kind, e, s], y_recv.at[kind, e, s], to)

    def y_start(e, s):
        side = (y_hi + s) % 2
        for kind in (UP, DOWN, FREE_UP, FREE_DOWN):
            n_copy(kind, e, side).wait_recv()
        rows = pl.ds(pl.multiple_of(side * 448, 64), 448)
        n_all[e, y, rows] = -(n_part[e, 3, side] + (n_got[0, e, side] + n_got[1, e, side]))
        y_copy(UP, e, s).start()
        y_copy(DOWN, e, s).start()

    def y_pass(e, s):
        y_copy(UP, e, s).wait_recv()
        y_copy(HALF_UP, e, s).start()
        y_copy(DOWN, e, s).wait_recv()
        y_copy(HALF_DOWN, e, s).start()

    @pl.loop(0, 10)
    def _(q):
        def after(step, action, *args):
            @pl.when(q == step)
            def _():
                action(*args)

        def among(*steps):
            return functools.reduce(jnp.logical_or, [q == step for step in steps])

        after(3, n_first, 2)
        after(6, n_first, 3)
        partners = among(2, 5, 8, 9)
        own_block = among(3, 6)
        add = jnp.logical_not(jnp.logical_or(partners, own_block))
        r = jnp.where(
            partners,
            jnp.where(q == 2, 0, jnp.where(q == 5, 1, q - 6)),
            jnp.where(q < 2, q, jnp.where(q < 5, 2, 3)),
        )
        n_dots(r, jnp.where(partners, theirs, y_hi), jnp.where(own_block, y_lo, 1 - y_lo), add)
        after(0, n_far_start, 0, y_hi)
        after(1, n_free_start, 0, y_hi)
        after(0, pass_on, z_copy, 3)
        after(1, core_start, 2)
        after(3, core_start, 3)
        after(4, n_far_start, 1, y_hi)
        after(5, n_near_start, 0, y_hi)
        after(7, n_free_start, 1, y_hi)
        after(8, n_near_start, 1, y_hi)

    k_pass(HALF_UP).wait_recv()
    k_pass(HALF_DOWN).wait_recv()
    take_k((y + 2) % 4, k_all.at[(y + 2) % 4])

    @pl.loop(0, 4)
    def _(t):
        n_dots(t, theirs, y_lo, t >= 0)

        @pl.when(t == 0)
        def _():
            n_far_start(0, theirs)
            y_start(0, 0)

        @pl.when(t == 1)
        def _():
            n_free_start(0, theirs)

        @pl.when(t == 2)
        def _():
            y_start(1, 0)
            n_near_start(0, theirs)
            n_far_start(1, theirs)

        @pl.when(t == 3)
        def _():
            n_free_start(1, theirs)

    y_pass(0, 0)

    def take_z(e):
        x_copy(HALF_UP, e).wait_recv()
        x_copy(HALF_DOWN, e).wait_recv()

        @pl.loop(0, 4)
        def _(there):
            for half in range(2):
                columns = slice(e * 128, (e + 1) * 128)
                pz_high[there, half, :, columns], pz_low[there, half, :, columns] = split(
                    p_z[e, there, half].reshape(448, 128)
                )

    take_z(0)
    take_z(1)
    y_start(0, 1)
    n_near_start(1, theirs)
    y_pass(1, 0)

    def c_copy(e, k):
        there = (z + k) % 4
        return remote(d_part.at[e, there, 1 - core], d_core.at[e, there], c_send.at[e, k], c_recv.at[e, k], other_core)

    def d_copy(kind, e):
        two, up_, down_ = ((z + k) % 4 for k in (2, 1, 3))
        src, dst = {
            HALF_UP: (d_part.at[e, two, core, 0], d_far.at[0, e]),
            HALF_DOWN: (d_part.at[e, two, core, 1], d_far.at[1, e]),
            UP: (d_part.at[e, up_, core, 0], d_got.at[0, e, 0]),
            DOWN: (d_part.at[e, down_, core, 1], d_got.at[1, e, 1]),
            FREE_UP: (d_part.at[e, up_, core, 1], d_got.at[0, e, 1]),
            FREE_DOWN: (d_part.at[e, down_, core, 0], d_got.at[1, e, 0]),
        }[kind]
        to = on_z(1 if kind in (UP, HALF_UP, FREE_UP) else 3)
        return remote(src, dst, d_send.at[kind, e], d_recv.at[kind, e], to)

    def d_cores(e, k):
        there = (z + k) % 4
        c_copy(e, k).wait_recv()
        d_part[e, there, core] += d_core[e, there]

    def d_far_start(e):
        d_cores(e, 2)
        d_copy(HALF_UP, e).start()
        d_copy(HALF_DOWN, e).start()

    def d_near_start(e):
        d_copy(HALF_UP, e).wait_recv()
        d_part[e, (z + 1) % 4, core, 0] += d_far[0, e]
        d_copy(UP, e).start()
        d_copy(HALF_DOWN, e).wait_recv()
        d_part[e, (z + 3) % 4, core, 1] += d_far[1, e]
        d_copy(DOWN, e).start()

    def n_out(e, half):
        src = n_all.at[e, half * 2 + y_lo, pl.ds(pl.multiple_of(y_hi * 448, 64), 448)]
        columns = pl.ds(pl.multiple_of(half * 256 + e * 128, 128), 128)
        return pltpu.make_async_copy(src, n_ref.at[:, columns], out_sem.at[e, half])

    def d_rows(e, s):
        for kind in (HALF_UP, HALF_DOWN):
            y_copy(kind, e, s).wait_recv()
        for high in range(2):
            for low in range(2):
                lines = slice(low * 128, (low + 1) * 128)
                for first_row, size in ((0, 128), (128, 128), (256, 128), (384, 64)):
                    start = (high + s) % 2 * 448 + first_row
                    value = n_all[e, 2 * high + low, start : start + size].T
                    columns = slice(first_row, first_row + size)
                    t_high[high, lines, columns], t_low[high, lines, columns] = split(value)

    def d_dots(s, there, high):
        side = (high + s) % 2
        return three(t_high[high], t_low[high], pz_high[there, side], pz_low[there, side])

    def d_early(e):
        d_rows(e, 0)

        @pl.loop(0, 8)
        def _(q):
            there, high = q // 2, q % 2
            d_part[e, there, :, high] = d_dots(0, there, high).reshape(2, 128, 256)

    def d_late(e):
        d_rows(e, 1)
        for half in range(2):
            n_out(e, half).start()

        @pl.loop(0, 4)
        def _(j):
            k = jnp.where(j == 0, 2, jnp.where(j == 1, 1, jnp.where(j == 2, 3, 0)))
            there = (z + k) % 4

            @pl.loop(0, 2)
            def _(high):
                d_part[e, there, :, high] += d_dots(1, there, high).reshape(2, 128, 256)

            c_copy(e, k).start()

            @pl.when(j == 2)
            def _():
                d_far_start(e)

            @pl.when(j == 3)
            def _():
                d_cores(e, 1)
                d_copy(FREE_UP, e).start()
                if e == 0:
                    y_pass(1, 1)

        d_cores(e, 3)
        d_copy(FREE_DOWN, e).start()
        d_cores(e, 0)

    d_early(0)
    y_pass(0, 1)
    y_start(1, 1)
    d_early(1)
    d_late(0)
    d_near_start(0)
    d_late(1)

    def o_copy(e):
        return remote(d_sum.at[e], d_ref.at[:, e], o_send.at[e], o_recv.at[e], at(y_lo, z, y_hi, core, x))

    def o_here(e):
        return pltpu.make_async_copy(d_sum.at[e], d_ref.at[:, e], o_recv.at[e])

    def o_start(e):
        for kind in (UP, DOWN, FREE_UP, FREE_DOWN):
            d_copy(kind, e).wait_recv()
        d_sum[e] = d_part[e, z, core] + (d_got[0, e] + d_got[1, e])

        @pl.when(stays)
        def _():
            o_here(e).start()

        @pl.when(jnp.logical_not(stays))
        def _():
            o_copy(e).start()

    o_start(0)
    d_near_start(1)
    o_start(1)

    for e in range(2):

        @pl.loop(1, 16)
        def _(k):
            first(e, k).wait_send()

        @pl.loop(1, 8)
        def _(k):
            third(e, k).wait_send()

        for k in (1, 2, 3):
            second(e, k).wait_send()
        for kind in range(4):
            x_copy(kind, e).wait_send()
            c_copy(e, kind).wait_send()
            for side in range(2):
                y_copy(kind, e, side).wait_send()
        for kind in range(6):
            d_copy(kind, e).wait_send()
            for side in range(2):
                n_copy(kind, e, side).wait_send()

        @pl.when(jnp.logical_not(stays))
        def _():
            o_copy(e).wait_send()

    for half in range(2):
        k_copy(UP, half).wait_send()
        k_copy(DOWN, half).wait_send()
    k_pass(HALF_UP).wait_send()
    k_pass(HALF_DOWN).wait_send()

    @pl.loop(0, 4)
    def _(r):
        for kind in range(5):
            z_copy(kind, r).wait_send()

    for e in range(2):
        for half in range(2):
            n_out(e, half).wait()
        o_here(e).wait()


def on_device(known_inverse, factor_panel, diag_base, ancestor_map):
    whole = pl.BlockSpec(memory_space=pl.ANY)
    dma = pltpu.SemaphoreType.DMA
    new_column, reduced = pl.pallas_call(
        kernel,
        out_shape=(jax.ShapeDtypeStruct((448, 512), F32), jax.ShapeDtypeStruct((2, 2, 128, 256), F32)),
        in_specs=[pl.BlockSpec(memory_space=pltpu.SMEM), whole, whole],
        out_specs=(whole, whole),
        scratch_shapes=[
            pltpu.VMEM((4, 448, 896), F32),
            pltpu.VMEM((4, 448, 896), BF),
            pltpu.VMEM((4, 448, 896), BF),
            pltpu.VMEM((112, 8, 128), F32),
            pltpu.VMEM((112, 8, 128), F32),
            pltpu.VMEM((2, 2, 56, 8, 128), F32),
            pltpu.VMEM((2, 2, 2, 2, 14, 4, 2, 8, 128), F32),
            pltpu.VMEM((4, 2, 896, 256), BF),
            pltpu.VMEM((4, 2, 896, 256), BF),
            pltpu.VMEM((2, 4, 2, 7, 8, 8, 128), F32),
            pltpu.VMEM((4, 2, 448, 256), BF),
            pltpu.VMEM((4, 2, 448, 256), BF),
            pltpu.VMEM((2, 4, 2, 448, 128), F32),
            pltpu.VMEM((2, 2, 2, 224, 128), F32),
            pltpu.VMEM((2, 2, 2, 448, 128), F32),
            pltpu.VMEM((2, 4, 896, 128), F32),
            pltpu.VMEM((2, 256, 448), BF),
            pltpu.VMEM((2, 256, 448), BF),
            pltpu.VMEM((2, 4, 2, 2, 128, 256), F32),
            pltpu.VMEM((2, 4, 2, 128, 256), F32),
            pltpu.VMEM((2, 2, 128, 256), F32),
            pltpu.VMEM((2, 2, 2, 128, 256), F32),
            pltpu.VMEM((2, 2, 128, 256), F32),
            dma((2, 16)), dma((2, 16)), dma((2, 4)), dma((2, 4)), dma((2, 8)), dma((2, 8)), dma((7,)), dma((4, 2)), dma((4, 2)),
            dma((5, 4)), dma((5, 4)), dma((4, 2)), dma((4, 2)), dma((6, 2, 2)), dma((6, 2, 2)), dma((4, 2, 2)), dma((4, 2, 2)),
            dma((2, 4)), dma((2, 4)), dma((6, 2)), dma((6, 2)), dma((2, 2)), dma((2,)), dma((2,)),
        ],
        compiler_params=pltpu.CompilerParams(collective_id=0, has_side_effects=True, vmem_limit_bytes=60 << 20),
        cost_estimate=pl.CostEstimate(
            flops=6 * (448 * 1792 * 2048 + 256 * 1792 * 2048), bytes_accessed=4 << 20, transcendentals=0
        ),
        name="selected_inverse",
    )(ancestor_map, known_inverse, factor_panel.reshape(7, 8, 8, 512))
    return (new_column, diag_base - reduced.reshape(512, 256))


def solution(mesh):
    placed = (P("col", "row"), P("col", "row"), P("row", "col"), P())
    return jax.shard_map(
        on_device,
        mesh=mesh,
        in_specs=placed,
        out_specs=(P("col", "row"), P("row", "col")),
        check_vma=False,
    )
```

```python
import functools

import jax
import jax.numpy as jnp
from jax import lax
from jax.experimental import pallas as pl
from jax.experimental.pallas import tpu as pltpu
from jax.sharding import PartitionSpec as P

MESH = pl.DeviceIdType.MESH
BF = jnp.bfloat16
F32 = jnp.float32

UP, DOWN, HALF_UP, HALF_DOWN, CORE = range(5)
FREE_UP, FREE_DOWN = 4, 5


def split(value):
    high = value.astype(BF)
    return high, (value - high.astype(F32)).astype(BF)


def three(a_high, a_low, b_high, b_low):
    def dot(a, b):
        return jnp.dot(a, b, preferred_element_type=F32)

    return dot(a_high, b_high) + (dot(a_high, b_low) + dot(a_low, b_high))


def kernel(
    map_ref, k_ref, f_ref, n_ref, d_ref,
    k_all, k_high, k_low, sent_0, sent_1, picked, p_x, p_high, p_low, p_z, pz_high, pz_low,
    n_part, n_far, n_got, n_all, t_high, t_low, d_part, d_core, d_far, d_got, d_sum,
    one_send, one_recv, two_send, two_recv, three_send, three_recv, local_sem, k_send, k_recv,
    z_send, z_recv, x_send, x_recv, n_send, n_recv, y_send, y_recv,
    c_send, c_recv, d_send, d_recv, out_sem, o_send, o_recv,
):
    row, col = lax.axis_index("row"), lax.axis_index("col")
    x, y_lo = row % 4, row // 4
    core, z, y_hi = col % 2, (col // 2) % 4, col // 8
    y, place = y_hi * 2 + y_lo, col % 8

    def at(y_hi_, z_, core_, y_lo_, x_):
        return (y_lo_ * 4 + x_, y_hi_ * 8 + z_ * 2 + core_)

    def on_x(k):
        return (y_lo * 4 + (x + k) % 4, col)

    def on_y(k):
        there = (y + k) % 4
        return at(there // 2, z, core, there % 2, x)

    def on_z(k):
        return (row, y_hi * 8 + ((z + k) % 4) * 2 + core)

    other_core = (row, y_hi * 8 + z * 2 + 1 - core)
    stays = jnp.logical_and(y_hi == y_lo, y_hi == core)

    def remote(src, dst, send, recv, device):
        return pltpu.make_async_remote_copy(
            src_ref=src, dst_ref=dst, send_sem=send, recv_sem=recv, device_id=device, device_id_type=MESH
        )

    barrier = pltpu.get_barrier_semaphore()

    def greet(device):
        pl.semaphore_signal(barrier, inc=1, device_id=device, device_id_type=MESH)

    @pl.loop(1, 16)
    def _(k):
        greet((row, (col + k) % 16))

    for k in (1, 2, 3):
        greet(on_x(k))
    for k in (1, 3):
        greet(on_y(k))

    @pl.when(jnp.logical_not(stays))
    def _():
        greet(at(core, z, y_lo, y_hi, x))

    pl.semaphore_wait(barrier, 21 - stays.astype(jnp.int32))

    sent = (sent_0, sent_1)

    def piece(to, e):
        return f_ref.at[:, to % 8, :, pl.ds(pl.multiple_of((to // 8) * 256 + e * 128, 128), 128)]

    def first(e, k):
        to = (col + k) % 16
        return remote(piece(to, e), sent[e].at[pl.ds(col * 7, 7)], one_send.at[e, k], one_recv.at[e, k], (row, to))

    def first_here(e):
        return pltpu.make_async_copy(piece(col, e), sent[e].at[pl.ds(col * 7, 7)], local_sem.at[e])

    for e in range(2):

        @pl.loop(1, 16)
        def _(k):
            first(e, k).start()

        first_here(e).start()

    def k_copy(kind, half):
        rows = pl.ds(half * 224, 224)
        return remote(
            k_ref.at[rows], k_all.at[y, rows], k_send.at[kind, half], k_recv.at[kind, half], on_y(1 if kind == UP else 3)
        )

    def k_pass(kind):
        rows = pl.ds(0, 224) if kind == HALF_UP else pl.ds(224, 224)
        ref = k_all.at[(y + (3 if kind == HALF_UP else 1)) % 4, rows]
        return remote(ref, ref, k_send.at[kind, 0], k_recv.at[kind, 0], on_y(1 if kind == HALF_UP else 3))

    k_copy(UP, 0).start()
    k_copy(DOWN, 1).start()

    def take_k(there, ref):
        k_high[there], k_low[there] = split(ref[...])

    k_here = pltpu.make_async_copy(k_ref, k_all.at[y], local_sem.at[6])
    k_here.start()
    k_here.wait()
    take_k(y, k_all.at[y])

    def second(e, k):
        to = (x + 4 - k) % 4
        i = (k + 3) % 4
        src = picked.at[e, :, pl.ds(to * 14, 14)]
        dst = p_x.at[e, i // 2, i % 2, :, :, z, core]
        if k == 0:
            return pltpu.make_async_copy(src, dst, local_sem.at[2 + e])
        return remote(src, dst, two_send.at[e, k], two_recv.at[e, k], on_x(4 - k))

    def third(e, k):
        to = (place + k) % 8
        src = picked.at[e, :, pl.ds(to * 7, 7)]
        dst = p_z.at[e, x, :, :, place]
        return remote(src, dst, three_send.at[e, k], three_recv.at[e, k], (row, y_hi * 8 + to))

    def third_here(e):
        src = picked.at[e, :, pl.ds(place * 7, 7)]
        return pltpu.make_async_copy(src, p_z.at[e, x, :, :, place], local_sem.at[4 + e])

    stored = [map_ref[t] for t in range(28)]
    inverse = [functools.reduce(jnp.maximum, [jnp.where(stored[t] == j, t, 0) for t in range(1, 28)]) for j in range(28)]

    def third_start(e):
        @pl.loop(1, 8)
        def _(k):
            third(e, k).start()

        third_here(e).start()

    for e in range(2):
        first_here(e).wait()

        @pl.loop(1, 16)
        def _(k):
            first(e, k).wait_recv()

        for j in range(28):
            picked[e, j // 14, (j % 14) * 4 : (j % 14) * 4 + 4] = sent[e][pl.ds(inverse[j] * 4, 4)]
        for k in (1, 2, 3, 0):
            second(e, k).start()
        third_start(e)
        if e == 0:
            k_copy(UP, 1).start()
            k_copy(DOWN, 0).start()

    def z_copy(kind, r):
        def rows(there, chunk=slice(None)):
            return p_x.at[r // 2, r % 2, :, chunk, :, there, core]

        if kind == CORE:
            ref, to = p_x.at[r // 2, r % 2, :, :, :, :, core], other_core
        else:
            ref, to = {
                UP: (rows(z), on_z(1)),
                DOWN: (rows(z), on_z(3)),
                HALF_UP: (rows((z + 3) % 4, 0), on_z(1)),
                HALF_DOWN: (rows((z + 1) % 4, 1), on_z(3)),
            }[kind]
        return remote(ref, ref, z_send.at[kind, r], z_recv.at[kind, r], to)

    def x_copy(kind, e):
        def block(there, half=slice(None)):
            return p_z.at[e, there, half]

        ref, to = {
            UP: (block(x), on_x(1)),
            DOWN: (block(x), on_x(3)),
            HALF_UP: (block((x + 3) % 4, 0), on_x(1)),
            HALF_DOWN: (block((x + 1) % 4, 1), on_x(3)),
        }[kind]
        return remote(ref, ref, x_send.at[kind, e], x_recv.at[kind, e], to)

    def pass_on(copy, r):
        copy(UP, r).wait_recv()
        copy(HALF_UP, r).start()
        copy(DOWN, r).wait_recv()
        copy(HALF_DOWN, r).start()

    def z_start(e):
        for p in range(2):
            z_copy(UP, 2 * e + p).start()
            z_copy(DOWN, 2 * e + p).start()

    def x_start(e):
        x_copy(UP, e).start()
        x_copy(DOWN, e).start()

    def third_done(e):
        third_here(e).wait()

        @pl.loop(1, 8)
        def _(k):
            third(e, k).wait_recv()

    def second_done(e):
        second(e, 0).wait()
        for k in (1, 2, 3):
            second(e, k).wait_recv()

    second_done(0)
    z_start(0)
    third_done(0)
    x_start(0)
    second_done(1)
    third_done(1)
    x_start(1)
    pass_on(z_copy, 0)
    pass_on(x_copy, 0)
    pass_on(z_copy, 1)
    z_start(1)

    def core_start(r):
        z_copy(HALF_UP, r).wait_recv()
        z_copy(HALF_DOWN, r).wait_recv()
        z_copy(CORE, r).start()

    core_start(0)
    core_start(1)
    pass_on(x_copy, 1)

    def n_copy(kind, e, side):
        low, high = pl.ds(0, 224), pl.ds(224, 224)
        src, dst = {
            HALF_UP: (n_part.at[e, 1, side, low], n_far.at[0, e, side]),
            HALF_DOWN: (n_part.at[e, 1, side, high], n_far.at[1, e, side]),
            UP: (n_part.at[e, 0, side, low], n_got.at[0, e, side, low]),
            DOWN: (n_part.at[e, 2, side, high], n_got.at[1, e, side, high]),
            FREE_UP: (n_part.at[e, 0, side, high], n_got.at[0, e, side, high]),
            FREE_DOWN: (n_part.at[e, 2, side, low], n_got.at[1, e, side, low]),
        }[kind]
        to = on_x(1 if kind in (UP, HALF_UP, FREE_UP) else 3)
        return remote(src, dst, n_send.at[kind, e, side], n_recv.at[kind, e, side], to)

    def n_far_start(e, side):
        n_copy(HALF_UP, e, side).start()
        n_copy(HALF_DOWN, e, side).start()

    def n_free_start(e, side):
        n_copy(FREE_UP, e, side).start()
        n_copy(FREE_DOWN, e, side).start()

    def n_near_start(e, side):
        n_copy(HALF_UP, e, side).wait_recv()
        n_part[e, 0, side, 0:224] += n_far[0, e, side]
        n_copy(UP, e, side).start()
        n_copy(HALF_DOWN, e, side).wait_recv()
        n_part[e, 2, side, 224:448] += n_far[1, e, side]
        n_copy(DOWN, e, side).start()

    def take_p(r):
        for half in range(2):

            @pl.loop(0, 7)
            def _(k):
                rows = pl.ds(pl.multiple_of(k * 128, 128), 128)
                for i in range(2):
                    columns = slice(i * 128, (i + 1) * 128)
                    p_high[r, half, rows, columns], p_low[r, half, rows, columns] = split(
                        p_x[r // 2, r % 2, i, half, pl.ds(2 * k, 2)].reshape(128, 128)
                    )

    def n_dots(r, side, half, add):
        there = side * 2 + half
        value = three(k_high[there], k_low[there], p_high[r, half], p_low[r, half])

        @pl.when(add)
        def _():
            for i in range(2):
                n_part[r // 2, 2 * (r % 2) + i, side] += value[:, i * 128 : (i + 1) * 128]

        @pl.when(jnp.logical_not(add))
        def _():
            for i in range(2):
                n_part[r // 2, 2 * (r % 2) + i, side] = value[:, i * 128 : (i + 1) * 128]

    def n_first(r):
        z_copy(CORE, r).wait_recv()
        take_p(r)

    theirs = 1 - y_hi

    @pl.loop(0, 2)
    def _(r):
        n_first(r)
        n_dots(r, y_hi, y_lo, r < 0)

    k_copy(UP, 0).wait_recv()
    k_pass(HALF_UP).start()
    k_copy(DOWN, 1).wait_recv()
    k_pass(HALF_DOWN).start()
    pass_on(z_copy, 2)
    k_copy(UP, 1).wait_recv()
    k_copy(DOWN, 0).wait_recv()
    take_k((y + 3) % 4, k_all.at[(y + 3) % 4])
    take_k((y + 1) % 4, k_all.at[(y + 1) % 4])

    def y_copy(kind, e, s):
        there = (y + {UP: 0, DOWN: 0, HALF_UP: 3, HALF_DOWN: 1}[kind]) % 4
        start = ((there // 2 + s) % 2) * 448 + (224 if kind == HALF_DOWN else 0)
        size = 448 if kind in (UP, DOWN) else 224
        ref = n_all.at[e, there, pl.ds(pl.multiple_of(start, 32), size)]
        to = on_y(1 if kind in (UP, HALF_UP) else 3)
        return remote(ref, ref, y_send.at[kind, e, s], y_recv.at[kind, e, s], to)

    def y_start(e, s):
        side = (y_hi + s) % 2
        for kind in (UP, DOWN, FREE_UP, FREE_DOWN):
            n_copy(kind, e, side).wait_recv()
        rows = pl.ds(pl.multiple_of(side * 448, 64), 448)
        n_all[e, y, rows] = -(n_part[e, 3, side] + (n_got[0, e, side] + n_got[1, e, side]))
        y_copy(UP, e, s).start()
        y_copy(DOWN, e, s).start()

    def y_pass(e, s):
        y_copy(UP, e, s).wait_recv()
        y_copy(HALF_UP, e, s).start()
        y_copy(DOWN, e, s).wait_recv()
        y_copy(HALF_DOWN, e, s).start()

    @pl.loop(0, 10)
    def _(q):
        def after(step, action, *args):
            @pl.when(q == step)
            def _():
                action(*args)

        def among(*steps):
            return functools.reduce(jnp.logical_or, [q == step for step in steps])

        after(3, n_first, 2)
        after(6, n_first, 3)
        partners = among(2, 5, 8, 9)
        own_block = among(3, 6)
        add = jnp.logical_not(jnp.logical_or(partners, own_block))
        r = jnp.where(
            partners,
            jnp.where(q == 2, 0, jnp.where(q == 5, 1, q - 6)),
            jnp.where(q < 2, q, jnp.where(q < 5, 2, 3)),
        )
        n_dots(r, jnp.where(partners, theirs, y_hi), jnp.where(own_block, y_lo, 1 - y_lo), add)
        after(0, n_far_start, 0, y_hi)
        after(1, n_free_start, 0, y_hi)
        after(0, pass_on, z_copy, 3)
        after(1, core_start, 2)
        after(3, core_start, 3)
        after(4, n_far_start, 1, y_hi)
        after(5, n_near_start, 0, y_hi)
        after(7, n_free_start, 1, y_hi)
        after(8, n_near_start, 1, y_hi)

    k_pass(HALF_UP).wait_recv()
    k_pass(HALF_DOWN).wait_recv()
    take_k((y + 2) % 4, k_all.at[(y + 2) % 4])

    @pl.loop(0, 4)
    def _(t):
        n_dots(t, theirs, y_lo, t >= 0)

        @pl.when(t == 0)
        def _():
            n_far_start(0, theirs)
            y_start(0, 0)

        @pl.when(t == 1)
        def _():
            n_free_start(0, theirs)

        @pl.when(t == 2)
        def _():
            y_start(1, 0)
            n_near_start(0, theirs)
            n_far_start(1, theirs)

        @pl.when(t == 3)
        def _():
            n_free_start(1, theirs)

    y_pass(0, 0)

    def take_z(e):
        x_copy(HALF_UP, e).wait_recv()
        x_copy(HALF_DOWN, e).wait_recv()

        @pl.loop(0, 4)
        def _(there):
            for half in range(2):
                columns = slice(e * 128, (e + 1) * 128)
                pz_high[there, half, :, columns], pz_low[there, half, :, columns] = split(
                    p_z[e, there, half].reshape(448, 128)
                )

    take_z(0)
    take_z(1)
    y_start(0, 1)
    n_near_start(1, theirs)
    y_pass(1, 0)

    def c_copy(e, k):
        there = (z + k) % 4
        return remote(d_part.at[e, there, 1 - core], d_core.at[e, there], c_send.at[e, k], c_recv.at[e, k], other_core)

    def d_copy(kind, e):
        two, up_, down_ = ((z + k) % 4 for k in (2, 1, 3))
        src, dst = {
            HALF_UP: (d_part.at[e, two, core, 0], d_far.at[0, e]),
            HALF_DOWN: (d_part.at[e, two, core, 1], d_far.at[1, e]),
            UP: (d_part.at[e, up_, core, 0], d_got.at[0, e, 0]),
            DOWN: (d_part.at[e, down_, core, 1], d_got.at[1, e, 1]),
            FREE_UP: (d_part.at[e, up_, core, 1], d_got.at[0, e, 1]),
            FREE_DOWN: (d_part.at[e, down_, core, 0], d_got.at[1, e, 0]),
        }[kind]
        to = on_z(1 if kind in (UP, HALF_UP, FREE_UP) else 3)
        return remote(src, dst, d_send.at[kind, e], d_recv.at[kind, e], to)

    def d_cores(e, k):
        there = (z + k) % 4
        c_copy(e, k).wait_recv()
        d_part[e, there, core] += d_core[e, there]

    def d_far_start(e):
        d_cores(e, 2)
        d_copy(HALF_UP, e).start()
        d_copy(HALF_DOWN, e).start()

    def d_near_start(e):
        d_copy(HALF_UP, e).wait_recv()
        d_part[e, (z + 1) % 4, core, 0] += d_far[0, e]
        d_copy(UP, e).start()
        d_copy(HALF_DOWN, e).wait_recv()
        d_part[e, (z + 3) % 4, core, 1] += d_far[1, e]
        d_copy(DOWN, e).start()

    def n_out(e, half):
        src = n_all.at[e, half * 2 + y_lo, pl.ds(pl.multiple_of(y_hi * 448, 64), 448)]
        columns = pl.ds(pl.multiple_of(half * 256 + e * 128, 128), 128)
        return pltpu.make_async_copy(src, n_ref.at[:, columns], out_sem.at[e, half])

    def d_rows(e, s):
        for kind in (HALF_UP, HALF_DOWN):
            y_copy(kind, e, s).wait_recv()
        for high in range(2):
            for low in range(2):
                lines = slice(low * 128, (low + 1) * 128)
                for first_row, size in ((0, 128), (128, 128), (256, 128), (384, 64)):
                    start = (high + s) % 2 * 448 + first_row
                    value = n_all[e, 2 * high + low, start : start + size].T
                    columns = slice(first_row, first_row + size)
                    t_high[high, lines, columns], t_low[high, lines, columns] = split(value)

    def d_dots(s, there, high):
        side = (high + s) % 2
        return three(t_high[high], t_low[high], pz_high[there, side], pz_low[there, side])

    def d_early(e):
        d_rows(e, 0)

        @pl.loop(0, 8)
        def _(q):
            there, high = q // 2, q % 2
            d_part[e, there, :, high] = d_dots(0, there, high).reshape(2, 128, 256)

    def d_late(e):
        d_rows(e, 1)
        for half in range(2):
            n_out(e, half).start()

        @pl.loop(0, 4)
        def _(j):
            k = jnp.where(j == 0, 2, jnp.where(j == 1, 1, jnp.where(j == 2, 3, 0)))
            there = (z + k) % 4

            @pl.loop(0, 2)
            def _(high):
                d_part[e, there, :, high] += d_dots(1, there, high).reshape(2, 128, 256)

            c_copy(e, k).start()

            @pl.when(j == 2)
            def _():
                d_far_start(e)

            @pl.when(j == 3)
            def _():
                d_cores(e, 1)
                d_copy(FREE_UP, e).start()
                if e == 0:
                    y_pass(1, 1)

        d_cores(e, 3)
        d_copy(FREE_DOWN, e).start()
        d_cores(e, 0)

    d_early(0)
    y_pass(0, 1)
    y_start(1, 1)
    d_early(1)
    d_late(0)
    d_near_start(0)
    d_late(1)

    def o_copy(e):
        return remote(d_sum.at[e], d_ref.at[:, e], o_send.at[e], o_recv.at[e], at(y_lo, z, y_hi, core, x))

    def o_here(e):
        return pltpu.make_async_copy(d_sum.at[e], d_ref.at[:, e], o_recv.at[e])

    def o_start(e):
        for kind in (UP, DOWN, FREE_UP, FREE_DOWN):
            d_copy(kind, e).wait_recv()
        d_sum[e] = d_part[e, z, core] + (d_got[0, e] + d_got[1, e])

        @pl.when(stays)
        def _():
            o_here(e).start()

        @pl.when(jnp.logical_not(stays))
        def _():
            o_copy(e).start()

    d_near_start(1)
    o_start(0)
    o_start(1)

    for e in range(2):

        @pl.loop(1, 16)
        def _(k):
            first(e, k).wait_send()

        @pl.loop(1, 8)
        def _(k):
            third(e, k).wait_send()

        for k in (1, 2, 3):
            second(e, k).wait_send()
        for kind in range(4):
            x_copy(kind, e).wait_send()
            c_copy(e, kind).wait_send()
            for side in range(2):
                y_copy(kind, e, side).wait_send()
        for kind in range(6):
            d_copy(kind, e).wait_send()
            for side in range(2):
                n_copy(kind, e, side).wait_send()

        @pl.when(jnp.logical_not(stays))
        def _():
            o_copy(e).wait_send()

    for half in range(2):
        k_copy(UP, half).wait_send()
        k_copy(DOWN, half).wait_send()
    k_pass(HALF_UP).wait_send()
    k_pass(HALF_DOWN).wait_send()

    @pl.loop(0, 4)
    def _(r):
        for kind in range(5):
            z_copy(kind, r).wait_send()

    for e in range(2):
        for half in range(2):
            n_out(e, half).wait()
        o_here(e).wait()


def on_device(known_inverse, factor_panel, diag_base, ancestor_map):
    whole = pl.BlockSpec(memory_space=pl.ANY)
    dma = pltpu.SemaphoreType.DMA
    new_column, reduced = pl.pallas_call(
        kernel,
        out_shape=(jax.ShapeDtypeStruct((448, 512), F32), jax.ShapeDtypeStruct((2, 2, 128, 256), F32)),
        in_specs=[pl.BlockSpec(memory_space=pltpu.SMEM), whole, whole],
        out_specs=(whole, whole),
        scratch_shapes=[
            pltpu.VMEM((4, 448, 896), F32),
            pltpu.VMEM((4, 448, 896), BF),
            pltpu.VMEM((4, 448, 896), BF),
            pltpu.VMEM((112, 8, 128), F32),
            pltpu.VMEM((112, 8, 128), F32),
            pltpu.VMEM((2, 2, 56, 8, 128), F32),
            pltpu.VMEM((2, 2, 2, 2, 14, 4, 2, 8, 128), F32),
            pltpu.VMEM((4, 2, 896, 256), BF),
            pltpu.VMEM((4, 2, 896, 256), BF),
            pltpu.VMEM((2, 4, 2, 7, 8, 8, 128), F32),
            pltpu.VMEM((4, 2, 448, 256), BF),
            pltpu.VMEM((4, 2, 448, 256), BF),
            pltpu.VMEM((2, 4, 2, 448, 128), F32),
            pltpu.VMEM((2, 2, 2, 224, 128), F32),
            pltpu.VMEM((2, 2, 2, 448, 128), F32),
            pltpu.VMEM((2, 4, 896, 128), F32),
            pltpu.VMEM((2, 256, 448), BF),
            pltpu.VMEM((2, 256, 448), BF),
            pltpu.VMEM((2, 4, 2, 2, 128, 256), F32),
            pltpu.VMEM((2, 4, 2, 128, 256), F32),
            pltpu.VMEM((2, 2, 128, 256), F32),
            pltpu.VMEM((2, 2, 2, 128, 256), F32),
            pltpu.VMEM((2, 2, 128, 256), F32),
            dma((2, 16)), dma((2, 16)), dma((2, 4)), dma((2, 4)), dma((2, 8)), dma((2, 8)), dma((7,)), dma((4, 2)), dma((4, 2)),
            dma((5, 4)), dma((5, 4)), dma((4, 2)), dma((4, 2)), dma((6, 2, 2)), dma((6, 2, 2)), dma((4, 2, 2)), dma((4, 2, 2)),
            dma((2, 4)), dma((2, 4)), dma((6, 2)), dma((6, 2)), dma((2, 2)), dma((2,)), dma((2,)),
        ],
        compiler_params=pltpu.CompilerParams(collective_id=0, has_side_effects=True, vmem_limit_bytes=60 << 20),
        cost_estimate=pl.CostEstimate(
            flops=6 * (448 * 1792 * 2048 + 256 * 1792 * 2048), bytes_accessed=4 << 20, transcendentals=0
        ),
        name="selected_inverse",
    )(ancestor_map, known_inverse, factor_panel.reshape(7, 8, 8, 512))
    return (new_column, diag_base - reduced.reshape(512, 256))


def solution(mesh):
    placed = (P("col", "row"), P("col", "row"), P("row", "col"), P())
    return jax.shard_map(
        on_device,
        mesh=mesh,
        in_specs=placed,
        out_specs=(P("col", "row"), P("row", "col")),
        check_vma=False,
    )
```

```python
import functools

import jax
import jax.numpy as jnp
from jax import lax
from jax.experimental import pallas as pl
from jax.experimental.pallas import tpu as pltpu
from jax.sharding import PartitionSpec as P

MESH = pl.DeviceIdType.MESH
BF = jnp.bfloat16
F32 = jnp.float32

UP, DOWN, HALF_UP, HALF_DOWN, CORE = range(5)
FREE_UP, FREE_DOWN = 4, 5


def split(value):
    high = value.astype(BF)
    return high, (value - high.astype(F32)).astype(BF)


def three(a_high, a_low, b_high, b_low):
    def dot(a, b):
        return jnp.dot(a, b, preferred_element_type=F32)

    return dot(a_high, b_high) + (dot(a_high, b_low) + dot(a_low, b_high))


def kernel(
    map_ref, k_ref, f_ref, n_ref, d_ref,
    k_all, k_high, k_low, sent_0, sent_1, picked, p_x, p_high, p_low, p_z, pz_high, pz_low,
    n_part, n_far, n_got, n_all, t_high, t_low, d_part, d_core, d_far, d_got, d_sum,
    one_send, one_recv, two_send, two_recv, three_send, three_recv, local_sem, k_send, k_recv,
    z_send, z_recv, x_send, x_recv, n_send, n_recv, y_send, y_recv,
    c_send, c_recv, d_send, d_recv, out_sem, o_send, o_recv,
):
    row, col = lax.axis_index("row"), lax.axis_index("col")
    x, y_lo = row % 4, row // 4
    core, z, y_hi = col % 2, (col // 2) % 4, col // 8
    y, place = y_hi * 2 + y_lo, col % 8

    def at(y_hi_, z_, core_, y_lo_, x_):
        return (y_lo_ * 4 + x_, y_hi_ * 8 + z_ * 2 + core_)

    def on_x(k):
        return (y_lo * 4 + (x + k) % 4, col)

    def on_y(k):
        there = (y + k) % 4
        return at(there // 2, z, core, there % 2, x)

    def on_z(k):
        return (row, y_hi * 8 + ((z + k) % 4) * 2 + core)

    other_core = (row, y_hi * 8 + z * 2 + 1 - core)
    stays = jnp.logical_and(y_hi == y_lo, y_hi == core)

    def remote(src, dst, send, recv, device):
        return pltpu.make_async_remote_copy(
            src_ref=src, dst_ref=dst, send_sem=send, recv_sem=recv, device_id=device, device_id_type=MESH
        )

    barrier = pltpu.get_barrier_semaphore()

    def greet(device):
        pl.semaphore_signal(barrier, inc=1, device_id=device, device_id_type=MESH)

    @pl.loop(1, 16)
    def _(k):
        greet((row, (col + k) % 16))

    for k in (1, 2, 3):
        greet(on_x(k))
    for k in (1, 3):
        greet(on_y(k))

    @pl.when(jnp.logical_not(stays))
    def _():
        greet(at(core, z, y_lo, y_hi, x))

    pl.semaphore_wait(barrier, 21 - stays.astype(jnp.int32))

    sent = (sent_0, sent_1)

    def piece(to, e):
        return f_ref.at[:, to % 8, :, pl.ds(pl.multiple_of((to // 8) * 256 + e * 128, 128), 128)]

    def first(e, k):
        to = (col + k) % 16
        return remote(piece(to, e), sent[e].at[pl.ds(col * 7, 7)], one_send.at[e, k], one_recv.at[e, k], (row, to))

    def first_here(e):
        return pltpu.make_async_copy(piece(col, e), sent[e].at[pl.ds(col * 7, 7)], local_sem.at[e])

    def k_copy(kind, half):
        rows = pl.ds(half * 224, 224)
        return remote(
            k_ref.at[rows], k_all.at[y, rows], k_send.at[kind, half], k_recv.at[kind, half], on_y(1 if kind == UP else 3)
        )

    def k_pass(kind):
        rows = pl.ds(0, 224) if kind == HALF_UP else pl.ds(224, 224)
        ref = k_all.at[(y + (3 if kind == HALF_UP else 1)) % 4, rows]
        return remote(ref, ref, k_send.at[kind, 0], k_recv.at[kind, 0], on_y(1 if kind == HALF_UP else 3))

    k_copy(UP, 0).start()
    k_copy(DOWN, 1).start()

    for e in range(2):

        @pl.loop(1, 16)
        def _(k):
            first(e, k).start()

        first_here(e).start()

    def take_k(there, ref):
        k_high[there], k_low[there] = split(ref[...])

    k_here = pltpu.make_async_copy(k_ref, k_all.at[y], local_sem.at[6])
    k_here.start()
    k_here.wait()
    take_k(y, k_all.at[y])

    def second(e, k):
        to = (x + 4 - k) % 4
        i = (k + 3) % 4
        src = picked.at[e, :, pl.ds(to * 14, 14)]
        dst = p_x.at[e, i // 2, i % 2, :, :, z, core]
        if k == 0:
            return pltpu.make_async_copy(src, dst, local_sem.at[2 + e])
        return remote(src, dst, two_send.at[e, k], two_recv.at[e, k], on_x(4 - k))

    def third(e, k):
        to = (place + k) % 8
        src = picked.at[e, :, pl.ds(to * 7, 7)]
        dst = p_z.at[e, x, :, :, place]
        return remote(src, dst, three_send.at[e, k], three_recv.at[e, k], (row, y_hi * 8 + to))

    def third_here(e):
        src = picked.at[e, :, pl.ds(place * 7, 7)]
        return pltpu.make_async_copy(src, p_z.at[e, x, :, :, place], local_sem.at[4 + e])

    stored = [map_ref[t] for t in range(28)]
    inverse = [functools.reduce(jnp.maximum, [jnp.where(stored[t] == j, t, 0) for t in range(1, 28)]) for j in range(28)]

    def third_start(e):
        @pl.loop(1, 8)
        def _(k):
            third(e, k).start()

        third_here(e).start()

    for e in range(2):
        first_here(e).wait()

        @pl.loop(1, 16)
        def _(k):
            first(e, k).wait_recv()

        for j in range(28):
            picked[e, j // 14, (j % 14) * 4 : (j % 14) * 4 + 4] = sent[e][pl.ds(inverse[j] * 4, 4)]
        for k in (1, 2, 3, 0):
            second(e, k).start()
        third_start(e)
        if e == 0:
            k_copy(UP, 1).start()
            k_copy(DOWN, 0).start()

    def z_copy(kind, r):
        def rows(there, chunk=slice(None)):
            return p_x.at[r // 2, r % 2, :, chunk, :, there, core]

        if kind == CORE:
            ref, to = p_x.at[r // 2, r % 2, :, :, :, :, core], other_core
        else:
            ref, to = {
                UP: (rows(z), on_z(1)),
                DOWN: (rows(z), on_z(3)),
                HALF_UP: (rows((z + 3) % 4, 0), on_z(1)),
                HALF_DOWN: (rows((z + 1) % 4, 1), on_z(3)),
            }[kind]
        return remote(ref, ref, z_send.at[kind, r], z_recv.at[kind, r], to)

    def x_copy(kind, e):
        def block(there, half=slice(None)):
            return p_z.at[e, there, half]

        ref, to = {
            UP: (block(x), on_x(1)),
            DOWN: (block(x), on_x(3)),
            HALF_UP: (block((x + 3) % 4, 0), on_x(1)),
            HALF_DOWN: (block((x + 1) % 4, 1), on_x(3)),
        }[kind]
        return remote(ref, ref, x_send.at[kind, e], x_recv.at[kind, e], to)

    def pass_on(copy, r):
        copy(UP, r).wait_recv()
        copy(HALF_UP, r).start()
        copy(DOWN, r).wait_recv()
        copy(HALF_DOWN, r).start()

    def z_start(e):
        for p in range(2):
            z_copy(UP, 2 * e + p).start()
            z_copy(DOWN, 2 * e + p).start()

    def x_start(e):
        x_copy(UP, e).start()
        x_copy(DOWN, e).start()

    def third_done(e):
        third_here(e).wait()

        @pl.loop(1, 8)
        def _(k):
            third(e, k).wait_recv()

    def second_done(e):
        second(e, 0).wait()
        for k in (1, 2, 3):
            second(e, k).wait_recv()

    second_done(0)
    z_start(0)
    third_done(0)
    x_start(0)
    second_done(1)
    third_done(1)
    x_start(1)
    pass_on(z_copy, 0)
    pass_on(x_copy, 0)
    pass_on(z_copy, 1)
    z_start(1)

    def core_start(r):
        z_copy(HALF_UP, r).wait_recv()
        z_copy(HALF_DOWN, r).wait_recv()
        z_copy(CORE, r).start()

    core_start(0)
    core_start(1)
    pass_on(x_copy, 1)

    def n_copy(kind, e, side):
        low, high = pl.ds(0, 224), pl.ds(224, 224)
        src, dst = {
            HALF_UP: (n_part.at[e, 1, side, low], n_far.at[0, e, side]),
            HALF_DOWN: (n_part.at[e, 1, side, high], n_far.at[1, e, side]),
            UP: (n_part.at[e, 0, side, low], n_got.at[0, e, side, low]),
            DOWN: (n_part.at[e, 2, side, high], n_got.at[1, e, side, high]),
            FREE_UP: (n_part.at[e, 0, side, high], n_got.at[0, e, side, high]),
            FREE_DOWN: (n_part.at[e, 2, side, low], n_got.at[1, e, side, low]),
        }[kind]
        to = on_x(1 if kind in (UP, HALF_UP, FREE_UP) else 3)
        return remote(src, dst, n_send.at[kind, e, side], n_recv.at[kind, e, side], to)

    def n_far_start(e, side):
        n_copy(HALF_UP, e, side).start()
        n_copy(HALF_DOWN, e, side).start()

    def n_free_start(e, side):
        n_copy(FREE_UP, e, side).start()
        n_copy(FREE_DOWN, e, side).start()

    def n_near_start(e, side):
        n_copy(HALF_UP, e, side).wait_recv()
        n_part[e, 0, side, 0:224] += n_far[0, e, side]
        n_copy(UP, e, side).start()
        n_copy(HALF_DOWN, e, side).wait_recv()
        n_part[e, 2, side, 224:448] += n_far[1, e, side]
        n_copy(DOWN, e, side).start()

    def take_p(r):
        for half in range(2):

            @pl.loop(0, 7)
            def _(k):
                rows = pl.ds(pl.multiple_of(k * 128, 128), 128)
                for i in range(2):
                    columns = slice(i * 128, (i + 1) * 128)
                    p_high[r, half, rows, columns], p_low[r, half, rows, columns] = split(
                        p_x[r // 2, r % 2, i, half, pl.ds(2 * k, 2)].reshape(128, 128)
                    )

    def n_dots(r, side, half, add):
        there = side * 2 + half
        value = three(k_high[there], k_low[there], p_high[r, half], p_low[r, half])

        @pl.when(add)
        def _():
            for i in range(2):
                n_part[r // 2, 2 * (r % 2) + i, side] += value[:, i * 128 : (i + 1) * 128]

        @pl.when(jnp.logical_not(add))
        def _():
            for i in range(2):
                n_part[r // 2, 2 * (r % 2) + i, side] = value[:, i * 128 : (i + 1) * 128]

    def n_first(r):
        z_copy(CORE, r).wait_recv()
        take_p(r)

    theirs = 1 - y_hi

    @pl.loop(0, 2)
    def _(r):
        n_first(r)
        n_dots(r, y_hi, y_lo, r < 0)

    k_copy(UP, 0).wait_recv()
    k_pass(HALF_UP).start()
    k_copy(DOWN, 1).wait_recv()
    k_pass(HALF_DOWN).start()
    pass_on(z_copy, 2)
    k_copy(UP, 1).wait_recv()
    k_copy(DOWN, 0).wait_recv()
    take_k((y + 3) % 4, k_all.at[(y + 3) % 4])
    take_k((y + 1) % 4, k_all.at[(y + 1) % 4])

    def y_copy(kind, e, s):
        there = (y + {UP: 0, DOWN: 0, HALF_UP: 3, HALF_DOWN: 1}[kind]) % 4
        start = ((there // 2 + s) % 2) * 448 + (224 if kind == HALF_DOWN else 0)
        size = 448 if kind in (UP, DOWN) else 224
        ref = n_all.at[e, there, pl.ds(pl.multiple_of(start, 32), size)]
        to = on_y(1 if kind in (UP, HALF_UP) else 3)
        return remote(ref, ref, y_send.at[kind, e, s], y_recv.at[kind, e, s], to)

    def y_start(e, s):
        side = (y_hi + s) % 2
        for kind in (UP, DOWN, FREE_UP, FREE_DOWN):
            n_copy(kind, e, side).wait_recv()
        rows = pl.ds(pl.multiple_of(side * 448, 64), 448)
        n_all[e, y, rows] = -(n_part[e, 3, side] + (n_got[0, e, side] + n_got[1, e, side]))
        y_copy(UP, e, s).start()
        y_copy(DOWN, e, s).start()

    def y_pass(e, s):
        y_copy(UP, e, s).wait_recv()
        y_copy(HALF_UP, e, s).start()
        y_copy(DOWN, e, s).wait_recv()
        y_copy(HALF_DOWN, e, s).start()

    @pl.loop(0, 10)
    def _(q):
        def after(step, action, *args):
            @pl.when(q == step)
            def _():
                action(*args)

        def among(*steps):
            return functools.reduce(jnp.logical_or, [q == step for step in steps])

        after(3, n_first, 2)
        after(6, n_first, 3)
        partners = among(2, 5, 8, 9)
        own_block = among(3, 6)
        add = jnp.logical_not(jnp.logical_or(partners, own_block))
        r = jnp.where(
            partners,
            jnp.where(q == 2, 0, jnp.where(q == 5, 1, q - 6)),
            jnp.where(q < 2, q, jnp.where(q < 5, 2, 3)),
        )
        n_dots(r, jnp.where(partners, theirs, y_hi), jnp.where(own_block, y_lo, 1 - y_lo), add)
        after(0, n_far_start, 0, y_hi)
        after(1, n_free_start, 0, y_hi)
        after(0, pass_on, z_copy, 3)
        after(1, core_start, 2)
        after(3, core_start, 3)
        after(4, n_far_start, 1, y_hi)
        after(5, n_near_start, 0, y_hi)
        after(7, n_free_start, 1, y_hi)
        after(8, n_near_start, 1, y_hi)

    k_pass(HALF_UP).wait_recv()
    k_pass(HALF_DOWN).wait_recv()
    take_k((y + 2) % 4, k_all.at[(y + 2) % 4])

    @pl.loop(0, 4)
    def _(t):
        n_dots(t, theirs, y_lo, t >= 0)

        @pl.when(t == 0)
        def _():
            n_far_start(0, theirs)
            y_start(0, 0)

        @pl.when(t == 1)
        def _():
            n_free_start(0, theirs)

        @pl.when(t == 2)
        def _():
            y_start(1, 0)
            n_near_start(0, theirs)
            n_far_start(1, theirs)

        @pl.when(t == 3)
        def _():
            n_free_start(1, theirs)

    y_pass(0, 0)

    def take_z(e):
        x_copy(HALF_UP, e).wait_recv()
        x_copy(HALF_DOWN, e).wait_recv()

        @pl.loop(0, 4)
        def _(there):
            for half in range(2):
                columns = slice(e * 128, (e + 1) * 128)
                pz_high[there, half, :, columns], pz_low[there, half, :, columns] = split(
                    p_z[e, there, half].reshape(448, 128)
                )

    take_z(0)
    take_z(1)
    y_start(0, 1)
    n_near_start(1, theirs)
    y_pass(1, 0)

    def c_copy(e, k):
        there = (z + k) % 4
        return remote(d_part.at[e, there, 1 - core], d_core.at[e, there], c_send.at[e, k], c_recv.at[e, k], other_core)

    def d_copy(kind, e):
        two, up_, down_ = ((z + k) % 4 for k in (2, 1, 3))
        src, dst = {
            HALF_UP: (d_part.at[e, two, core, 0], d_far.at[0, e]),
            HALF_DOWN: (d_part.at[e, two, core, 1], d_far.at[1, e]),
            UP: (d_part.at[e, up_, core, 0], d_got.at[0, e, 0]),
            DOWN: (d_part.at[e, down_, core, 1], d_got.at[1, e, 1]),
            FREE_UP: (d_part.at[e, up_, core, 1], d_got.at[0, e, 1]),
            FREE_DOWN: (d_part.at[e, down_, core, 0], d_got.at[1, e, 0]),
        }[kind]
        to = on_z(1 if kind in (UP, HALF_UP, FREE_UP) else 3)
        return remote(src, dst, d_send.at[kind, e], d_recv.at[kind, e], to)

    def d_cores(e, k):
        there = (z + k) % 4
        c_copy(e, k).wait_recv()
        d_part[e, there, core] += d_core[e, there]

    def d_far_start(e):
        d_cores(e, 2)
        d_copy(HALF_UP, e).start()
        d_copy(HALF_DOWN, e).start()

    def d_near_start(e):
        d_copy(HALF_UP, e).wait_recv()
        d_part[e, (z + 1) % 4, core, 0] += d_far[0, e]
        d_copy(UP, e).start()
        d_copy(HALF_DOWN, e).wait_recv()
        d_part[e, (z + 3) % 4, core, 1] += d_far[1, e]
        d_copy(DOWN, e).start()

    def n_out(e, half):
        src = n_all.at[e, half * 2 + y_lo, pl.ds(pl.multiple_of(y_hi * 448, 64), 448)]
        columns = pl.ds(pl.multiple_of(half * 256 + e * 128, 128), 128)
        return pltpu.make_async_copy(src, n_ref.at[:, columns], out_sem.at[e, half])

    def d_rows(e, s):
        for kind in (HALF_UP, HALF_DOWN):
            y_copy(kind, e, s).wait_recv()
        for high in range(2):
            for low in range(2):
                lines = slice(low * 128, (low + 1) * 128)
                for first_row, size in ((0, 128), (128, 128), (256, 128), (384, 64)):
                    start = (high + s) % 2 * 448 + first_row
                    value = n_all[e, 2 * high + low, start : start + size].T
                    columns = slice(first_row, first_row + size)
                    t_high[high, lines, columns], t_low[high, lines, columns] = split(value)

    def d_dots(s, there, high):
        side = (high + s) % 2
        return three(t_high[high], t_low[high], pz_high[there, side], pz_low[there, side])

    def d_early(e):
        d_rows(e, 0)

        @pl.loop(0, 8)
        def _(q):
            there, high = q // 2, q % 2
            d_part[e, there, :, high] = d_dots(0, there, high).reshape(2, 128, 256)

    def d_late(e):
        d_rows(e, 1)
        for half in range(2):
            n_out(e, half).start()

        @pl.loop(0, 4)
        def _(j):
            k = jnp.where(j == 0, 2, jnp.where(j == 1, 1, jnp.where(j == 2, 3, 0)))
            there = (z + k) % 4

            @pl.loop(0, 2)
            def _(high):
                d_part[e, there, :, high] += d_dots(1, there, high).reshape(2, 128, 256)

            c_copy(e, k).start()

            @pl.when(j == (2 if e == 0 else 1))
            def _():
                d_far_start(e)

            @pl.when(j == 3)
            def _():
                d_cores(e, 1)
                d_copy(FREE_UP, e).start()
                if e == 0:
                    y_pass(1, 1)

        d_cores(e, 3)
        d_copy(FREE_DOWN, e).start()
        d_cores(e, 0)

    d_early(0)
    y_pass(0, 1)
    y_start(1, 1)
    d_early(1)
    d_late(0)
    d_near_start(0)
    d_late(1)

    def o_copy(e):
        return remote(d_sum.at[e], d_ref.at[:, e], o_send.at[e], o_recv.at[e], at(y_lo, z, y_hi, core, x))

    def o_here(e):
        return pltpu.make_async_copy(d_sum.at[e], d_ref.at[:, e], o_recv.at[e])

    def o_start(e):
        for kind in (UP, DOWN, FREE_UP, FREE_DOWN):
            d_copy(kind, e).wait_recv()
        d_sum[e] = d_part[e, z, core] + (d_got[0, e] + d_got[1, e])

        @pl.when(stays)
        def _():
            o_here(e).start()

        @pl.when(jnp.logical_not(stays))
        def _():
            o_copy(e).start()

    d_near_start(1)
    o_start(0)
    o_start(1)

    for e in range(2):

        @pl.loop(1, 16)
        def _(k):
            first(e, k).wait_send()

        @pl.loop(1, 8)
        def _(k):
            third(e, k).wait_send()

        for k in (1, 2, 3):
            second(e, k).wait_send()
        for kind in range(4):
            x_copy(kind, e).wait_send()
            c_copy(e, kind).wait_send()
            for side in range(2):
                y_copy(kind, e, side).wait_send()
        for kind in range(6):
            d_copy(kind, e).wait_send()
            for side in range(2):
                n_copy(kind, e, side).wait_send()

        @pl.when(jnp.logical_not(stays))
        def _():
            o_copy(e).wait_send()

    for half in range(2):
        k_copy(UP, half).wait_send()
        k_copy(DOWN, half).wait_send()
    k_pass(HALF_UP).wait_send()
    k_pass(HALF_DOWN).wait_send()

    @pl.loop(0, 4)
    def _(r):
        for kind in range(5):
            z_copy(kind, r).wait_send()

    for e in range(2):
        for half in range(2):
            n_out(e, half).wait()
        o_here(e).wait()


def on_device(known_inverse, factor_panel, diag_base, ancestor_map):
    whole = pl.BlockSpec(memory_space=pl.ANY)
    dma = pltpu.SemaphoreType.DMA
    new_column, reduced = pl.pallas_call(
        kernel,
        out_shape=(jax.ShapeDtypeStruct((448, 512), F32), jax.ShapeDtypeStruct((2, 2, 128, 256), F32)),
        in_specs=[pl.BlockSpec(memory_space=pltpu.SMEM), whole, whole],
        out_specs=(whole, whole),
        scratch_shapes=[
            pltpu.VMEM((4, 448, 896), F32),
            pltpu.VMEM((4, 448, 896), BF),
            pltpu.VMEM((4, 448, 896), BF),
            pltpu.VMEM((112, 8, 128), F32),
            pltpu.VMEM((112, 8, 128), F32),
            pltpu.VMEM((2, 2, 56, 8, 128), F32),
            pltpu.VMEM((2, 2, 2, 2, 14, 4, 2, 8, 128), F32),
            pltpu.VMEM((4, 2, 896, 256), BF),
            pltpu.VMEM((4, 2, 896, 256), BF),
            pltpu.VMEM((2, 4, 2, 7, 8, 8, 128), F32),
            pltpu.VMEM((4, 2, 448, 256), BF),
            pltpu.VMEM((4, 2, 448, 256), BF),
            pltpu.VMEM((2, 4, 2, 448, 128), F32),
            pltpu.VMEM((2, 2, 2, 224, 128), F32),
            pltpu.VMEM((2, 2, 2, 448, 128), F32),
            pltpu.VMEM((2, 4, 896, 128), F32),
            pltpu.VMEM((2, 256, 448), BF),
            pltpu.VMEM((2, 256, 448), BF),
            pltpu.VMEM((2, 4, 2, 2, 128, 256), F32),
            pltpu.VMEM((2, 4, 2, 128, 256), F32),
            pltpu.VMEM((2, 2, 128, 256), F32),
            pltpu.VMEM((2, 2, 2, 128, 256), F32),
            pltpu.VMEM((2, 2, 128, 256), F32),
            dma((2, 16)), dma((2, 16)), dma((2, 4)), dma((2, 4)), dma((2, 8)), dma((2, 8)), dma((7,)), dma((4, 2)), dma((4, 2)),
            dma((5, 4)), dma((5, 4)), dma((4, 2)), dma((4, 2)), dma((6, 2, 2)), dma((6, 2, 2)), dma((4, 2, 2)), dma((4, 2, 2)),
            dma((2, 4)), dma((2, 4)), dma((6, 2)), dma((6, 2)), dma((2, 2)), dma((2,)), dma((2,)),
        ],
        compiler_params=pltpu.CompilerParams(collective_id=0, has_side_effects=True, vmem_limit_bytes=60 << 20),
        cost_estimate=pl.CostEstimate(
            flops=6 * (448 * 1792 * 2048 + 256 * 1792 * 2048), bytes_accessed=4 << 20, transcendentals=0
        ),
        name="selected_inverse",
    )(ancestor_map, known_inverse, factor_panel.reshape(7, 8, 8, 512))
    return (new_column, diag_base - reduced.reshape(512, 256))


def solution(mesh):
    placed = (P("col", "row"), P("col", "row"), P("row", "col"), P())
    return jax.shard_map(
        on_device,
        mesh=mesh,
        in_specs=placed,
        out_specs=(P("col", "row"), P("row", "col")),
        check_vma=False,
    )
```
